32 devices in a mesh: clips: 8 (over z, x), units: 4 (over y, core).
Axes of the slice: x: 2, y: 2, z: 4, core: 2. Of those that a mesh axis runs over, the one named last changes fastest.
Arguments:
- tokens: bfloat16 [16, 8, 28, 28, 192], P('clips', 'units'), may hold values from -6 to 6
- cotangent: bfloat16 [16, 8, 14, 14, 384], P('clips', 'units'), may hold values from -6 to 6
- frames: int32 [16], P('clips'), may hold values from 1 to 8, as said below
- norm_gain: float32 [192], replicated, may hold values from 0.1 to 1.9
- norm_shift: float32 [192], replicated, may hold values from -2.5 to 2.5
- w_qkv: bfloat16 [192, 1152], replicated, may hold values from -0.4375 to 0.4375
- qv_bias: float32 [2, 384], replicated, may hold values from -2.5 to 2.5
- w_proj: bfloat16 [384, 384], replicated, may hold values from -6 to 6
- proj_bias: float32 [384], replicated, may hold values from -2.5 to 2.5
- w_res: bfloat16 [192, 384], replicated, may hold values from -0.4375 to 0.4375
- res_bias: float32 [384], replicated, may hold values from -2.5 to 2.5
- mlp_gain: float32 [384], replicated, may hold values from 0.1 to 1.9
- mlp_shift: float32 [384], replicated, may hold values from -2.5 to 2.5
- w_fc1: bfloat16 [384, 1536], replicated, may hold values from -0.3125 to 0.3125
- fc1_bias: float32 [1536], replicated, may hold values from -2.5 to 2.5
- w_fc2: bfloat16 [1536, 384], replicated, may hold values from -0.3125 to 0.3125
- fc2_bias: float32 [384], replicated, may hold values from -2.5 to 2.5
Outputs:
- block_out: bfloat16 [16, 8, 14, 14, 384], P('clips', 'units')
- grad_tokens: bfloat16 [16, 8, 28, 28, 192], P('clips', 'units')
- grad_norm_gain: float32 [192], replicated
- grad_norm_shift: float32 [192], replicated
- grad_qkv: float32 [192, 1152], replicated
- grad_qv_bias: float32 [2, 384], replicated
- grad_proj: float32 [384, 384], replicated
- grad_proj_bias: float32 [384], replicated
- grad_res: float32 [192, 384], replicated
- grad_res_bias: float32 [384], replicated
- grad_mlp_gain: float32 [384], replicated
- grad_mlp_shift: float32 [384], replicated
- grad_fc1: float32 [384, 1536], replicated
- grad_fc1_bias: float32 [1536], replicated
- grad_fc2: float32 [1536, 384], replicated
- grad_fc2_bias: float32 [384], replicated
The draws below stay inside these ranges and needn't reach their ends.
Inputs may be any that keep to these rules, and one draw needn't show every extreme that they name: In every aligned block of 2 clips one clip has all 8 frames.
All inputs are finite; a program needn't handle non-finite values.
Results may differ from the reference program's by a relative error of at most 0.01.
Values may be sent and summed in bfloat16 or wider, within the bound.
No kernel may reach another device: no remote copies, remote signals or barrier semaphores. Data moves between devices by JAX's collectives and lax.ppermute only.
A program may use at most 256 MiB of HBM per device.

```python
import jax
import jax.numpy as jnp
from jax import lax

DI = 192
DM = 384
HEADS = 4
HIDDEN_SIZE = 1536
FRAMES = 8
GRID = 28
CLIPS_DEV = 2
HALF = 14
CLIPS = 16
N_UNITS = 4


def draw_frames(key, part):
    key = jax.random.fold_in(key, 7)
    first, second = jax.random.split(key)
    counts = jax.random.randint(first, (CLIPS,), 1, FRAMES + 1)
    chosen = jax.random.randint(second, (CLIPS // CLIPS_DEV,), 0, CLIPS_DEV)
    places = jnp.arange(CLIPS) % CLIPS_DEV
    marked = jnp.repeat(chosen, CLIPS_DEV)
    return jnp.where(places == marked, FRAMES, counts).astype(jnp.int32)


def block_scale(own_key, shape, shards, smallest, top_value):
    level, own = 1.0, jax.random.fold_in(own_key, 6)
    for axis_at, blocks in shards:
        draws = jnp.exp(jax.random.uniform(jax.random.fold_in(own, axis_at), (blocks,), jnp.float32, smallest / len(shards), top_value / len(shards)))
        level = level * jnp.repeat(draws, shape[axis_at] // blocks).reshape([-1 if axis == axis_at else 1 for axis in range(len(shape))])
    return level


def noise(rng, dims, scale, limit, pieces=(), held_as=jnp.bfloat16):
    entries = scale * jax.random.normal(rng, dims, jnp.float32)
    if pieces:
        entries = entries * block_scale(rng, dims, pieces, -0.22, 0.18)
    return jnp.clip(entries, -limit, limit).astype(held_as)


def setup_inputs(seed: int = 0) -> dict:
    arg_keys = jax.random.split(jax.random.key(seed), 18)
    tokens = noise(arg_keys[0], (CLIPS, FRAMES, GRID, GRID, DI), 1.0, 6.0, ((0, 8), (1, 4)))
    cotangent = noise(arg_keys[1], (CLIPS, FRAMES, HALF, HALF, DM), 1.0, 6.0, ((0, 8), (1, 4)))
    frames = draw_frames(jax.random.fold_in(arg_keys[17], 71), 0)
    norm_gain = jnp.clip(1.0 + 0.18 * jax.random.normal(arg_keys[3], (DI,), jnp.float32), 0.1, 1.9)
    norm_shift = noise(arg_keys[4], (DI,), 0.5, 2.5, (), jnp.float32)
    w_qkv = noise(arg_keys[5], (DI, 3 * DM), DI ** -0.5, 0.4375)
    qv_bias = noise(arg_keys[6], (2, DM), 0.5, 2.5, (), jnp.float32)
    w_proj = noise(arg_keys[7], (DM, DM), 1 ** -0.5, 6.0)
    proj_bias = noise(arg_keys[8], (DM,), 0.5, 2.5, (), jnp.float32)
    w_res = noise(arg_keys[9], (DI, DM), DI ** -0.5, 0.4375)
    res_bias = noise(arg_keys[10], (DM,), 0.5, 2.5, (), jnp.float32)
    mlp_gain = jnp.clip(1.0 + 0.18 * jax.random.normal(arg_keys[11], (DM,), jnp.float32), 0.1, 1.9)
    mlp_shift = noise(arg_keys[12], (DM,), 0.5, 2.5, (), jnp.float32)
    w_fc1 = noise(arg_keys[13], (DM, HIDDEN_SIZE), DM ** -0.5, 0.3125)
    fc1_bias = noise(arg_keys[14], (HIDDEN_SIZE,), 0.5, 2.5, (), jnp.float32)
    w_fc2 = noise(arg_keys[15], (HIDDEN_SIZE, DM), (HIDDEN_SIZE // 4) ** -0.5, 0.3125)
    fc2_bias = noise(arg_keys[16], (DM,), 0.5, 2.5, (), jnp.float32)
    return {"tokens": tokens, "cotangent": cotangent, "frames": frames, "norm_gain": norm_gain, "norm_shift": norm_shift, "w_qkv": w_qkv, "qv_bias": qv_bias, "w_proj": w_proj, "proj_bias": proj_bias, "w_res": w_res, "res_bias": res_bias, "mlp_gain": mlp_gain, "mlp_shift": mlp_shift, "w_fc1": w_fc1, "fc1_bias": fc1_bias, "w_fc2": w_fc2, "fc2_bias": fc2_bias}


EPS = 1e-06
HI = lax.Precision.HIGHEST

@jax.custom_vjp
def low(v):
    return lax.optimization_barrier(v.astype(jnp.bfloat16)).astype(jnp.float32)

@jax.custom_vjp
def low_back(v):
    return v

def low_keep(v):
    return (low(v), None)

def low_pass(kept, grad):
    return (grad,)

def back_keep(v):
    return (v, None)

def back_low(kept, grad):
    return (low(grad),)
low.defvjp(low_keep, low_pass)
low_back.defvjp(back_keep, back_low)

def norm_rows(value, gain, shift):
    centre = value - lax.optimization_barrier(jnp.mean(value, axis=-1, keepdims=True))
    spread = lax.optimization_barrier(jnp.mean(centre * centre, axis=-1, keepdims=True))
    return centre * lax.rsqrt(spread + EPS) * gain + shift

def matmul(left, right):
    return jnp.dot(left, right, precision=HI, preferred_element_type=jnp.float32)

def clip_forward(clip_tokens, count, params):
    norm_gain, norm_shift, w_qkv, qv_bias, w_proj, proj_bias, w_res, res_bias, mlp_gain, mlp_shift, w_fc1, fc1_bias, w_fc2, fc2_bias = params
    frame_count, grid_rows, grid_cols, width_in = clip_tokens.shape
    half_rows = grid_rows // 2
    half_cols = grid_cols // 2
    normed = norm_rows(clip_tokens, norm_gain, norm_shift)
    low_normed = low(normed).reshape(-1, width_in)
    width = w_proj.shape[0]
    head_dim = width // HEADS

    def pool(value):
        columns = value.shape[-1]
        shaped = value.reshape(frame_count, half_rows, 2, half_cols, 2, columns)
        return lax.optimization_barrier(jnp.mean(shaped, axis=(2, 4))).reshape(-1, columns)
    combined = matmul(low_normed, w_qkv)
    query = low_back(low(pool(combined[:, :width]) + qv_bias[0]))
    key = low(combined[:, width:2 * width])
    value = low(combined[:, 2 * width:] + qv_bias[1])
    residual = pool(matmul(low_normed, w_res)) + res_bias
    key_count = key.shape[0]
    valid = jnp.arange(key_count) // (grid_rows * grid_cols) < count

    def group_attend(query_group):
        key_group = low_back(key)
        value_group = low_back(value)
        rows = query_group.shape[0]
        qh = query_group.reshape(rows, HEADS, head_dim)
        kh = key_group.reshape(key_count, HEADS, head_dim)
        vh = value_group.reshape(key_count, HEADS, head_dim)
        scores = low_back(jnp.einsum('qhd,khd->hqk', qh, kh, precision=HI) * (1.0 / head_dim ** 0.5))
        scores = jnp.where(valid[None, None, :], scores, -1e+30)
        probs = low(jax.nn.softmax(scores, axis=-1))
        return jnp.einsum('hqk,khd->qhd', probs, vh, precision=HI).reshape(rows, width)
    groups = query.reshape(N_UNITS, -1, width)
    attended = lax.map(jax.checkpoint(group_attend), groups).reshape(-1, width)
    attended = low_back(low(attended))
    mid = low_back(matmul(attended, w_proj) + proj_bias + residual)
    mlp_in = low(norm_rows(mid, mlp_gain, mlp_shift))
    pre = low_back(matmul(mlp_in, w_fc1) + fc1_bias)
    act = low(jax.nn.gelu(pre))
    return mid + matmul(act, w_fc2) + fc2_bias

def reference(tokens, cotangent, frames, norm_gain, norm_shift, w_qkv, qv_bias, w_proj, proj_bias, w_res, res_bias, mlp_gain, mlp_shift, w_fc1, fc1_bias, w_fc2, fc2_bias):
    params = tuple((p.astype(jnp.float32) for p in (norm_gain, norm_shift, w_qkv, qv_bias, w_proj, proj_bias, w_res, res_bias, mlp_gain, mlp_shift, w_fc1, fc1_bias, w_fc2, fc2_bias)))

    def step(total, item):
        clip_tokens, clip_cot, count = item

        def forward(inputs, weights):
            return clip_forward(inputs, count, weights)
        output, pull = jax.vjp(forward, clip_tokens.astype(jnp.float32), params)
        grad_in, grad_params = pull(clip_cot.astype(jnp.float32).reshape(output.shape))
        total = tuple((t + g for t, g in zip(total, grad_params)))
        return (total, (output.reshape(clip_cot.shape).astype(jnp.bfloat16), grad_in.astype(jnp.bfloat16)))
    zeros = tuple((jnp.zeros_like(p) for p in params))
    sums, (block_out, grad_tokens) = lax.scan(step, zeros, (tokens, cotangent, frames))
    g_norm_gain, g_norm_shift, g_qkv, g_qv_bias, g_proj, g_proj_bias, g_res, g_res_bias, g_mlp_gain, g_mlp_shift, g_fc1, g_fc1_bias, g_fc2, g_fc2_bias = sums
    return (block_out, grad_tokens, g_norm_gain, g_norm_shift, g_qkv, g_qv_bias, g_proj, g_proj_bias, g_res, g_res_bias, g_mlp_gain, g_mlp_shift, g_fc1, g_fc1_bias, g_fc2, g_fc2_bias)
```

```python
import functools

import jax
import jax.numpy as jnp
import numpy as np
from jax import lax
from jax.experimental import pallas as pl
from jax.experimental.pallas import tpu as pltpu
from jax.sharding import PartitionSpec as P

HEADS = 4
LANES = 128
EPS = 1e-06
LOG2E = 1.4426950408889634
ABSENT = -1e30
BOTH = ("clips", "units")
F32 = jnp.float32
BF16 = jnp.bfloat16
MIB = 2**20


def dot(left, right, dim_left=1, dim_right=0):
    return lax.dot_general(
        left, right, (((dim_left,), (dim_right,)), ((), ())), preferred_element_type=F32
    )


def norm_stats(value):
    centre = value - jnp.mean(value, axis=-1, keepdims=True)
    scale_inv = lax.rsqrt(jnp.mean(centre * centre, axis=-1, keepdims=True) + EPS)
    return centre * scale_inv, scale_inv


def norm_back(d_hat, hat, scale_inv):
    first = jnp.mean(d_hat, axis=-1, keepdims=True)
    second = jnp.mean(d_hat * hat, axis=-1, keepdims=True)
    return scale_inv * (d_hat - first - hat * second)


def three_parts(value):
    high = value.astype(BF16).astype(F32)
    rest = value - high
    middle = rest.astype(BF16).astype(F32)
    return high, middle, rest - middle


def with_columns(base, lane, column):
    high, middle, small = three_parts(-column)
    out = jnp.where(lane == 96, high, base)
    out = jnp.where(lane == 98, middle, out)
    return jnp.where(lane == 99, small, out)


def forward_kernel(
    dims,
    mask_ref,
    tok0_ref,
    tok1_ref,
    tok2_ref,
    tok3_ref,
    gain_ref,
    shift_ref,
    wkv_ref,
    kv_bias_ref,
    wq_ref,
    q_bias_ref,
    wres_ref,
    res_bias_ref,
    pool_ref,
    ones_ref,
    probs_ref,
    att_ref,
    residual_ref,
    pooled_ref,
    pooled_hat_ref,
    key_out,
    value_out,
    query_out,
    low_out,
    hat_out,
    tok_ref,
    key_ref,
    value_ref,
    query_ref,
    low_ref,
    hat_ref,
    acc_ref,
    peak_ref,
    sems,
):
    di, rows, part, half, chunk, chunks, head_dim = dims
    frame = rows // 2
    width = HEADS * LANES
    head = pl.program_id(0)
    step = pl.program_id(1)
    factor = 1.0 / head_dim**0.5
    copies = [
        pltpu.make_async_copy(src, dst, sems.at[i])
        for i, (src, dst) in enumerate(
            (
                (key_ref, key_out),
                (value_ref, value_out),
                (query_ref, query_out),
                (low_ref, low_out),
                (hat_ref, hat_out),
            )
        )
    ]

    @pl.when((head == 0) & (step == 0))
    def _():
        for i, ref in enumerate((tok0_ref, tok1_ref, tok2_ref, tok3_ref)):
            for j in range(2):
                tok_ref[2 * i + j] = ref[j * frame : (j + 1) * frame, :]
        total = 2 * part
        tail = lax.broadcasted_iota(jnp.int32, (total, LANES), 1)
        ones_tail = jnp.where(tail == di - LANES, 1.0, 0.0).astype(BF16)
        for ref in (low_ref, hat_ref):
            ref[:, LANES:] = ones_tail
            for base in (0, part):
                ref[base + 2 * rows : base + part, :di] = jnp.zeros((part - 2 * rows, di), BF16)
        empty = part - 2 * rows
        empty_lane = lax.broadcasted_iota(jnp.int32, (empty, LANES), 1)
        for base in (0, part):
            for h in range(HEADS):
                key_ref[h, base + 2 * rows : base + part, :] = jnp.where(
                    empty_lane == 97, ABSENT, 0.0
                ).astype(BF16)
                value_ref[h, base + 2 * rows : base + part, :] = jnp.zeros((empty, LANES), BF16)
        peak_ref[0:8, :] = jnp.zeros((8, LANES), F32)
        mask_lane = lax.broadcasted_iota(jnp.int32, (1, width), 1) % LANES == 97

        @pl.loop(0, 8)
        def _(i):
            base = pl.multiple_of(
                i * frame + jnp.where(i >= 4, part - 2 * rows, 0).astype(jnp.int32), 16
            )
            hat, _ = norm_stats(tok_ref[i].astype(F32))
            low = (hat * gain_ref[...] + shift_ref[...]).astype(BF16)
            low_ref[pl.ds(base, frame), :di] = low
            hat_ref[pl.ds(base, frame), :di] = hat.astype(BF16)
            key = dot(low, wkv_ref[:, :width])
            squares = dot((key * key).astype(BF16), ones_ref[...])
            peak_ref[0:8, :] = jnp.maximum(
                peak_ref[0:8, :], jnp.max(squares, axis=0, keepdims=True)
            )
            key = key + kv_bias_ref[:, :width] + jnp.where(mask_lane, mask_ref[i], 0.0)
            key = key.astype(BF16)
            value = (dot(low, wkv_ref[:, width:]) + kv_bias_ref[:, width:]).astype(BF16)
            for h in range(HEADS):
                key_ref[h, pl.ds(base, frame), :] = key[:, h * LANES : (h + 1) * LANES]
                value_ref[h, pl.ds(base, frame), :] = value[:, h * LANES : (h + 1) * LANES]

        for index in (0, 1, 3, 4):
            copies[index].start()
        pooled_ref[:, LANES:] = ones_tail[: 2 * half]
        pooled_hat_ref[:, LANES:] = ones_tail[: 2 * half]
        lows = []
        for i in range(2):
            at = slice(i * half, (i + 1) * half)
            pooled = dot(pool_ref[...], low_ref[i * rows : (i + 1) * rows, :di])
            high = pooled.astype(BF16).astype(F32)
            lows.append((high, pooled - high))
        high = jnp.concatenate([a for a, _ in lows], axis=0).astype(BF16)
        rest = jnp.concatenate([b for _, b in lows], axis=0).astype(BF16)
        pooled_ref[:, :di] = high
        pooled_hat_ref[:, :di] = jnp.concatenate(
            [
                dot(pool_ref[...], hat_ref[i * rows : (i + 1) * rows, :di])
                for i in range(2)
            ],
            axis=0,
        ).astype(BF16)
        residual_ref[...] = dot(high, wres_ref[...]) + dot(rest, wres_ref[...]) + res_bias_ref[...]
        query = dot(high, wq_ref[...]) + dot(rest, wq_ref[...]) + q_bias_ref[...]
        query = query.astype(BF16).astype(F32)
        squares = dot((query * query).astype(BF16), ones_ref[...])
        bound = jnp.sqrt(squares * jnp.max(peak_ref[0:8, :], axis=0, keepdims=True)) * 1.02
        lane = lax.broadcasted_iota(jnp.int32, (2 * half, LANES), 1)
        for h in range(HEADS):
            query_ref[h] = jnp.where(
                lane == 97, 1.0, query[:, h * LANES : (h + 1) * LANES]
            ).astype(BF16)
        loose = jnp.max(bound) * factor > 30.0

        @pl.when(jnp.logical_not(loose))
        def _():
            peak_ref[...] = bound

        @pl.when(loose)
        def _():
            peak_ref[...] = jnp.full((2 * half, LANES), -3e38, F32)

            @pl.loop(0, HEADS)
            def _(h):
                @pl.loop(0, chunks)
                def _(j):
                    at = pl.ds(pl.multiple_of(j * chunk, LANES), chunk)
                    scores = dot(query_ref[h], key_ref[h, at, :], 1, 1)
                    top = jnp.max(scores, axis=-1, keepdims=True)
                    peak_ref[...] = jnp.where(
                        lane == h, jnp.maximum(peak_ref[...], top), peak_ref[...]
                    )

        for h in range(HEADS):
            query_ref[h] = with_columns(
                query_ref[h].astype(F32), lane, peak_ref[:, h : h + 1]
            ).astype(BF16)
        copies[2].start()

    at = pl.ds(pl.multiple_of(step * chunk, LANES), chunk)
    scores = dot(query_ref[head], key_ref[head, at, :], 1, 1)
    probs = jnp.exp2(scores * (factor * LOG2E)).astype(BF16)
    probs_ref[0] = probs
    gathered = dot(probs, value_ref[head, at, :])

    @pl.when(step == 0)
    def _():
        acc_ref[...] = gathered

    @pl.when(step > 0)
    def _():
        acc_ref[...] += gathered

    @pl.when(step == chunks - 1)
    def _():
        lane = lax.broadcasted_iota(jnp.int32, (2 * half, LANES), 1)
        acc = acc_ref[...]
        total_inv = 1.0 / acc[:, 96:97]
        att_ref[0] = jnp.where(
            lane < 96, acc * total_inv, jnp.where(lane == 96, total_inv, 0.0)
        )

    @pl.when((head == HEADS - 1) & (step == chunks - 1))
    def _():
        for copy in copies:
            copy.wait()


def middle_kernel(
    att_ref,
    residual_ref,
    cot_ref,
    pooled_ref,
    wproj_ref,
    proj_bias_ref,
    gain_ref,
    shift_ref,
    wfc1_ref,
    fc1_bias_ref,
    wfc2_ref,
    fc2_bias_ref,
    out_ref,
    grads_ref,
    d_mid_ref,
    d_att_ref,
):
    count = att_ref.shape[1]
    width = residual_ref.shape[1]
    hidden = wfc1_ref.shape[1]
    lane = lax.broadcasted_iota(jnp.int32, (count, LANES), 1)
    attended = jnp.concatenate(
        [jnp.where(lane < 96, att_ref[h], 0.0).astype(BF16) for h in range(HEADS)], axis=1
    )
    mid = dot(attended, wproj_ref[...]) + proj_bias_ref[...] + residual_ref[...]
    hat, scale_inv = norm_stats(mid)
    mlp_in = (hat * gain_ref[...] + shift_ref[...]).astype(BF16)
    cot = cot_ref[...]
    d_in = jnp.zeros((count, width), F32)
    out = mid + fc2_bias_ref[...]
    fc1_at = hidden
    blocks = hidden // width
    vec_at = 2 * hidden + 2 * width - width // 2
    for i in range(blocks):
        at = slice(i * width, (i + 1) * width)
        x = dot(mlp_in, wfc1_ref[:, at]) + fc1_bias_ref[:, at]
        c0 = 0.7978845608028654
        square = x * x
        th = jnp.tanh(c0 * x * (1.0 + 0.044715 * square))
        half_up = 0.5 * (1.0 + th)
        act = (x * half_up).astype(BF16)
        slope = half_up + (0.5 * c0) * x * (1.0 - th * th) * (1.0 + (3 * 0.044715) * square)
        out = out + dot(act, wfc2_ref[at, :])
        grads_ref[at, :] = dot(act, cot, 0, 0).astype(BF16)
        d_pre32 = dot(cot, wfc2_ref[at, :], 1, 1) * slope
        d_pre = d_pre32.astype(BF16)
        grads_ref[fc1_at + i * width : fc1_at + (i + 1) * width, :] = dot(
            mlp_in, d_pre, 0, 0
        ).astype(BF16)
        grads_ref[vec_at + 8 * i : vec_at + 8 * (i + 1), :] = jnp.broadcast_to(
            jnp.sum(d_pre.astype(F32), axis=0, keepdims=True), (8, width)
        ).astype(BF16)
        d_in = d_in + dot(d_pre, wfc1_ref[:, at], 1, 1)
    out_ref[...] = out.astype(BF16)
    cot32 = cot.astype(F32)
    d_mid = (cot32 + norm_back(d_in * gain_ref[...], hat, scale_inv)).astype(BF16)
    d_mid_ref[...] = d_mid
    proj_at = 2 * hidden
    g_proj = dot(attended, d_mid, 0, 0).astype(BF16)
    for h in range(HEADS):
        grads_ref[proj_at + 96 * h : proj_at + 96 * (h + 1), :] = g_proj[
            h * LANES : h * LANES + 96, :
        ]
    res_at = proj_at + width
    grads_ref[res_at : res_at + width // 2, :] = dot(pooled_ref[...], d_mid, 0, 0)[
        : width // 2
    ].astype(BF16)
    vectors = (
        jnp.sum(cot32, axis=0, keepdims=True),
        jnp.sum(d_in * hat, axis=0, keepdims=True),
        jnp.sum(d_in, axis=0, keepdims=True),
        jnp.sum(d_mid.astype(F32), axis=0, keepdims=True),
    )
    for i, vector in enumerate(vectors):
        row = vec_at + 8 * (blocks + i)
        grads_ref[row : row + 8, :] = jnp.broadcast_to(vector, (8, width)).astype(BF16)
    end = vec_at + 8 * (blocks + len(vectors))
    grads_ref[end:, :] = jnp.zeros((grads_ref.shape[0] - end, width), BF16)
    d_att = dot(d_mid, wproj_ref[...], 1, 1).astype(BF16).astype(F32)
    for h in range(HEADS):
        att = att_ref[h]
        scaled = (d_att[:, h * LANES : (h + 1) * LANES] * att[:, 96:97]).astype(BF16).astype(F32)
        delta = jnp.sum(jnp.where(lane < 96, scaled * att, 0.0), axis=-1, keepdims=True)
        d_att_ref[h] = with_columns(scaled, lane, delta).astype(BF16)


def backward_kernel(
    first,
    chunks,
    factor,
    probs_ref,
    key_ref,
    value_ref,
    query_ref,
    d_att_ref,
    low_ref,
    wkv_ref,
    pooled_ref,
    *rest,
):
    if first:
        dn_ref, pack_ref, dq_ref, gw_ref, acc_ref = rest
    else:
        prev_ref, dn_ref, pack_ref, dq_ref, gw_ref, acc_ref = rest
    step = pl.program_id(0)
    probs = probs_ref[0]
    key = key_ref[0]
    d_prob = dot(d_att_ref[0], value_ref[0], 1, 1)
    d_scores = (probs.astype(F32) * d_prob).astype(BF16)
    d_value = dot(d_att_ref[0], probs, 0, 0)[:96]
    d_key = dot(query_ref[0], d_scores, 0, 0)[:96] * factor
    both = jnp.concatenate([d_key, d_value], axis=0).astype(BF16)
    back = dot(wkv_ref[0], both)
    dn_ref[...] = back if first else prev_ref[...] + back
    g_w = dot(both, low_ref[...])
    d_query = dot(d_scores, key)

    @pl.when(step == 0)
    def _():
        gw_ref[...] = g_w
        acc_ref[...] = d_query

    @pl.when(step > 0)
    def _():
        gw_ref[...] += g_w
        acc_ref[...] += d_query

    @pl.when(step == chunks - 1)
    def _():
        lane = lax.broadcasted_iota(jnp.int32, acc_ref.shape, 1)
        dq = jnp.where(lane < 96, acc_ref[...] * factor, 0.0).astype(BF16)
        dq_ref[...] = dq
        g_q = dot(pooled_ref[...], dq, 0, 0)
        size = gw_ref.shape[0]
        pack_ref[:size, :256] = gw_ref[...]
        pack_ref[:, 256:] = g_q[: pack_ref.shape[0]]
        pack_ref[size:, :256] = jnp.zeros((pack_ref.shape[0] - size, 256), F32)


def turn_kernel(
    dn_ref,
    hat_ref,
    dq0_ref,
    dq1_ref,
    dq2_ref,
    dq3_ref,
    d_mid_ref,
    wq_ref,
    wres_ref,
    pooled_hat_ref,
    sib_ref,
    d_pool_ref,
    norm_ref,
):
    part = sib_ref.shape[1]
    di = dn_ref.shape[0]
    sib_ref[...] = dn_ref[:, part:].astype(BF16)
    d_pool = dot(d_mid_ref[...], wres_ref[...], 1, 1)
    for h, ref in enumerate((dq0_ref, dq1_ref, dq2_ref, dq3_ref)):
        d_pool = d_pool + dot(ref[...], wq_ref[:, h * LANES : (h + 1) * LANES], 1, 1)
    low = d_pool.astype(BF16)
    d_pool_ref[...] = low
    both = dot(low, pooled_hat_ref[...], 0, 0)
    for i in range(2):
        at = slice(i * part, (i + 1) * part)
        both = both + dot(dn_ref[:, at].astype(BF16), hat_ref[at, :])
    row = lax.broadcasted_iota(jnp.int32, both.shape, 0)
    col = lax.broadcasted_iota(jnp.int32, both.shape, 1)
    gain = jnp.sum(jnp.where(row == col, both, 0.0), axis=1, keepdims=True)
    lane = lax.broadcasted_iota(jnp.int32, norm_ref.shape, 1)
    norm_ref[...] = jnp.where(lane == 0, gain, jnp.where(lane == 1, both[:, di : di + 1], 0.0))


def end_kernel(
    dn_ref, got_ref, d_pool_ref, pool_ref, tok0_ref, tok1_ref, gain_ref, out0_ref, out1_ref, turn_ref
):
    part = got_ref.shape[1]
    rows = tok0_ref.shape[0]
    half = pool_ref.shape[0]
    piece = part // 5
    for i in range(5):
        at = slice(i * piece, (i + 1) * piece)
        turn_ref[at, :] = (dn_ref[:, at] + got_ref[:, at].astype(F32)).T
    for i, (tok_ref, out_ref) in enumerate(((tok0_ref, out0_ref), (tok1_ref, out1_ref))):
        spread = dot(pool_ref[...], d_pool_ref[i * half : (i + 1) * half, :], 0, 0)
        hat, scale_inv = norm_stats(tok_ref[...].astype(F32))
        d_normed = turn_ref[i * rows : (i + 1) * rows, :] + spread
        out_ref[...] = norm_back(d_normed * gain_ref[...], hat, scale_inv).astype(BF16)


def exchange(value, clip_mask, unit_mask):
    clips, units = lax.axis_size("clips"), lax.axis_size("units")
    mask = clip_mask * units + unit_mask
    return lax.ppermute(value, BOTH, [(i, i ^ mask) for i in range(clips * units)])


def stages():
    clips = lax.axis_size("clips")
    out = [[(0, 1)], [(0, 2), (1, 0), (1, 2)]]
    bit = 2
    while bit < clips:
        if bit * 2 < clips:
            out.append([(bit, 0), (2 * bit, 0), (3 * bit, 0)])
            bit *= 4
        else:
            out.append([(bit, 0)])
            bit *= 2
    return out


def place(stage):
    clip, unit = lax.axis_index("clips"), lax.axis_index("units")
    index = jnp.int32(0)
    for k in range(len(stage).bit_length()):
        clip_mask, unit_mask = stage[(1 << k) - 1]
        bit = ((clip & clip_mask) != 0) | ((unit & unit_mask) != 0)
        index = index | (bit.astype(jnp.int32) << k)
    return index


def sum_pieces(pieces):
    pieces = [p.astype(F32) for p in pieces]
    while len(pieces) > 1:
        pieces = [a + b for a, b in zip(pieces[::2], pieces[1::2])]
    return pieces[0]


def reduce_big(value):
    held = value
    plan = stages()
    places = [place(stage) for stage in plan]
    for stage, where in zip(plan, places):
        size = len(stage) + 1
        cut = held.reshape(size, held.shape[0] // size, held.shape[1])

        def take(index):
            return lax.dynamic_index_in_dim(cut, index, 0, keepdims=False)

        got = [exchange(take(where ^ (k + 1)), *mask) for k, mask in enumerate(stage)]
        held = sum_pieces([take(where)] + got).astype(BF16)
    for stage, where in reversed(list(zip(plan, places))):
        size = len(stage) + 1
        got = [held] + [exchange(held, *mask) for mask in stage]
        stacked = jnp.stack(got)
        order = jnp.arange(size) ^ where
        held = jnp.concatenate(
            [lax.dynamic_index_in_dim(stacked, order[k], 0, keepdims=False) for k in range(size)]
        )
    return held


def reduce_small(value):
    plan = stages()
    where = place(plan[0])
    cut = value.reshape(2, value.shape[0] // 2, value.shape[1])
    low = cut.astype(BF16)
    other = exchange(lax.dynamic_index_in_dim(low, 1 - where, 0, keepdims=False), *plan[0][0])
    held = lax.dynamic_index_in_dim(low, where, 0, keepdims=False).astype(F32) + other.astype(F32)
    for stage in plan[1:]:
        sent = held.astype(BF16)
        held = sum_pieces([sent] + [exchange(sent, *mask) for mask in stage])
    held = held.astype(BF16)
    other = exchange(held, *plan[0][0])
    first = jnp.where(where == 0, held, other)
    second = jnp.where(where == 0, other, held)
    return jnp.concatenate([first, second]).astype(F32)


def call(kernel, out_shape, args, flops=0, **kwargs):
    sizes = [np.prod(a.shape) * a.dtype.itemsize for a in args]
    return pl.pallas_call(
        kernel,
        out_shape=out_shape,
        compiler_params=pltpu.CompilerParams(vmem_limit_bytes=60 * MIB),
        cost_estimate=pl.CostEstimate(
            flops=int(flops), bytes_accessed=int(sum(sizes)), transcendentals=0
        ),
        **kwargs,
    )(*args)


def body(
    tokens,
    cotangent,
    frames,
    norm_gain,
    norm_shift,
    w_qkv,
    qv_bias,
    w_proj,
    proj_bias,
    w_res,
    res_bias,
    mlp_gain,
    mlp_shift,
    w_fc1,
    fc1_bias,
    w_fc2,
    fc2_bias,
):
    clip_count, frame_local, grid_rows, grid_cols, di = tokens.shape
    width = w_proj.shape[0]
    head_dim = width // HEADS
    hidden = w_fc1.shape[1]
    frame = grid_rows * grid_cols
    rows = frame_local * frame
    half = rows // 4
    part = -(-2 * rows // LANES) * LANES
    chunk = 1280
    chunks = 2 * part // chunk
    wide = HEADS * LANES
    factor = 1.0 / head_dim**0.5

    unit = lax.axis_index("units")
    clip_at = unit // 2

    flat = tokens.reshape(clip_count, rows, di)
    other = lax.dynamic_index_in_dim(flat, 1 - clip_at, 0, keepdims=False)
    mine = lax.dynamic_index_in_dim(flat, clip_at, 0, keepdims=False)
    got = exchange(other, 0, 2)
    near = exchange(mine, 0, 1)
    near_got = exchange(got, 0, 1)
    cot_flat = cotangent.reshape(clip_count, half, width)
    cot_got = exchange(
        lax.dynamic_index_in_dim(cot_flat, 1 - clip_at, 0, keepdims=False), 0, 2
    )
    cot = jnp.concatenate(
        [lax.dynamic_index_in_dim(cot_flat, clip_at, 0, keepdims=False), cot_got]
    )
    count = lax.dynamic_index_in_dim(frames, clip_at, 0, keepdims=False)
    holder = jnp.stack([unit, unit ^ 2, unit ^ 1, unit ^ 3])
    frame_index = (holder[:, None] * frame_local + jnp.arange(frame_local)[None, :]).reshape(-1)
    mask = jnp.where(frame_index < count, 0.0, ABSENT).astype(F32)

    def by_head(weight):
        lead = weight.shape[:-1]
        split = weight.reshape(*lead, HEADS, head_dim)
        pads = [(0, 0)] * (len(lead) + 1) + [(0, LANES - head_dim)]
        return jnp.pad(split, pads).reshape(*lead, wide)

    w_heads = by_head(w_qkv.reshape(di, 3, width))
    wq = w_heads[:, 0]
    wkv = w_heads[:, 1:].reshape(di, 2 * wide)
    ones_np = np.zeros((1, wide), np.float32)
    for h in range(HEADS):
        for lane in (96, 98, 99):
            ones_np[0, h * LANES + lane] = 1.0
    kv_bias = jnp.concatenate([jnp.asarray(ones_np), by_head(qv_bias[1:2]) + ones_np], axis=1)
    q_bias = by_head(qv_bias[0:1])
    ones_block = np.zeros((wide, LANES), np.float32)
    for h in range(HEADS):
        ones_block[h * LANES : h * LANES + head_dim, h] = 1.0
    pool_np = np.zeros((half, rows), np.float32)
    token = np.arange(rows)
    f, r, c = token // frame, token // grid_cols % grid_rows, token % grid_cols
    pool_np[f * (frame // 4) + (r // 2) * (grid_cols // 2) + c // 2, token] = 0.25
    pool = jnp.asarray(pool_np, BF16)
    w_proj_pad = jnp.pad(
        w_proj.reshape(HEADS, head_dim, width), ((0, 0), (0, LANES - head_dim), (0, 0))
    ).reshape(wide, width)
    w_kv_heads = (
        w_qkv[:, width:].reshape(di, 2, HEADS, head_dim).transpose(2, 0, 1, 3)
    ).reshape(HEADS, di, 2 * head_dim)

    vmem = pl.BlockSpec(memory_space=pltpu.VMEM)
    hbm = pl.BlockSpec(memory_space=pl.ANY)
    sds = jax.ShapeDtypeStruct
    gain_row, shift_row = norm_gain[None], norm_shift[None]
    kept = [
        ((HEADS, 2 * part, LANES), BF16),
        ((HEADS, 2 * part, LANES), BF16),
        ((HEADS, 2 * half, LANES), BF16),
        ((2 * part, 256), BF16),
        ((2 * part, 256), BF16),
    ]
    dims = (di, rows, part, half, chunk, chunks, head_dim)
    probs, att, residual, pooled, pooled_hat, key, value, query, low, hat = call(
        functools.partial(forward_kernel, dims),
        [
            sds((HEADS, 2 * half, 2 * part), BF16),
            sds((HEADS, 2 * half, LANES), F32),
            sds((2 * half, width), F32),
            sds((2 * half, 256), BF16),
            sds((2 * half, 256), BF16),
        ]
        + [sds(s, d) for s, d in kept],
        (
            mask,
            mine,
            got,
            near,
            near_got,
            gain_row,
            shift_row,
            wkv,
            kv_bias,
            wq,
            q_bias,
            w_res,
            res_bias[None],
            pool,
            jnp.asarray(ones_block, BF16),
        ),
        flops=25e9,
        grid=(HEADS, chunks),
        in_specs=[pl.BlockSpec(memory_space=pltpu.SMEM)] + [vmem] * 14,
        out_specs=[
            pl.BlockSpec((1, 2 * half, chunk), lambda h, j: (h, 0, j)),
            pl.BlockSpec((1, 2 * half, LANES), lambda h, j: (h, 0, 0)),
            vmem,
            vmem,
            vmem,
        ]
        + [hbm] * 5,
        scratch_shapes=[pltpu.VMEM((8, frame, di), BF16)]
        + [pltpu.VMEM(s, d) for s, d in kept]
        + [
            pltpu.VMEM((2 * half, LANES), F32),
            pltpu.VMEM((2 * half, LANES), F32),
            pltpu.SemaphoreType.DMA((5,)),
        ],
    )

    grad_rows = 4096
    out, grads, d_mid, d_att = call(
        middle_kernel,
        [
            sds((2 * half, width), BF16),
            sds((grad_rows, width), BF16),
            sds((2 * half, width), BF16),
            sds((HEADS, 2 * half, LANES), BF16),
        ],
        (
            att,
            residual,
            cot,
            pooled,
            w_proj_pad,
            proj_bias[None],
            mlp_gain[None],
            mlp_shift[None],
            w_fc1,
            fc1_bias[None],
            w_fc2,
            fc2_bias[None],
        ),
        flops=8e9,
        in_specs=[vmem] * 12,
        out_specs=[vmem] * 4,
    )
    big = reduce_big(grads)
    out_got = exchange(out[half:], 0, 2)

    packs, dqs = [], []
    dn = None
    for h in range(HEADS):
        first = h == 0
        args = [probs, key, value, query, d_att, low, w_kv_heads, pooled]
        specs = [
            pl.BlockSpec((1, 2 * half, chunk), lambda j, h=h: (h, 0, j)),
            pl.BlockSpec((1, chunk, LANES), lambda j, h=h: (h, j, 0)),
            pl.BlockSpec((1, chunk, LANES), lambda j, h=h: (h, j, 0)),
            pl.BlockSpec((1, 2 * half, LANES), lambda j, h=h: (h, 0, 0)),
            pl.BlockSpec((1, 2 * half, LANES), lambda j, h=h: (h, 0, 0)),
            pl.BlockSpec((chunk, 256), lambda j: (j, 0)),
            pl.BlockSpec((1, di, 2 * head_dim), lambda j, h=h: (h, 0, 0)),
            vmem,
        ]
        if not first:
            args.append(dn)
            specs.append(pl.BlockSpec((di, chunk), lambda j: (0, j)))
        dn, pack, dq = call(
            functools.partial(backward_kernel, first, chunks, factor),
            [
                sds((di, 2 * part), F32),
                sds((208, 384), F32),
                sds((2 * half, LANES), BF16),
            ],
            args,
            flops=9e9,
            grid=(chunks,),
            in_specs=specs,
            out_specs=[pl.BlockSpec((di, chunk), lambda j: (0, j)), vmem, vmem],
            scratch_shapes=[
                pltpu.VMEM((2 * head_dim, 256), F32),
                pltpu.VMEM((2 * half, LANES), F32),
            ],
        )
        packs.append(pack)
        dqs.append(dq)

    sib, d_pool, norm_cols = call(
        turn_kernel,
        [sds((di, part), BF16), sds((2 * half, di), BF16), sds((di, LANES), F32)],
        (dn, hat, *dqs, d_mid, wq, w_res, pooled_hat),
        flops=2e9,
        in_specs=[vmem] * 10,
        out_specs=[vmem] * 3,
    )
    sib_got = exchange(sib, 0, 1)
    norm_rows = jnp.pad(norm_cols[:, :2].T, ((0, 14), (0, 384 - di)))
    small = reduce_small(jnp.concatenate(packs + [norm_rows]))
    grad_mine, grad_far = call(
        end_kernel,
        [sds((rows, di), BF16)] * 2,
        (dn, sib_got, d_pool, pool, mine, got, gain_row),
        flops=1e9,
        grid=(1,),
        in_specs=[pl.BlockSpec((di, part), lambda i: (0, 0))] + [vmem] * 6,
        out_specs=[vmem] * 2,
        scratch_shapes=[pltpu.VMEM((part, di), F32)],
    )
    grad_got = exchange(grad_far, 0, 2)

    def in_order(own, foreign, shape):
        first = jnp.where(clip_at == 0, own, foreign)
        second = jnp.where(clip_at == 0, foreign, own)
        return jnp.stack([first, second]).reshape(shape)

    block_out = in_order(
        out[:half], out_got, (clip_count, frame_local, grid_rows // 2, grid_cols // 2, width)
    )
    grad_tokens = in_order(grad_mine, grad_got, tokens.shape)

    big = big.astype(F32)
    s_fc2 = big[:hidden]
    blocks = hidden // width
    s_fc1 = (
        big[hidden : 2 * hidden].reshape(blocks, width, width).transpose(1, 0, 2)
    ).reshape(width, hidden)
    at = 2 * hidden
    s_proj = big[at : at + width]
    s_res = big[at + width : at + width + di]
    at = at + width + di
    vectors = big[at : at + 8 * (blocks + 4)].reshape(blocks + 4, 8, width)[:, 0]
    s_fc1_bias = vectors[:blocks].reshape(hidden)
    s_fc2_bias, s_mlp_gain, s_mlp_shift, s_bias_mid = (vectors[blocks + i] for i in range(4))
    heads = small[: 208 * HEADS].reshape(HEADS, 208, 384)
    g_q = heads[:, :di, 256 : 256 + head_dim].transpose(1, 0, 2).reshape(di, width)
    g_k = heads[:, :head_dim, :di].transpose(2, 0, 1).reshape(di, width)
    g_v = heads[:, head_dim : 2 * head_dim, :di].transpose(2, 0, 1).reshape(di, width)
    s_qkv = jnp.concatenate([g_q, g_k, g_v], axis=1)
    s_qv_bias = jnp.stack(
        [
            heads[:, di, 256 : 256 + head_dim].reshape(width),
            heads[:, head_dim : 2 * head_dim, di].reshape(width),
        ]
    )
    s_norm_gain, s_norm_shift = small[208 * HEADS, :di], small[208 * HEADS + 1, :di]
    return (
        block_out,
        grad_tokens,
        s_norm_gain,
        s_norm_shift,
        s_qkv,
        s_qv_bias,
        s_proj,
        s_bias_mid,
        s_res,
        s_bias_mid,
        s_mlp_gain,
        s_mlp_shift,
        s_fc1,
        s_fc1_bias,
        s_fc2,
        s_fc2_bias,
    )


def solution(mesh):
    split = P("clips", "units", None, None, None)
    return jax.shard_map(
        body,
        mesh=mesh,
        in_specs=(split, split, P("clips")) + (P(),) * 14,
        out_specs=(split, split) + (P(),) * 14,
        check_vma=False,
    )
```

```python
import functools

import jax
import jax.numpy as jnp
import numpy as np
from jax import lax
from jax.experimental import pallas as pl
from jax.experimental.layout import Layout, with_layout_constraint
from jax.experimental.pallas import tpu as pltpu
from jax.sharding import PartitionSpec as P

HEADS = 4
LANES = 128
EPS = 1e-06
LOG2E = 1.4426950408889634
ABSENT = -1e30
BOTH = ("clips", "units")
F32 = jnp.float32
BF16 = jnp.bfloat16
MIB = 2**20


def dot(left, right, dim_left=1, dim_right=0):
    return lax.dot_general(
        left, right, (((dim_left,), (dim_right,)), ((), ())), preferred_element_type=F32
    )


def norm_stats(value):
    centre = value - jnp.mean(value, axis=-1, keepdims=True)
    scale_inv = lax.rsqrt(jnp.mean(centre * centre, axis=-1, keepdims=True) + EPS)
    return centre * scale_inv, scale_inv


def norm_back(d_hat, hat, scale_inv):
    first = jnp.mean(d_hat, axis=-1, keepdims=True)
    second = jnp.mean(d_hat * hat, axis=-1, keepdims=True)
    return scale_inv * (d_hat - first - hat * second)


def three_parts(value):
    high = value.astype(BF16).astype(F32)
    rest = value - high
    middle = rest.astype(BF16).astype(F32)
    return high, middle, rest - middle


def with_columns(base, lane, column):
    high, middle, small = three_parts(-column)
    out = jnp.where(lane == 96, high, base)
    out = jnp.where(lane == 98, middle, out)
    return jnp.where(lane == 99, small, out)


def weights_kernel(w_qkv_ref, qv_bias_ref, w_proj_ref, wq_ref, wkv_ref, heads_ref, proj_ref, bias_ref):
    di = w_qkv_ref.shape[0]
    width = w_proj_ref.shape[0]
    size = width // HEADS

    def by_head(value):
        pad = jnp.zeros((value.shape[0], LANES - size), value.dtype)
        pieces = []
        for h in range(HEADS):
            pieces += [value[:, h * size : (h + 1) * size], pad]
        return jnp.concatenate(pieces, axis=1)

    w = w_qkv_ref[...].astype(F32)
    query, key, value = (w[:, i * width : (i + 1) * width] for i in range(3))
    wq_ref[...] = by_head(query).astype(BF16)
    wkv_ref[:, : HEADS * LANES] = by_head(key).astype(BF16)
    wkv_ref[:, HEADS * LANES :] = by_head(value).astype(BF16)
    for h in range(HEADS):
        at = slice(h * size, (h + 1) * size)
        heads_ref[h] = jnp.concatenate([key[:, at], value[:, at]], axis=1).astype(BF16)
        proj_ref[h * LANES : h * LANES + size, :] = w_proj_ref[at, :]
        proj_ref[h * LANES + size : (h + 1) * LANES, :] = jnp.zeros((LANES - size, width), BF16)
    lane = lax.broadcasted_iota(jnp.int32, (8, HEADS * LANES), 1) % LANES
    ones = jnp.where((lane == 96) | (lane >= 98) & (lane < 100), 1.0, 0.0)
    biases = by_head(jnp.broadcast_to(qv_bias_ref[0:1, :], (8, width)))
    bias_ref[0:8, :] = biases
    bias_ref[8:16, :] = by_head(jnp.broadcast_to(qv_bias_ref[1:2, :], (8, width))) + ones
    bias_ref[16:24, :] = ones


def row_of(ref):
    return ref[...].reshape(1, ref.shape[-1])


def keys_of(tokens, base, first_mask, second_mask, refs, targets):
    gain_ref, shift_ref, wkv_ref, bias_ref = refs
    key_ref, value_ref, low_ref, hat_ref, peak_ref = targets
    positions, _, di = tokens.shape
    rows = 2 * positions
    wide = HEADS * LANES
    value = tokens.reshape(rows, di).astype(F32)
    hat, _ = norm_stats(value)
    low = (hat * row_of(gain_ref) + row_of(shift_ref)).astype(BF16)
    at = pl.ds(base, rows)
    low_ref[at, :di] = low
    hat_ref[at, :di] = hat.astype(BF16)
    key = dot(low, wkv_ref[:, :wide])
    squares = key[:, :LANES] * key[:, :LANES]
    for h in range(1, HEADS):
        squares = squares + key[:, h * LANES : (h + 1) * LANES] * key[:, h * LANES : (h + 1) * LANES]
    top = jnp.max(jnp.sum(squares, axis=-1, keepdims=True))
    peak_ref[...] = jnp.maximum(peak_ref[...], top)
    row = lax.broadcasted_iota(jnp.int32, (8, wide), 0) % 2
    lane = lax.broadcasted_iota(jnp.int32, (8, wide), 1) % LANES
    mask = jnp.where(row == 0, first_mask, second_mask)
    pattern = bias_ref[16:24, :] + jnp.where(lane == 97, mask, 0.0)
    key = (key.reshape(rows // 8, 8, wide) + pattern[None]).reshape(rows, wide).astype(BF16)
    for h in range(HEADS):
        key_ref[h, at, :] = key[:, h * LANES : (h + 1) * LANES]
    value = dot(low, wkv_ref[:, wide:])
    value = (value.reshape(rows // 8, 8, wide) + bias_ref[8:16, :][None]).reshape(rows, wide)
    value = value.astype(BF16)
    for h in range(HEADS):
        value_ref[h, at, :] = value[:, h * LANES : (h + 1) * LANES]


def fill_pads(base, rows, room, di, targets):
    key_ref, value_ref, low_ref, hat_ref, _ = targets
    empty = room - rows
    lane = lax.broadcasted_iota(jnp.int32, (empty, LANES), 1)
    at = slice(base + rows, base + room)
    for h in range(HEADS):
        key_ref[h, at, :] = jnp.where(lane == 97, ABSENT, 0.0).astype(BF16)
        value_ref[h, at, :] = jnp.zeros((empty, LANES), BF16)
    tail = lax.broadcasted_iota(jnp.int32, (room, LANES), 1)
    ones_tail = jnp.where(tail == di - LANES, 1.0, 0.0).astype(BF16)
    for ref in (low_ref, hat_ref):
        ref[base : base + room, LANES:] = ones_tail
        ref[at, :di] = jnp.zeros((empty, di), BF16)


def absent(place_ref, holder, frame):
    index = 2 * (place_ref[2] ^ holder) + frame
    return jnp.where(index < place_ref[3], 0.0, ABSENT).astype(F32)


def near_kernel(
    place_ref,
    mine_ref,
    near_ref,
    gain_ref,
    shift_ref,
    wkv_ref,
    bias_ref,
    pool_ref,
    key_out,
    value_out,
    low_out,
    hat_out,
    pooled_ref,
    pooled_hat_ref,
    peak_ref,
    key_ref,
    value_ref,
    low_ref,
    hat_ref,
    sems,
):
    _, positions, _, di = mine_ref.shape
    rows = 2 * positions
    room = key_ref.shape[1] // 2
    refs = (gain_ref, shift_ref, wkv_ref, bias_ref)
    targets = (key_ref, value_ref, low_ref, hat_ref, peak_ref)
    peak_ref[...] = jnp.zeros(peak_ref.shape, F32)
    pieces = 2
    step = positions // pieces
    copies = []
    for i in range(2):
        base = i * room
        fill_pads(base, rows, room, di, targets)

        @pl.loop(0, pieces)
        def _(j):
            at = pl.ds(j * step, step)
            tokens = mine_ref[0, at] if i == 0 else near_ref[at]
            keys_of(
                tokens,
                pl.multiple_of(base + 2 * j * step, 16),
                absent(place_ref, i, 0),
                absent(place_ref, i, 1),
                refs,
                targets,
            )

        at, to = pl.ds(base, room), pl.ds(2 * base, room)
        for k, (src, dst) in enumerate(((key_ref, key_out), (value_ref, value_out))):
            copies.append(
                pltpu.make_async_copy(src.at[:, at, :], dst.at[:, to, :], sems.at[4 * i + k])
            )
        for k, (src, dst) in enumerate(((low_ref, low_out), (hat_ref, hat_out))):
            copies.append(
                pltpu.make_async_copy(src.at[at, :], dst.at[to, :], sems.at[4 * i + k + 2])
            )
        for copy in copies[-4:]:
            copy.start()
    pooled_ref[...] = dot(pool_ref[...], low_ref[:rows, :di])
    pooled_hat_ref[...] = dot(pool_ref[...], hat_ref[:rows, :di])
    for copy in copies:
        copy.wait()


def forward_kernel(
    dims,
    place_ref,
    got_ref,
    near_got_ref,
    gain_ref,
    shift_ref,
    wkv_ref,
    bias_ref,
    wq_ref,
    wres_ref,
    res_bias_ref,
    pool_ref,
    pooled_in,
    pooled_hat_in,
    peak_in,
    key_in,
    value_in,
    low_in,
    hat_in,
    probs_ref,
    att_ref,
    residual_ref,
    pooled_ref,
    pooled_hat_ref,
    key_out,
    value_out,
    query_out,
    low_out,
    hat_out,
    key_ref,
    value_ref,
    query_ref,
    low_ref,
    hat_ref,
    acc_ref,
    norm_ref,
    peak_ref,
    sems,
):
    di, rows, room, half, chunk, chunks, head_dim = dims
    positions = rows // 2
    head = pl.program_id(0)
    step = pl.program_id(1)
    factor = 1.0 / head_dim**0.5
    loads, stores = [], []
    for i in range(2):
        at, to = pl.ds(2 * i * room, room), pl.ds((2 * i + 1) * room, room)
        for k, (src, dst) in enumerate(((key_in, key_ref), (value_in, value_ref))):
            loads.append(
                pltpu.make_async_copy(src.at[:, at, :], dst.at[:, at, :], sems.at[2 * i + k])
            )
        for k, (src, dst) in enumerate(((key_ref, key_out), (value_ref, value_out))):
            stores.append(
                pltpu.make_async_copy(src.at[:, to, :], dst.at[:, to, :], sems.at[4 + 2 * i + k])
            )
        for k, (src, dst) in enumerate(((low_ref, low_out), (hat_ref, hat_out))):
            stores.append(
                pltpu.make_async_copy(
                    src.at[pl.ds(i * room, room), :], dst.at[to, :], sems.at[8 + 2 * i + k]
                )
            )
    stores.append(pltpu.make_async_copy(query_ref, query_out, sems.at[12]))

    @pl.when((head == 0) & (step == 0))
    def _():
        for copy in loads:
            copy.start()
        refs = (gain_ref, shift_ref, wkv_ref, bias_ref)
        norm_ref[...] = peak_in[...]
        pieces = 2
        size = positions // pieces
        for i, ref in enumerate((got_ref, near_got_ref)):
            keys = (
                key_ref.at[:, pl.ds((2 * i + 1) * room, room), :],
                value_ref.at[:, pl.ds((2 * i + 1) * room, room), :],
                low_ref.at[pl.ds(i * room, room), :],
                hat_ref.at[pl.ds(i * room, room), :],
                norm_ref,
            )
            fill_pads(0, rows, room, di, keys)

            @pl.loop(0, pieces)
            def _(j):
                keys_of(
                    ref[pl.ds(j * size, size)],
                    pl.multiple_of(2 * j * size, 16),
                    absent(place_ref, 2 + i, 0),
                    absent(place_ref, 2 + i, 1),
                    refs,
                    keys,
                )

        for copy in stores[:-1]:
            copy.start()
        tail = lax.broadcasted_iota(jnp.int32, (2 * half, LANES), 1)
        ones_tail = jnp.where(tail == di - LANES, 1.0, 0.0).astype(BF16)
        pooled_ref[:, LANES:] = ones_tail
        pooled_hat_ref[:, LANES:] = ones_tail
        pooled = jnp.concatenate([pooled_in[...], dot(pool_ref[...], low_ref[:rows, :di])], axis=0)
        high = pooled.astype(BF16)
        rest = (pooled - high.astype(F32)).astype(BF16)
        pooled_ref[:, :di] = high
        pooled_hat_ref[:, :di] = jnp.concatenate(
            [pooled_hat_in[...], dot(pool_ref[...], hat_ref[:rows, :di])], axis=0
        ).astype(BF16)
        residual_ref[...] = (
            dot(high, wres_ref[...]) + dot(rest, wres_ref[...]) + row_of(res_bias_ref)
        )
        query = dot(high, wq_ref[...]) + dot(rest, wq_ref[...]) + bias_ref[0:1, :]
        query = query.astype(BF16).astype(F32)
        lane = lax.broadcasted_iota(jnp.int32, (2 * half, LANES), 1)
        top = jnp.float32(0.0)
        for h in range(HEADS):
            part_h = query[:, h * LANES : (h + 1) * LANES]
            top = jnp.maximum(top, jnp.max(jnp.sum(part_h * part_h, axis=-1, keepdims=True)))
            query_ref[h] = jnp.where(lane == 97, 1.0, part_h).astype(BF16)
        for copy in loads:
            copy.wait()
        reach = jnp.sqrt(jnp.max(norm_ref[...]) * top) * (1.02 * factor)

        @pl.when(jnp.logical_not(reach < 60.0))
        def _():
            peak_ref[...] = jnp.full((2 * half, LANES), -3e38, F32)

            @pl.loop(0, HEADS)
            def _(h):
                @pl.loop(0, chunks)
                def _(j):
                    at = pl.ds(pl.multiple_of(j * chunk, LANES), chunk)
                    scores = dot(query_ref[h], key_ref[h, at, :], 1, 1)
                    highest = jnp.max(scores, axis=-1, keepdims=True)
                    peak_ref[...] = jnp.where(
                        lane == h, jnp.maximum(peak_ref[...], highest), peak_ref[...]
                    )

            for h in range(HEADS):
                query_ref[h] = with_columns(
                    query_ref[h].astype(F32), lane, peak_ref[:, h : h + 1]
                ).astype(BF16)

        stores[-1].start()

    at = pl.ds(pl.multiple_of(step * chunk, LANES), chunk)
    scores = dot(query_ref[head], key_ref[head, at, :], 1, 1)
    probs = jnp.exp2(scores * (factor * LOG2E)).astype(BF16)
    probs_ref[0] = probs
    gathered = dot(probs, value_ref[head, at, :])

    @pl.when(step == 0)
    def _():
        acc_ref[...] = gathered

    @pl.when(step > 0)
    def _():
        acc_ref[...] += gathered

    @pl.when(step == chunks - 1)
    def _():
        lane = lax.broadcasted_iota(jnp.int32, (2 * half, LANES), 1)
        acc = acc_ref[...]
        total_inv = 1.0 / acc[:, 96:97]
        att_ref[0] = jnp.where(
            lane < 96, acc * total_inv, jnp.where(lane == 96, total_inv, 0.0)
        )

    @pl.when((head == HEADS - 1) & (step == chunks - 1))
    def _():
        for copy in stores:
            copy.wait()


def middle_kernel(
    place_ref,
    att_ref,
    residual_ref,
    cot_ref,
    cot_got_ref,
    wproj_ref,
    proj_bias_ref,
    gain_ref,
    shift_ref,
    wfc1_ref,
    fc1_bias_ref,
    wfc2_ref,
    fc2_bias_ref,
    out_ref,
    out_far_ref,
    grads_ref,
    vec_ref,
    d_in_ref,
    mid_ref,
    cot_out_ref,
):
    clip, core = place_ref[0], place_ref[1]
    count = att_ref.shape[1]
    half = count // 2
    width = residual_ref.shape[1]
    hidden = wfc1_ref.shape[1]
    lane = lax.broadcasted_iota(jnp.int32, (count, LANES), 1)
    attended = jnp.concatenate(
        [jnp.where(lane < 96, att_ref[h], 0.0).astype(BF16) for h in range(HEADS)], axis=1
    )
    mid = dot(attended, wproj_ref[...]) + row_of(proj_bias_ref) + residual_ref[...]
    mid_ref[...] = mid
    hat, scale_inv = norm_stats(mid)
    mlp_in = (hat * row_of(gain_ref) + row_of(shift_ref)).astype(BF16)
    cot32 = jnp.concatenate(
        [
            cot_ref[clip].reshape(half, width).astype(F32),
            cot_got_ref[...].reshape(half, width).astype(F32),
        ],
        axis=0,
    )
    cot = cot32.astype(BF16)
    cot_out_ref[...] = cot
    d_in = jnp.zeros((count, width), F32)
    out = mid + row_of(fc2_bias_ref)
    blocks = hidden // width
    fc1_bias = row_of(fc1_bias_ref)
    vec_row = lax.broadcasted_iota(jnp.int32, (8, width), 0)
    vectors = jnp.where(vec_row == blocks, jnp.sum(cot32, axis=0, keepdims=True), 0.0)
    for i in range(blocks):
        at = slice(i * width, (i + 1) * width)
        x = dot(mlp_in, wfc1_ref[:, at]) + fc1_bias[:, at]
        c0 = 0.7978845608028654
        square = x * x
        th = jnp.tanh(c0 * x * (1.0 + 0.044715 * square))
        half_up = 0.5 * (1.0 + th)
        act = (x * half_up).astype(BF16)
        slope = half_up + (0.5 * c0) * x * (1.0 - th * th) * (1.0 + (3 * 0.044715) * square)
        out = out + dot(act, wfc2_ref[at, :])
        grads_ref[core, at, :] = dot(act, cot, 0, 0).astype(BF16)
        d_pre = (dot(cot, wfc2_ref[at, :], 1, 1) * slope).astype(BF16)
        grads_ref[1 - core, at, :] = dot(mlp_in, d_pre, 0, 0).astype(BF16)
        vectors = jnp.where(
            vec_row == i, jnp.sum(d_pre.astype(F32), axis=0, keepdims=True), vectors
        )
        d_in = d_in + dot(d_pre, wfc1_ref[:, at], 1, 1)
    vec_ref[...] = vectors
    d_in_ref[...] = d_in
    out_ref[clip] = out[:half].astype(BF16).reshape(out_far_ref.shape)
    out_far_ref[...] = out[half:].astype(BF16).reshape(out_far_ref.shape)


def turn_kernel(
    att_ref,
    mid_ref,
    d_in_ref,
    cot_ref,
    pooled_ref,
    wproj_ref,
    gain_ref,
    vec_ref,
    grads_ref,
    d_mid_ref,
    d_att_ref,
):
    count, width = mid_ref.shape
    size = width // HEADS
    lane = lax.broadcasted_iota(jnp.int32, (count, LANES), 1)
    hat, scale_inv = norm_stats(mid_ref[...])
    d_in = d_in_ref[...]
    d_mid = cot_ref[...].astype(F32) + norm_back(d_in * row_of(gain_ref), hat, scale_inv)
    d_mid = d_mid.astype(BF16)
    d_mid_ref[...] = d_mid
    d_att = dot(d_mid, wproj_ref[...], 1, 1).astype(BF16).astype(F32)
    for h in range(HEADS):
        att = att_ref[h]
        scaled = (d_att[:, h * LANES : (h + 1) * LANES] * att[:, 96:97]).astype(BF16).astype(F32)
        delta = jnp.sum(jnp.where(lane < 96, scaled * att, 0.0), axis=-1, keepdims=True)
        d_att_ref[h] = with_columns(scaled, lane, delta).astype(BF16)
        grads_ref[size * h : size * (h + 1), :] = dot(
            jnp.where(lane < 96, att, 0.0).astype(BF16), d_mid, 0, 0
        )[:size].astype(BF16)
    di = 2 * size
    grads_ref[width : width + di, :] = dot(pooled_ref[...], d_mid, 0, 0)[:di].astype(BF16)
    row = lax.broadcasted_iota(jnp.int32, (8, width), 0)
    extra = jnp.where(row == 0, jnp.sum(d_in * hat, axis=0, keepdims=True), 0.0)
    extra = jnp.where(row == 1, jnp.sum(d_in, axis=0, keepdims=True), extra)
    extra = jnp.where(row == 2, jnp.sum(d_mid.astype(F32), axis=0, keepdims=True), extra)
    grads_ref[width + di :, :] = jnp.concatenate([vec_ref[...], extra], axis=0).astype(BF16)


def backward_kernel(
    first,
    last,
    heads,
    chunks,
    factor,
    probs_ref,
    key_ref,
    value_ref,
    query_ref,
    d_att_ref,
    low_ref,
    wkv_ref,
    pooled_ref,
    *rest,
):
    rest = list(rest)
    prev_ref = None if first else rest.pop(0)
    hat_ref = rest.pop(0) if last else None
    out_ref, pack_ref, dq_ref = rest[:3]
    norm_ref = rest[3] if last else None
    dn_ref, gw_ref, acc_ref = rest[-3:]
    head, step = pl.program_id(0), pl.program_id(1)
    chunk = probs_ref.shape[2]
    at = pl.ds(pl.multiple_of(step * chunk, LANES), chunk)
    probs = probs_ref[0]
    d_prob = dot(d_att_ref[0], value_ref[0], 1, 1)
    d_value = dot(d_att_ref[0], probs, 0, 0)[:96]
    d_scores = (probs.astype(F32) * d_prob).astype(BF16)
    d_key = dot(query_ref[0], d_scores, 0, 0)[:96] * factor
    d_query = dot(d_scores, key_ref[0])
    both = jnp.concatenate([d_key, d_value], axis=0).astype(BF16)
    back = dot(wkv_ref[0], both)
    g_w = dot(both, low_ref[...])

    @pl.when(head == 0)
    def _():
        dn_ref[:, at] = back if first else prev_ref[...] + back

    if heads > 1:

        @pl.when(head > 0)
        def _():
            dn_ref[:, at] += back

    @pl.when(head == heads - 1)
    def _():
        dn = dn_ref[:, at].astype(out_ref.dtype)
        out_ref[...] = dn
        if last:
            sums = dot(dn, hat_ref[...])
            norm_ref[...] = jnp.where(step == 0, sums, norm_ref[...] + sums)

    @pl.when(step == 0)
    def _():
        gw_ref[...] = g_w
        acc_ref[...] = d_query

    @pl.when(step > 0)
    def _():
        gw_ref[...] += g_w
        acc_ref[...] += d_query

    @pl.when(step == chunks - 1)
    def _():
        lane = lax.broadcasted_iota(jnp.int32, acc_ref.shape, 1)
        dq = jnp.where(lane < 96, acc_ref[...] * factor, 0.0).astype(BF16)
        dq_ref[0] = dq
        g_q = dot(pooled_ref[...], dq, 0, 0)
        size = gw_ref.shape[0]
        rows = pack_ref.shape[1]
        pack_ref[0, :size, :256] = gw_ref[...]
        pack_ref[0, :, 256:] = g_q[:rows]
        pack_ref[0, size:, :256] = jnp.zeros((rows - size, 256), F32)


def gather_kernel(
    place_ref,
    norm_ref,
    dq0_ref,
    dq1_ref,
    dq2_ref,
    pack0_ref,
    pack1_ref,
    pack2_ref,
    mlp_ref,
    d_mid_ref,
    wq_ref,
    wres_ref,
    pooled_hat_ref,
    d_pool_ref,
    grads_ref,
):
    core = place_ref[1]
    di = wq_ref.shape[0]
    d_pool = dot(d_mid_ref[...], wres_ref[...], 1, 1)
    for h, dq in enumerate((dq0_ref[0], dq1_ref[0], dq2_ref[0], dq2_ref[1])):
        d_pool = d_pool + dot(dq, wq_ref[:, h * LANES : (h + 1) * LANES], 1, 1)
    low = d_pool.astype(BF16)
    d_pool_ref[...] = low
    both = norm_ref[...] + dot(low, pooled_hat_ref[...], 0, 0)
    row = lax.broadcasted_iota(jnp.int32, both.shape, 0)
    col = lax.broadcasted_iota(jnp.int32, both.shape, 1)
    gain = jnp.sum(jnp.where(row == col, both, 0.0), axis=1, keepdims=True)
    lane = lax.broadcasted_iota(jnp.int32, (di, LANES), 1)
    norms = jnp.where(lane == 65, gain, jnp.where(lane == 66, both[:, di : di + 1], 0.0))
    pieces = [mlp_ref[...]]
    for pack in (pack0_ref[0], pack1_ref[0], pack2_ref[0]):
        pieces.append(pack.astype(BF16))
    last = pack2_ref[1]
    middle = last[:, LANES : 2 * LANES] + jnp.concatenate(
        [norms, jnp.zeros((last.shape[0] - di, LANES), F32)], axis=0
    )
    pieces.append(
        jnp.concatenate([last[:, :LANES], middle, last[:, 2 * LANES :]], axis=1).astype(BF16)
    )
    cut = grads_ref.shape[1]
    at = 0
    for piece in pieces:
        size = piece.shape[0]
        done = 0
        while done < size:
            side, row = divmod(at + done, cut)
            take = min(size - done, cut - row)
            slot = core if side == 0 else 1 - core
            grads_ref[slot, row : row + take, :] = piece[done : done + take]
            done += take
        at += size
    grads_ref[1 - core, at - cut :, :] = jnp.zeros((2 * cut - at, grads_ref.shape[2]), BF16)


def end_kernel(own, place_ref, dn_ref, got_ref, d_pool_ref, spread_ref, tokens_ref, gain_ref, out_ref):
    positions, _, di = tokens_ref.shape[-3:]
    rows = 2 * positions
    half = spread_ref.shape[1]
    room = dn_ref.shape[1] // 2
    start = own * room
    lead = start % LANES
    at = slice(start - lead, start - lead + -(-(lead + rows) // LANES) * LANES)
    turned = (dn_ref[:, at].astype(F32) + got_ref[:, at].astype(F32)).T[lead : lead + rows]
    spread = dot(spread_ref[...], d_pool_ref[own * half : (own + 1) * half, :])
    tokens = tokens_ref[0] if own == 0 else tokens_ref[...]
    hat, scale_inv = norm_stats(tokens.reshape(rows, di).astype(F32))
    grad = norm_back((turned + spread) * row_of(gain_ref), hat, scale_inv)
    grad = grad.astype(BF16).reshape(positions, 2, di)
    if own == 0:
        out_ref[place_ref[0]] = grad
    else:
        out_ref[...] = grad


def unpack_big_kernel(place_ref, own_ref, other_ref, fc2_ref, fc1_ref):
    core = place_ref[1]
    width = own_ref.shape[1]

    def write(first, second):
        fc2_ref[...] = first[...].astype(F32)
        for i in range(fc1_ref.shape[1] // width):
            at = slice(i * width, (i + 1) * width)
            fc1_ref[:, at] = second[at, :].astype(F32)

    @pl.when(core == 0)
    def _():
        write(own_ref, other_ref)

    @pl.when(core == 1)
    def _():
        write(other_ref, own_ref)


def unpack_small_kernel(
    place_ref,
    own_ref,
    other_ref,
    proj_ref,
    res_ref,
    fc1_bias_ref,
    fc2_bias_ref,
    mlp_gain_ref,
    mlp_shift_ref,
    proj_bias_ref,
    res_bias_ref,
    qkv_ref,
    qv_bias_ref,
    norm_gain_ref,
    norm_shift_ref,
    whole_ref,
):
    core = place_ref[1]
    cut, width = own_ref.shape
    size = width // HEADS
    di = 2 * size
    whole_ref[core] = own_ref[...]
    whole_ref[1 - core] = other_ref[...]

    def rows(start, count):
        pieces = []
        while count:
            side, row = divmod(start, cut)
            take = min(count, cut - row)
            pieces.append(whole_ref[side, row : row + take, :])
            start, count = start + take, count - take
        return (pieces[0] if len(pieces) == 1 else jnp.concatenate(pieces, axis=0)).astype(F32)

    proj_ref[...] = rows(0, width)
    res_ref[...] = rows(width, di)
    vectors = rows(width + di, 16)
    blocks = fc1_bias_ref.shape[0] // width
    fc1_bias_ref[...] = jnp.concatenate([vectors[i : i + 1] for i in range(blocks)], axis=1)[0]
    fc2_bias_ref[...] = vectors[blocks]
    mlp_gain_ref[...] = vectors[8]
    mlp_shift_ref[...] = vectors[9]
    proj_bias_ref[...] = vectors[10]
    res_bias_ref[...] = vectors[10]
    start = width + di + 16
    queries, keys, values, q_bias, v_bias = [], [], [], [], []
    for h in range(HEADS):
        pack = rows(start + 208 * h, 208)
        queries.append(pack[:di, 256 : 256 + size])
        turned = pack[:di, :256].T
        keys.append(turned[:di, :size])
        values.append(turned[:di, size:])
        q_bias.append(pack[di : di + 1, 256 : 256 + size])
        v_bias.append(turned[di : di + 1, size:])
    qkv_ref[...] = jnp.concatenate(queries + keys + values, axis=1)
    qv_bias_ref[0:1, :] = jnp.concatenate(q_bias, axis=1)
    qv_bias_ref[1:2, :] = jnp.concatenate(v_bias, axis=1)
    norm_gain_ref[...] = turned[di + 1]
    norm_shift_ref[...] = turned[di + 2]


def exchange(value, clip_mask, unit_mask):
    clips, units = lax.axis_size("clips"), lax.axis_size("units")
    mask = clip_mask * units + unit_mask
    return lax.ppermute(value, BOTH, [(i, i ^ mask) for i in range(clips * units)])


def stages():
    clips = lax.axis_size("clips")
    out = [[(0, 1)], [(0, 2), (1, 0), (1, 2)]]
    bit = 2
    while bit < clips:
        if bit * 2 < clips:
            out.append([(bit, 0), (2 * bit, 0), (3 * bit, 0)])
            bit *= 4
        else:
            out.append([(bit, 0)])
            bit *= 2
    return out


def place(stage):
    clip, unit = lax.axis_index("clips"), lax.axis_index("units")
    index = jnp.int32(0)
    for k in range(len(stage).bit_length()):
        clip_mask, unit_mask = stage[(1 << k) - 1]
        bit = ((clip & clip_mask) != 0) | ((unit & unit_mask) != 0)
        index = index | (bit.astype(jnp.int32) << k)
    return index


def sum_pieces(pieces):
    pieces = [p.astype(F32) for p in pieces]
    while len(pieces) > 1:
        pieces = [a + b for a, b in zip(pieces[::2], pieces[1::2])]
    return pieces[0]


class Sum:
    def __init__(self, keep, give, depth):
        self.plan = stages()
        self.depth = depth
        self.places = [place(stage) for stage in self.plan]
        self.held, self.pieces = keep, [give]
        self.at, self.back, self.done = 0, False, False

    def cut(self):
        if self.back or self.at > self.depth:
            self.pieces = [self.held] * len(self.plan[self.at])
            return
        size, where = len(self.plan[self.at]) + 1, self.places[self.at]
        whole = self.held.reshape(size, self.held.shape[0] // size, self.held.shape[1])

        def take(index):
            return lax.dynamic_index_in_dim(whole, index, 0, keepdims=False)

        self.held = take(where)
        self.pieces = [take(where ^ (k + 1)) for k in range(size - 1)]

    def send(self, other):
        (self.held, self.pieces), other = lax.optimization_barrier(((self.held, self.pieces), other))
        self.got = [exchange(p, *mask) for p, mask in zip(self.pieces, self.plan[self.at])]
        self.done = self.back and self.at == 0
        return other

    def merge(self, other):
        (self.held, self.got), other = lax.optimization_barrier(((self.held, self.got), other))
        if not self.back:
            self.held = sum_pieces([self.held] + self.got).astype(BF16)
            if self.at + 1 < len(self.plan):
                self.at += 1
            else:
                self.back, self.at = True, min(self.at, self.depth)
        else:
            size, where = len(self.got) + 1, self.places[self.at]
            stacked = jnp.stack([self.held] + self.got)
            self.held = jnp.concatenate(
                [
                    lax.dynamic_index_in_dim(stacked, where ^ k, 0, keepdims=False)
                    for k in range(size)
                ]
            )
            self.at -= 1
        self.cut()
        return other

    def advance(self, other):
        return other if self.done else self.send(self.merge(other))


def call(kernel, out_shape, args, flops=0, vmem=60, **kwargs):
    sizes = [np.prod(a.shape) * a.dtype.itemsize for a in args]
    return pl.pallas_call(
        kernel,
        out_shape=out_shape,
        compiler_params=pltpu.CompilerParams(vmem_limit_bytes=vmem * MIB),
        cost_estimate=pl.CostEstimate(
            flops=int(flops), bytes_accessed=int(sum(sizes)), transcendentals=0
        ),
        **kwargs,
    )(*args)


def body(
    tokens,
    cotangent,
    frames,
    norm_gain,
    norm_shift,
    w_qkv,
    qv_bias,
    w_proj,
    proj_bias,
    w_res,
    res_bias,
    mlp_gain,
    mlp_shift,
    w_fc1,
    fc1_bias,
    w_fc2,
    fc2_bias,
):
    clip_count, frame_local, grid_rows, grid_cols, di = tokens.shape
    width = w_proj.shape[0]
    head_dim = width // HEADS
    hidden = w_fc1.shape[1]
    frame = grid_rows * grid_cols
    rows = frame_local * frame
    half = rows // 4
    room = 1600
    chunk = 1280
    chunks = 4 * room // chunk
    wide = HEADS * LANES
    factor = 1.0 / head_dim**0.5
    vmem = pl.BlockSpec(memory_space=pltpu.VMEM)
    smem = pl.BlockSpec(memory_space=pltpu.SMEM)
    hbm = pl.BlockSpec(memory_space=pl.ANY)
    sds = jax.ShapeDtypeStruct

    unit = lax.axis_index("units")
    clip_at = unit // 2
    count = lax.dynamic_index_in_dim(frames, clip_at, 0, keepdims=False)
    placed = jnp.stack([clip_at, unit % 2, unit, count]).astype(jnp.int32)

    raw = tokens.transpose(0, 2, 3, 1, 4).reshape(clip_count, frame, frame_local, di)
    cot_raw = cotangent.transpose(0, 2, 3, 1, 4).reshape(
        clip_count, frame // 4, frame_local, width
    )

    def one(value, index):
        return lax.dynamic_index_in_dim(value, index, 0, keepdims=False)

    def cross(value, unit_mask):
        value = with_layout_constraint(value, Layout((0, 1, 2)))
        return with_layout_constraint(exchange(value, 0, unit_mask), Layout((0, 1, 2)))

    other = one(raw, 1 - clip_at)
    got = cross(other, 2)
    other, mine = lax.optimization_barrier((other, one(raw, clip_at)))
    near = cross(mine, 1)
    near, cot_far = lax.optimization_barrier((near, one(cot_raw, 1 - clip_at)))
    cot_got = cross(cot_far, 2)

    pool_np = np.zeros((half, rows), np.float32)
    token = np.arange(rows)
    position, f = token // frame_local, token % frame_local
    r, c = position // grid_cols, position % grid_cols
    pool_np[((r // 2) * (grid_cols // 2) + c // 2) * frame_local + f, token] = 0.25
    pool = jnp.asarray(pool_np, BF16)
    spread = jnp.asarray(pool_np.T, BF16)

    wq, wkv, w_kv_heads, w_proj_pad, bias = call(
        weights_kernel,
        [
            sds((di, wide), BF16),
            sds((di, 2 * wide), BF16),
            sds((HEADS, di, 2 * head_dim), BF16),
            sds((wide, width), BF16),
            sds((24, wide), F32),
        ],
        (w_qkv, qv_bias, w_proj),
        in_specs=[vmem] * 3,
        out_specs=[vmem] * 5,
    )
    whole = [
        sds((HEADS, 4 * room, LANES), BF16),
        sds((HEADS, 4 * room, LANES), BF16),
        sds((4 * room, 256), BF16),
        sds((4 * room, 256), BF16),
    ]
    one_clip = (1, frame, frame_local, di)
    key, value, low, hat, pooled_mine, pooled_hat_mine, peak = call(
        near_kernel,
        whole
        + [sds((half, di), F32), sds((half, di), F32), sds((8, LANES), F32)],
        (placed, raw, near, norm_gain, norm_shift, wkv, bias, pool),
        flops=3e9,
        grid_spec=pltpu.PrefetchScalarGridSpec(
            num_scalar_prefetch=1,
            grid=(1,),
            in_specs=[pl.BlockSpec(one_clip, lambda i, s: (s[0], 0, 0, 0))] + [vmem] * 6,
            out_specs=[hbm] * 4 + [vmem] * 3,
            scratch_shapes=[
                pltpu.VMEM((HEADS, 2 * room, LANES), BF16),
                pltpu.VMEM((HEADS, 2 * room, LANES), BF16),
                pltpu.VMEM((2 * room, 256), BF16),
                pltpu.VMEM((2 * room, 256), BF16),
                pltpu.SemaphoreType.DMA((8,)),
            ],
        ),
    )
    got, peak = lax.optimization_barrier((got, peak))
    near_got = cross(got, 1)
    dims = (di, rows, room, half, chunk, chunks, head_dim)
    probs, att, residual, pooled, pooled_hat, key, value, query, low, hat = call(
        functools.partial(forward_kernel, dims),
        [
            sds((HEADS, 2 * half, 4 * room), BF16),
            sds((HEADS, 2 * half, LANES), F32),
            sds((2 * half, width), F32),
            sds((2 * half, 256), BF16),
            sds((2 * half, 256), BF16),
        ]
        + whole[:2]
        + [sds((HEADS, 2 * half, LANES), BF16)]
        + whole[2:],
        (
            placed,
            got,
            near_got,
            norm_gain,
            norm_shift,
            wkv,
            bias,
            wq,
            w_res,
            res_bias,
            pool,
            pooled_mine,
            pooled_hat_mine,
            peak,
            key,
            value,
            low,
            hat,
        ),
        flops=25e9,
        grid=(HEADS, chunks),
        in_specs=[smem] + [vmem] * 13 + [hbm] * 4,
        out_specs=[
            pl.BlockSpec((1, 2 * half, chunk), lambda h, j: (h, 0, j)),
            pl.BlockSpec((1, 2 * half, LANES), lambda h, j: (h, 0, 0)),
            vmem,
            vmem,
            vmem,
        ]
        + [hbm] * 5,
        input_output_aliases={14: 5, 15: 6, 16: 8, 17: 9},
        scratch_shapes=[
            pltpu.VMEM((HEADS, 4 * room, LANES), BF16),
            pltpu.VMEM((HEADS, 4 * room, LANES), BF16),
            pltpu.VMEM((HEADS, 2 * half, LANES), BF16),
            pltpu.VMEM((2 * room, 256), BF16),
            pltpu.VMEM((2 * room, 256), BF16),
            pltpu.VMEM((2 * half, LANES), F32),
            pltpu.VMEM((8, LANES), F32),
            pltpu.VMEM((2 * half, LANES), F32),
            pltpu.SemaphoreType.DMA((13,)),
        ],
    )

    out_raw = sds(cot_raw.shape, BF16)
    out_far = sds(cot_raw.shape[1:], BF16)
    out, out_far, fc_grads, vectors, d_in, mid, cot = call(
        middle_kernel,
        [
            out_raw,
            out_far,
            sds((2, hidden, width), BF16),
            sds((8, width), F32),
            sds((2 * half, width), F32),
            sds((2 * half, width), F32),
            sds((2 * half, width), BF16),
        ],
        (
            placed,
            att,
            residual,
            cot_raw,
            cot_got,
            w_proj_pad,
            proj_bias,
            mlp_gain,
            mlp_shift,
            w_fc1,
            fc1_bias,
            w_fc2,
            fc2_bias,
        ),
        flops=8e9,
        in_specs=[smem] + [vmem] * 12,
        out_specs=[vmem] * 7,
    )
    big = Sum(fc_grads[0], fc_grads[1], len(stages()))
    d_in = big.send(d_in)
    mlp_rows = width + di + 16
    mlp_grads, d_mid, d_att = call(
        turn_kernel,
        [
            sds((mlp_rows, width), BF16),
            sds((2 * half, width), BF16),
            sds((HEADS, 2 * half, LANES), BF16),
        ],
        (att, mid, d_in, cot, pooled, w_proj_pad, mlp_gain, vectors),
        flops=2e9,
        in_specs=[vmem] * 8,
        out_specs=[vmem] * 3,
    )
    d_att = big.merge(d_att)
    d_att = big.send(d_att)

    packs, dqs = [], []
    dn = None
    groups = ((0,), (1,), (2, 3))
    for group in groups:
        first, last = group[0] == 0, group[-1] == HEADS - 1
        n, h = len(group), group[0]
        args = [probs, key, value, query, d_att, low, w_kv_heads, pooled]
        specs = [
            pl.BlockSpec((1, 2 * half, chunk), lambda i, j, h=h: (h + i, 0, j)),
            pl.BlockSpec((1, chunk, LANES), lambda i, j, h=h: (h + i, j, 0)),
            pl.BlockSpec((1, chunk, LANES), lambda i, j, h=h: (h + i, j, 0)),
            pl.BlockSpec((1, 2 * half, LANES), lambda i, j, h=h: (h + i, 0, 0)),
            pl.BlockSpec((1, 2 * half, LANES), lambda i, j, h=h: (h + i, 0, 0)),
            pl.BlockSpec((chunk, 256), lambda i, j: (j, 0)),
            pl.BlockSpec((1, di, 2 * head_dim), lambda i, j, h=h: (h + i, 0, 0)),
            vmem,
        ]
        if not first:
            args.append(dn)
            specs.append(pl.BlockSpec((di, chunk), lambda i, j: (0, jnp.where(i == 0, j, chunks - 1))))
        if last:
            args.append(hat)
            specs.append(
                pl.BlockSpec((chunk, 256), lambda i, j, n=n: (jnp.where(i == n - 1, j, 0), 0))
            )
        results = call(
            functools.partial(backward_kernel, first, last, n, chunks, factor),
            [
                sds((di, 4 * room), BF16 if last else F32),
                sds((n, 208, 384), F32),
                sds((n, 2 * half, LANES), BF16),
            ]
            + [sds((di, 256), F32)] * last,
            args,
            flops=9e9 * n,
            vmem=48,
            grid=(n, chunks),
            in_specs=specs,
            out_specs=[
                pl.BlockSpec((di, chunk), lambda i, j, n=n: (0, jnp.where(i == n - 1, j, 0))),
                pl.BlockSpec((1, 208, 384), lambda i, j: (i, 0, 0)),
                pl.BlockSpec((1, 2 * half, LANES), lambda i, j: (i, 0, 0)),
            ]
            + [vmem] * last,
            scratch_shapes=[
                pltpu.VMEM((di, 4 * room), F32),
                pltpu.VMEM((2 * head_dim, 256), F32),
                pltpu.VMEM((2 * half, LANES), F32),
            ],
        )
        dn, pack, dq = results[:3]
        packs.append(pack)
        dqs.append(dq)
        if not last:
            dn = big.advance(dn)
        if first:
            dn, out_far = lax.optimization_barrier((dn, out_far))
            out_got = cross(out_far, 2)
    norm_sums = results[3]

    cut = 768
    sib_got = exchange(dn[:, 2 * room :], 0, 1)
    d_pool, grads = call(
        gather_kernel,
        [sds((2 * half, di), BF16), sds((2, cut, width), BF16)],
        (placed, norm_sums, *dqs, *packs, mlp_grads, d_mid, wq, w_res, pooled_hat),
        flops=1e9,
        vmem=32,
        in_specs=[smem] + [vmem] * 12,
        out_specs=[vmem] * 2,
    )
    small = Sum(grads[0], grads[1], 1)
    sib_got = small.send(sib_got)

    def end(own, like, tokens, spec):
        return call(
            functools.partial(end_kernel, own),
            [like],
            (placed, dn, sib_got, d_pool, spread, tokens, norm_gain),
            flops=1e9,
            vmem=32,
            grid_spec=pltpu.PrefetchScalarGridSpec(
                num_scalar_prefetch=1,
                grid=(1,),
                in_specs=[
                    pl.BlockSpec((di, 2 * room), lambda i, s: (0, 0)),
                    vmem,
                    vmem,
                    vmem,
                    spec,
                    vmem,
                ],
                out_specs=[vmem],
            ),
        )[0]

    grad_far = end(1, sds(raw.shape[1:], BF16), got, vmem)
    grad_got = cross(grad_far, 2)
    sib_got, grad_far = lax.optimization_barrier((sib_got, grad_far))
    sib_got = small.advance(sib_got)
    grad_tokens = end(
        0, sds(raw.shape, BF16), raw, pl.BlockSpec(one_clip, lambda i, s: (s[0], 0, 0, 0))
    )
    token = jnp.int32(0)
    while not big.done:
        token = big.advance(token)
    while not small.done:
        token = small.advance(token)

    grad_tokens = lax.dynamic_update_index_in_dim(grad_tokens, grad_got, 1 - clip_at, 0)
    block_out = lax.dynamic_update_index_in_dim(out, out_got, 1 - clip_at, 0)

    def outward(value, like):
        shape = (clip_count, like.shape[2], like.shape[3], frame_local, like.shape[4])
        return value.reshape(shape).transpose(0, 3, 1, 2, 4)

    s_fc2, s_fc1 = call(
        unpack_big_kernel,
        [sds((hidden, width), F32), sds((width, hidden), F32)],
        (placed, big.held, big.got[0]),
        in_specs=[smem] + [vmem] * 2,
        out_specs=[vmem] * 2,
    )
    vector = sds((width,), F32)
    (
        s_proj,
        s_res,
        s_fc1_bias,
        s_fc2_bias,
        s_mlp_gain,
        s_mlp_shift,
        s_proj_bias,
        s_res_bias,
        s_qkv,
        s_qv_bias,
        s_norm_gain,
        s_norm_shift,
    ) = call(
        unpack_small_kernel,
        [sds((width, width), F32), sds((di, width), F32), sds((hidden,), F32)]
        + [vector] * 5
        + [sds((di, 3 * width), F32), sds((2, width), F32)]
        + [sds((di,), F32)] * 2,
        (placed, small.held, small.got[0]),
        vmem=24,
        in_specs=[smem] + [vmem] * 2,
        out_specs=[vmem] * 12,
        scratch_shapes=[pltpu.VMEM((2, cut, width), BF16)],
    )
    return (
        outward(block_out, cotangent),
        outward(grad_tokens, tokens),
        s_norm_gain,
        s_norm_shift,
        s_qkv,
        s_qv_bias,
        s_proj,
        s_proj_bias,
        s_res,
        s_res_bias,
        s_mlp_gain,
        s_mlp_shift,
        s_fc1,
        s_fc1_bias,
        s_fc2,
        s_fc2_bias,
    )


def solution(mesh):
    split = P("clips", "units", None, None, None)
    return jax.shard_map(
        body,
        mesh=mesh,
        in_specs=(split, split, P("clips")) + (P(),) * 14,
        out_specs=(split, split) + (P(),) * 14,
        check_vma=False,
    )
```

```python
import functools

import jax
import jax.numpy as jnp
import numpy as np
from jax import lax
from jax.experimental import pallas as pl
from jax.experimental.pallas import tpu as pltpu
from jax.sharding import PartitionSpec as P

HEADS = 4
LANES = 128
EPS = 1e-06
LOG2E = 1.4426950408889634
ABSENT = -1e30
BOTH = ("clips_far", "next_x", "next_y", "core")
F32 = jnp.float32
BF16 = jnp.bfloat16
MIB = 2**20


def dot(left, right, dim_left=1, dim_right=0):
    return lax.dot_general(
        left, right, (((dim_left,), (dim_right,)), ((), ())), preferred_element_type=F32
    )


def norm_stats(value):
    centre = value - jnp.mean(value, axis=-1, keepdims=True)
    scale_inv = lax.rsqrt(jnp.mean(centre * centre, axis=-1, keepdims=True) + EPS)
    return centre * scale_inv, scale_inv


def norm_back(d_hat, hat, scale_inv):
    first = jnp.mean(d_hat, axis=-1, keepdims=True)
    second = jnp.mean(d_hat * hat, axis=-1, keepdims=True)
    return scale_inv * (d_hat - first - hat * second)


def three_parts(value):
    high = value.astype(BF16).astype(F32)
    rest = value - high
    middle = rest.astype(BF16).astype(F32)
    return high, middle, rest - middle


def with_columns(base, lane, column):
    high, middle, small = three_parts(-column)
    out = jnp.where(lane == 96, high, base)
    out = jnp.where(lane == 98, middle, out)
    return jnp.where(lane == 99, small, out)


def own_place():
    return lax.axis_index("next_y"), lax.axis_index("core")


def pack_rows(value):
    rows = value.shape[0]
    rest = jnp.concatenate([value[: rows // 2, LANES:], value[rows // 2 :, LANES:]], axis=1)
    return value[:, :LANES], rest


def unpack_half(ref, half):
    rows = ref.shape[0] * 2 // 3
    size = rows // 2
    side = (ref.shape[1] // 2) * half
    first = ref[half * size : (half + 1) * size, :].astype(F32)
    rest = ref[rows:, :].astype(F32)[:, side : side + ref.shape[1] // 2]
    return jnp.concatenate([first, rest], axis=1)


def pick_kernel(other, raw_ref, out_ref, tokens_ref, sem):
    clip, _ = own_place()
    copy = pltpu.make_async_copy(raw_ref.at[1 - clip if other else clip], tokens_ref, sem)
    copy.start()
    copy.wait()
    positions, _, di = tokens_ref.shape
    rows = 2 * positions
    first, rest = pack_rows(tokens_ref[...].reshape(rows, di).astype(F32))
    out_ref[:rows, :] = first.astype(BF16)
    out_ref[rows:, :] = rest.astype(BF16)


def weights_kernel(w_qkv_ref, qv_bias_ref, w_proj_ref, wq_ref, wkv_ref, heads_ref, proj_ref, bias_ref):
    di = w_qkv_ref.shape[0]
    width = w_proj_ref.shape[0]
    size = width // HEADS

    def by_head(value):
        pad = jnp.zeros((value.shape[0], LANES - size), value.dtype)
        pieces = []
        for h in range(HEADS):
            pieces += [value[:, h * size : (h + 1) * size], pad]
        return jnp.concatenate(pieces, axis=1)

    w = w_qkv_ref[...].astype(F32)
    query, key, value = (w[:, i * width : (i + 1) * width] for i in range(3))
    wq_ref[...] = by_head(query).astype(BF16)
    wkv_ref[:, : HEADS * LANES] = by_head(key).astype(BF16)
    wkv_ref[:, HEADS * LANES :] = by_head(value).astype(BF16)
    for h in range(HEADS):
        at = slice(h * size, (h + 1) * size)
        heads_ref[h] = jnp.concatenate([key[:, at], value[:, at]], axis=1).astype(BF16)
        proj_ref[h * LANES : h * LANES + size, :] = w_proj_ref[at, :]
        proj_ref[h * LANES + size : (h + 1) * LANES, :] = jnp.zeros((LANES - size, width), BF16)
    lane = lax.broadcasted_iota(jnp.int32, (8, HEADS * LANES), 1) % LANES
    ones = jnp.where((lane == 96) | (lane >= 98) & (lane < 100), 1.0, 0.0)
    biases = by_head(jnp.broadcast_to(qv_bias_ref[0:1, :], (8, width)))
    bias_ref[0:8, :] = biases
    bias_ref[8:16, :] = by_head(jnp.broadcast_to(qv_bias_ref[1:2, :], (8, width))) + ones
    bias_ref[16:24, :] = ones


def row_of(ref):
    return ref[...].reshape(1, ref.shape[-1])


def keys_of(tokens, base, first_mask, second_mask, refs, targets):
    gain_ref, shift_ref, wkv_ref, bias_ref = refs
    key_ref, value_ref, low_ref, hat_ref, peak_ref = targets
    rows, di = tokens.shape
    wide = HEADS * LANES
    hat, _ = norm_stats(tokens)
    low = (hat * row_of(gain_ref) + row_of(shift_ref)).astype(BF16)
    at = pl.ds(base, rows)
    low_ref[at, :di] = low
    hat_ref[at, :di] = hat.astype(BF16)
    key = dot(low, wkv_ref[:, :wide])
    squares = key[:, :LANES] * key[:, :LANES]
    for h in range(1, HEADS):
        squares = squares + key[:, h * LANES : (h + 1) * LANES] * key[:, h * LANES : (h + 1) * LANES]
    top = jnp.max(jnp.sum(squares, axis=-1, keepdims=True))
    peak_ref[...] = jnp.maximum(peak_ref[...], top)
    row = lax.broadcasted_iota(jnp.int32, (8, wide), 0) % 2
    lane = lax.broadcasted_iota(jnp.int32, (8, wide), 1) % LANES
    mask = jnp.where(row == 0, first_mask, second_mask)
    pattern = bias_ref[16:24, :] + jnp.where(lane == 97, mask, 0.0)
    key = (key.reshape(rows // 8, 8, wide) + pattern[None]).reshape(rows, wide).astype(BF16)
    for h in range(HEADS):
        key_ref[h, at, :] = key[:, h * LANES : (h + 1) * LANES]
    value = dot(low, wkv_ref[:, wide:])
    value = (value.reshape(rows // 8, 8, wide) + bias_ref[8:16, :][None]).reshape(rows, wide)
    value = value.astype(BF16)
    for h in range(HEADS):
        value_ref[h, at, :] = value[:, h * LANES : (h + 1) * LANES]


def fill_pads(base, rows, room, di, targets):
    key_ref, value_ref, low_ref, hat_ref, _ = targets
    empty = room - rows
    lane = lax.broadcasted_iota(jnp.int32, (empty, LANES), 1)
    at = slice(base + rows, base + room)
    for h in range(HEADS):
        key_ref[h, at, :] = jnp.where(lane == 97, ABSENT, 0.0).astype(BF16)
        value_ref[h, at, :] = jnp.zeros((empty, LANES), BF16)
    tail = lax.broadcasted_iota(jnp.int32, (room, LANES), 1)
    ones_tail = jnp.where(tail == di - LANES, 1.0, 0.0).astype(BF16)
    for ref in (low_ref, hat_ref):
        ref[base : base + room, LANES:] = ones_tail
        ref[at, :di] = jnp.zeros((empty, di), BF16)


def absent(frames_ref, holder, frame):
    clip, core = own_place()
    index = 2 * ((2 * clip + core) ^ holder) + frame
    return jnp.where(index < frames_ref[clip], 0.0, ABSENT).astype(F32)


def near_kernel(
    frames_ref,
    raw_ref,
    near_ref,
    gain_ref,
    shift_ref,
    wkv_ref,
    bias_ref,
    pool_ref,
    key_out,
    value_out,
    low_out,
    hat_out,
    pooled_ref,
    pooled_hat_ref,
    peak_ref,
    key_ref,
    value_ref,
    low_ref,
    hat_ref,
    mine_ref,
    sems,
):
    positions, _, di = mine_ref.shape
    rows = 2 * positions
    clip, _ = own_place()
    load = pltpu.make_async_copy(raw_ref.at[clip], mine_ref, sems.at[8])
    load.start()
    load.wait()
    room = key_ref.shape[1] // 2
    refs = (gain_ref, shift_ref, wkv_ref, bias_ref)
    targets = (key_ref, value_ref, low_ref, hat_ref, peak_ref)
    peak_ref[...] = jnp.zeros(peak_ref.shape, F32)
    pieces = 2
    step = positions // pieces
    copies = []
    for i in range(2):
        base = i * room
        fill_pads(base, rows, room, di, targets)

        for j in range(pieces):
            if i == 0:
                tokens = mine_ref[j * step : (j + 1) * step].reshape(2 * step, di).astype(F32)
            else:
                tokens = unpack_half(near_ref, j)
            keys_of(
                tokens,
                base + 2 * j * step,
                absent(frames_ref, i, 0),
                absent(frames_ref, i, 1),
                refs,
                targets,
            )

        at, to = pl.ds(base, room), pl.ds(2 * base, room)
        for k, (src, dst) in enumerate(((key_ref, key_out), (value_ref, value_out))):
            copies.append(
                pltpu.make_async_copy(src.at[:, at, :], dst.at[:, to, :], sems.at[4 * i + k])
            )
        for k, (src, dst) in enumerate(((low_ref, low_out), (hat_ref, hat_out))):
            copies.append(
                pltpu.make_async_copy(src.at[at, :], dst.at[to, :], sems.at[4 * i + k + 2])
            )
        for copy in copies[-4:]:
            copy.start()
    pooled_ref[...] = dot(pool_ref[...], low_ref[:rows, :di])
    pooled_hat_ref[...] = dot(pool_ref[...], hat_ref[:rows, :di])
    for copy in copies:
        copy.wait()


def forward_kernel(
    dims,
    frames_ref,
    got_ref,
    near_got_ref,
    gain_ref,
    shift_ref,
    wkv_ref,
    bias_ref,
    wq_ref,
    wres_ref,
    res_bias_ref,
    pool_ref,
    pooled_in,
    pooled_hat_in,
    peak_in,
    key_in,
    value_in,
    low_in,
    hat_in,
    probs_ref,
    att_ref,
    residual_ref,
    pooled_ref,
    pooled_hat_ref,
    key_out,
    value_out,
    query_out,
    low_out,
    hat_out,
    key_ref,
    value_ref,
    query_ref,
    low_ref,
    hat_ref,
    acc_ref,
    norm_ref,
    peak_ref,
    sems,
):
    di, rows, room, half, chunk, chunks, head_dim = dims
    positions = rows // 2
    head = pl.program_id(0)
    step = pl.program_id(1)
    factor = 1.0 / head_dim**0.5
    loads, stores = [], []
    for i in range(2):
        at, to = pl.ds(2 * i * room, room), pl.ds((2 * i + 1) * room, room)
        for k, (src, dst) in enumerate(((key_in, key_ref), (value_in, value_ref))):
            loads.append(
                pltpu.make_async_copy(src.at[:, at, :], dst.at[:, at, :], sems.at[2 * i + k])
            )
        for k, (src, dst) in enumerate(((key_ref, key_out), (value_ref, value_out))):
            stores.append(
                pltpu.make_async_copy(src.at[:, to, :], dst.at[:, to, :], sems.at[4 + 2 * i + k])
            )
        for k, (src, dst) in enumerate(((low_ref, low_out), (hat_ref, hat_out))):
            stores.append(
                pltpu.make_async_copy(
                    src.at[pl.ds(i * room, room), :], dst.at[to, :], sems.at[8 + 2 * i + k]
                )
            )
    stores.append(pltpu.make_async_copy(query_ref, query_out, sems.at[12]))

    @pl.when((head == 0) & (step == 0))
    def _():
        for copy in loads:
            copy.start()
        refs = (gain_ref, shift_ref, wkv_ref, bias_ref)
        norm_ref[...] = peak_in[...]
        pieces = 2
        size = positions // pieces
        for i, ref in enumerate((got_ref, near_got_ref)):
            keys = (
                key_ref.at[:, pl.ds((2 * i + 1) * room, room), :],
                value_ref.at[:, pl.ds((2 * i + 1) * room, room), :],
                low_ref.at[pl.ds(i * room, room), :],
                hat_ref.at[pl.ds(i * room, room), :],
                norm_ref,
            )
            fill_pads(0, rows, room, di, keys)

            for j in range(pieces):
                keys_of(
                    unpack_half(ref, j),
                    2 * j * size,
                    absent(frames_ref, 2 + i, 0),
                    absent(frames_ref, 2 + i, 1),
                    refs,
                    keys,
                )

        for copy in stores[:-1]:
            copy.start()
        tail = lax.broadcasted_iota(jnp.int32, (2 * half, LANES), 1)
        ones_tail = jnp.where(tail == di - LANES, 1.0, 0.0).astype(BF16)
        pooled_ref[:, LANES:] = ones_tail
        pooled_hat_ref[:, LANES:] = ones_tail
        pooled = jnp.concatenate([pooled_in[...], dot(pool_ref[...], low_ref[:rows, :di])], axis=0)
        high = pooled.astype(BF16)
        rest = (pooled - high.astype(F32)).astype(BF16)
        pooled_ref[:, :di] = high
        pooled_hat_ref[:, :di] = jnp.concatenate(
            [pooled_hat_in[...], dot(pool_ref[...], hat_ref[:rows, :di])], axis=0
        ).astype(BF16)
        residual_ref[...] = (
            dot(high, wres_ref[...]) + dot(rest, wres_ref[...]) + row_of(res_bias_ref)
        )
        query = dot(high, wq_ref[...]) + dot(rest, wq_ref[...]) + bias_ref[0:1, :]
        query = query.astype(BF16).astype(F32)
        lane = lax.broadcasted_iota(jnp.int32, (2 * half, LANES), 1)
        top = jnp.float32(0.0)
        for h in range(HEADS):
            part_h = query[:, h * LANES : (h + 1) * LANES]
            top = jnp.maximum(top, jnp.max(jnp.sum(part_h * part_h, axis=-1, keepdims=True)))
            query_ref[h] = jnp.where(lane == 97, 1.0, part_h).astype(BF16)
        for copy in loads:
            copy.wait()
        reach = jnp.sqrt(jnp.max(norm_ref[...]) * top) * (1.02 * factor)

        @pl.when(jnp.logical_not(reach < 60.0))
        def _():
            peak_ref[...] = jnp.full((2 * half, LANES), -3e38, F32)

            @pl.loop(0, HEADS)
            def _(h):
                @pl.loop(0, chunks)
                def _(j):
                    at = pl.ds(pl.multiple_of(j * chunk, LANES), chunk)
                    scores = dot(query_ref[h], key_ref[h, at, :], 1, 1)
                    highest = jnp.max(scores, axis=-1, keepdims=True)
                    peak_ref[...] = jnp.where(
                        lane == h, jnp.maximum(peak_ref[...], highest), peak_ref[...]
                    )

            for h in range(HEADS):
                query_ref[h] = with_columns(
                    query_ref[h].astype(F32), lane, peak_ref[:, h : h + 1]
                ).astype(BF16)

        stores[-1].start()

    at = pl.ds(pl.multiple_of(step * chunk, LANES), chunk)
    scores = dot(query_ref[head], key_ref[head, at, :], 1, 1)
    probs = jnp.exp2(scores * (factor * LOG2E)).astype(BF16)
    probs_ref[0] = probs
    gathered = dot(probs, value_ref[head, at, :])

    @pl.when(step == 0)
    def _():
        acc_ref[...] = gathered

    @pl.when(step > 0)
    def _():
        acc_ref[...] += gathered

    @pl.when(step == chunks - 1)
    def _():
        lane = lax.broadcasted_iota(jnp.int32, (2 * half, LANES), 1)
        acc = acc_ref[...]
        total_inv = 1.0 / acc[:, 96:97]
        att_ref[0] = jnp.where(
            lane < 96, acc * total_inv, jnp.where(lane == 96, total_inv, 0.0)
        )

    @pl.when((head == HEADS - 1) & (step == chunks - 1))
    def _():
        for copy in stores:
            copy.wait()


def halves_out(halves_ref, keep_ref, give_ref, sems):
    core = lax.axis_index("core")
    copies = [
        pltpu.make_async_copy(halves_ref.at[core], keep_ref, sems.at[0]),
        pltpu.make_async_copy(halves_ref.at[1 - core], give_ref, sems.at[1]),
    ]
    for copy in copies:
        copy.start()
    return copies


def middle_kernel(
    att_ref,
    residual_ref,
    cot_ref,
    cot_got_ref,
    wproj_ref,
    proj_bias_ref,
    gain_ref,
    shift_ref,
    wfc1_ref,
    fc1_bias_ref,
    wfc2_ref,
    fc2_bias_ref,
    out_ref,
    out_far_ref,
    keep_ref,
    give_ref,
    vec_ref,
    d_in_ref,
    mid_ref,
    cot_out_ref,
    halves_ref,
    sems,
):
    clip, _ = own_place()
    count = att_ref.shape[1]
    half = count // 2
    width = residual_ref.shape[1]
    hidden = wfc1_ref.shape[1]
    lane = lax.broadcasted_iota(jnp.int32, (count, LANES), 1)
    attended = jnp.concatenate(
        [jnp.where(lane < 96, att_ref[h], 0.0).astype(BF16) for h in range(HEADS)], axis=1
    )
    mid = dot(attended, wproj_ref[...]) + row_of(proj_bias_ref) + residual_ref[...]
    mid_ref[...] = mid
    hat, scale_inv = norm_stats(mid)
    mlp_in = (hat * row_of(gain_ref) + row_of(shift_ref)).astype(BF16)
    cot32 = jnp.concatenate(
        [
            cot_ref[clip].reshape(half, width).astype(F32),
            cot_got_ref[...].reshape(half, width).astype(F32),
        ],
        axis=0,
    )
    cot = cot32.astype(BF16)
    cot_out_ref[...] = cot
    d_in = jnp.zeros((count, width), F32)
    out = mid + row_of(fc2_bias_ref)
    piece = 512
    fc1_bias = row_of(fc1_bias_ref)
    copies, sums = [], []
    for i in range(hidden // piece):
        at = slice(i * piece, (i + 1) * piece)
        x = dot(mlp_in, wfc1_ref[:, at]) + fc1_bias[:, at]
        c0 = 0.7978845608028654
        square = x * x
        th = jnp.tanh(c0 * x * (1.0 + 0.044715 * square))
        half_up = 0.5 * (1.0 + th)
        act = (x * half_up).astype(BF16)
        slope = half_up + (0.5 * c0) * x * (1.0 - th * th) * (1.0 + (3 * 0.044715) * square)
        out = out + dot(act, wfc2_ref[at, :])
        halves_ref[0, at, :] = dot(act, cot, 0, 0).astype(BF16)
        d_pre = (dot(cot, wfc2_ref[at, :], 1, 1) * slope).astype(BF16)
        g_fc1 = dot(mlp_in, d_pre, 0, 0).astype(BF16)
        for col in range(0, piece, LANES):
            block, lane_at = divmod(i * piece + col, width)
            halves_ref[1, block * width : (block + 1) * width, lane_at : lane_at + LANES] = g_fc1[
                :, col : col + LANES
            ]
        sums.append(jnp.sum(d_pre.astype(F32), axis=0, keepdims=True))
        d_in = d_in + dot(d_pre, wfc1_ref[:, at], 1, 1)
    copies = halves_out(halves_ref, keep_ref, give_ref, sems)
    sums = jnp.concatenate(sums, axis=1)
    blocks = hidden // width
    vec_row = lax.broadcasted_iota(jnp.int32, (8, width), 0)
    vectors = jnp.where(vec_row == blocks, jnp.sum(cot32, axis=0, keepdims=True), 0.0)
    for i in range(blocks):
        vectors = jnp.where(vec_row == i, sums[:, i * width : (i + 1) * width], vectors)
    vec_ref[...] = vectors
    d_in_ref[...] = d_in
    out_ref[clip] = out[:half].astype(BF16).reshape(out_far_ref.shape)
    out_far_ref[...] = out[half:].astype(BF16).reshape(out_far_ref.shape)
    for copy in copies:
        copy.wait()


def turn_kernel(
    att_ref,
    mid_ref,
    d_in_ref,
    cot_ref,
    pooled_ref,
    wproj_ref,
    gain_ref,
    vec_ref,
    keep_ref,
    give_ref,
    d_mid_ref,
    d_att_ref,
    halves_ref,
    sems,
):
    count, width = mid_ref.shape
    size = width // HEADS
    lane = lax.broadcasted_iota(jnp.int32, (count, LANES), 1)
    hat, scale_inv = norm_stats(mid_ref[...])
    d_in = d_in_ref[...]
    d_mid = cot_ref[...].astype(F32) + norm_back(d_in * row_of(gain_ref), hat, scale_inv)
    d_mid = d_mid.astype(BF16)
    d_mid_ref[...] = d_mid
    d_att = dot(d_mid, wproj_ref[...], 1, 1).astype(BF16).astype(F32)
    for h in range(HEADS):
        att = att_ref[h]
        scaled = (d_att[:, h * LANES : (h + 1) * LANES] * att[:, 96:97]).astype(BF16).astype(F32)
        delta = jnp.sum(jnp.where(lane < 96, scaled * att, 0.0), axis=-1, keepdims=True)
        d_att_ref[h] = with_columns(scaled, lane, delta).astype(BF16)
        halves_ref[0, size * h : size * (h + 1), :] = dot(
            jnp.where(lane < 96, att, 0.0).astype(BF16), d_mid, 0, 0
        )[:size].astype(BF16)
    di = 2 * size
    halves_ref[1, :di, :] = dot(pooled_ref[...], d_mid, 0, 0)[:di].astype(BF16)
    row = lax.broadcasted_iota(jnp.int32, (8, width), 0)
    extra = jnp.where(row == 0, jnp.sum(d_in * hat, axis=0, keepdims=True), 0.0)
    extra = jnp.where(row == 1, jnp.sum(d_in, axis=0, keepdims=True), extra)
    extra = jnp.where(row == 2, jnp.sum(d_mid.astype(F32), axis=0, keepdims=True), extra)
    halves_ref[1, di : di + 16, :] = jnp.concatenate([vec_ref[...], extra], axis=0).astype(BF16)
    halves_ref[1, di + 16 :, :] = jnp.zeros((width - di - 16, width), BF16)
    for copy in halves_out(halves_ref, keep_ref, give_ref, sems):
        copy.wait()


def backward_kernel(
    first,
    last,
    heads,
    chunks,
    factor,
    probs_ref,
    key_ref,
    value_ref,
    query_ref,
    d_att_ref,
    low_ref,
    wkv_ref,
    pooled_ref,
    *rest,
):
    rest = list(rest)
    prev_ref = None if first else rest.pop(0)
    hat_ref = rest.pop(0) if last else None
    out_ref, pack_ref, dq_ref = rest[:3]
    norm_ref = rest[3] if last else None
    dn_ref, gw_ref, acc_ref = rest[-3:]
    head, step = pl.program_id(0), pl.program_id(1)
    chunk = probs_ref.shape[2]
    at = pl.ds(pl.multiple_of(step * chunk, LANES), chunk)
    probs = probs_ref[0]
    d_prob = dot(d_att_ref[0], value_ref[0], 1, 1)
    d_value = dot(d_att_ref[0], probs, 0, 0)[:96]
    d_scores = (probs.astype(F32) * d_prob).astype(BF16)
    d_key = dot(query_ref[0], d_scores, 0, 0)[:96] * factor
    d_query = dot(d_scores, key_ref[0])
    both = jnp.concatenate([d_key, d_value], axis=0).astype(BF16)
    back = dot(wkv_ref[0], both)
    g_w = dot(both, low_ref[...])

    @pl.when(head == 0)
    def _():
        dn_ref[:, at] = back if first else prev_ref[...] + back

    if heads > 1:

        @pl.when(head > 0)
        def _():
            dn_ref[:, at] += back

    @pl.when(head == heads - 1)
    def _():
        dn = dn_ref[:, at].astype(out_ref.dtype)
        out_ref[...] = dn
        if last:
            sums = dot(dn, hat_ref[...])
            norm_ref[...] = jnp.where(step == 0, sums, norm_ref[...] + sums)

    @pl.when(step == 0)
    def _():
        gw_ref[...] = g_w
        acc_ref[...] = d_query

    @pl.when(step > 0)
    def _():
        gw_ref[...] += g_w
        acc_ref[...] += d_query

    @pl.when(step == chunks - 1)
    def _():
        lane = lax.broadcasted_iota(jnp.int32, acc_ref.shape, 1)
        dq = jnp.where(lane < 96, acc_ref[...] * factor, 0.0).astype(BF16)
        dq_ref[0] = dq
        g_q = dot(pooled_ref[...], dq, 0, 0)
        size = gw_ref.shape[0]
        rows = pack_ref.shape[1]
        pack_ref[0, :size, :256] = gw_ref[...]
        pack_ref[0, :, 256:] = g_q[:rows]
        pack_ref[0, size:, :256] = jnp.zeros((rows - size, 256), F32)


def gather_kernel(
    norm_ref,
    dq0_ref,
    dq1_ref,
    pack0_ref,
    pack1_ref,
    d_mid_ref,
    wq_ref,
    wres_ref,
    pooled_hat_ref,
    d_pool_ref,
    keep_ref,
    give_ref,
    halves_ref,
    sems,
):
    di = wq_ref.shape[0]
    d_pool = dot(d_mid_ref[...], wres_ref[...], 1, 1)
    for h, dq in enumerate((dq0_ref[0], dq1_ref[0], dq1_ref[1], dq1_ref[2])):
        d_pool = d_pool + dot(dq, wq_ref[:, h * LANES : (h + 1) * LANES], 1, 1)
    low = d_pool.astype(BF16)
    d_pool_ref[...] = low
    both = norm_ref[...] + dot(low, pooled_hat_ref[...], 0, 0)
    row = lax.broadcasted_iota(jnp.int32, both.shape, 0)
    col = lax.broadcasted_iota(jnp.int32, both.shape, 1)
    gain = jnp.sum(jnp.where(row == col, both, 0.0), axis=1, keepdims=True)
    lane = lax.broadcasted_iota(jnp.int32, (di, LANES), 1)
    norms = jnp.where(lane == 65, gain, jnp.where(lane == 66, both[:, di : di + 1], 0.0))
    pieces = []
    for pack in (pack0_ref[0], pack1_ref[0], pack1_ref[1]):
        pieces.append(pack.astype(BF16))
    last = pack1_ref[2]
    middle = last[:, LANES : 2 * LANES] + jnp.concatenate(
        [norms, jnp.zeros((last.shape[0] - di, LANES), F32)], axis=0
    )
    pieces.append(
        jnp.concatenate([last[:, :LANES], middle, last[:, 2 * LANES :]], axis=1).astype(BF16)
    )
    cut, width = keep_ref.shape
    pieces.append(jnp.zeros((2 * cut - sum(p.shape[0] for p in pieces), width), BF16))
    at = 0
    for piece in pieces:
        size = piece.shape[0]
        done = 0
        while done < size:
            side, row = divmod(at + done, cut)
            take = min(size - done, cut - row)
            halves_ref[side, row : row + take, :] = piece[done : done + take]
            done += take
        at += size
    for copy in halves_out(halves_ref, keep_ref, give_ref, sems):
        copy.wait()


def end_kernel(
    dn_ref,
    got_ref,
    d_pool_ref,
    spread_ref,
    raw_ref,
    far_ref,
    gain_ref,
    out_ref,
    out_far_ref,
    held_ref,
    sem,
):
    clip, _ = own_place()
    load = pltpu.make_async_copy(raw_ref.at[clip], held_ref, sem)
    load.start()
    positions, _, di = held_ref.shape
    rows = 2 * positions
    half = spread_ref.shape[1]
    room = dn_ref.shape[1] // 2
    for own in (1, 0):
        start = own * room
        lead = start % LANES
        at = slice(start - lead, start - lead + -(-(lead + rows) // LANES) * LANES)
        turned = (dn_ref[:, at].astype(F32) + got_ref[:, at].astype(F32)).T[lead : lead + rows]
        spread = dot(spread_ref[...], d_pool_ref[own * half : (own + 1) * half, :])
        if own == 0:
            load.wait()
            tokens = held_ref[...].reshape(rows, di).astype(F32)
        else:
            tokens = jnp.concatenate([unpack_half(far_ref, 0), unpack_half(far_ref, 1)], axis=0)
        hat, scale_inv = norm_stats(tokens)
        grad = norm_back((turned + spread) * row_of(gain_ref), hat, scale_inv)
        if own == 0:
            out_ref[clip] = grad.astype(BF16).reshape(positions, 2, di)
        else:
            first, rest = pack_rows(grad)
            out_far_ref[:rows, :] = first.astype(BF16)
            out_far_ref[rows:, :] = rest.astype(BF16)


def finish_kernel(tokens_in, out_in, got_ref, out_got_ref, tokens_ref, out_ref, held_ref, sems):
    clip, _ = own_place()
    positions, _, di = held_ref.shape
    copies = [
        pltpu.make_async_copy(out_got_ref, out_ref.at[1 - clip], sems.at[0]),
        pltpu.make_async_copy(held_ref, tokens_ref.at[1 - clip], sems.at[1]),
    ]
    copies[0].start()
    for j in range(2):
        at = slice(j * positions // 2, (j + 1) * positions // 2)
        held_ref[at] = unpack_half(got_ref, j).astype(BF16).reshape(positions // 2, 2, di)
    copies[1].start()
    for copy in copies:
        copy.wait()


def unpack_big_kernel(
    own_ref,
    other_ref,
    fc2_ref,
    fc1_ref,
    proj_ref,
    res_ref,
    fc1_bias_ref,
    fc2_bias_ref,
    mlp_gain_ref,
    mlp_shift_ref,
    proj_bias_ref,
    res_bias_ref,
):
    _, core = own_place()
    width = own_ref.shape[1]
    hidden = fc2_ref.shape[0]
    di = res_ref.shape[0]

    def write(first, second):
        fc2_ref[...] = first[:hidden, :].astype(F32)
        for i in range(hidden // width):
            at = slice(i * width, (i + 1) * width)
            fc1_ref[:, at] = second[at, :].astype(F32)
        proj_ref[...] = first[hidden : hidden + width, :].astype(F32)
        res_ref[...] = second[hidden : hidden + di, :].astype(F32)
        vectors = second[hidden + di : hidden + di + 16, :].astype(F32)
        blocks = hidden // width
        fc1_bias_ref[...] = jnp.concatenate([vectors[i : i + 1] for i in range(blocks)], axis=1)[0]
        fc2_bias_ref[...] = vectors[blocks]
        mlp_gain_ref[...] = vectors[8]
        mlp_shift_ref[...] = vectors[9]
        proj_bias_ref[...] = vectors[10]
        res_bias_ref[...] = vectors[10]

    @pl.when(core == 0)
    def _():
        write(own_ref, other_ref)

    @pl.when(core == 1)
    def _():
        write(other_ref, own_ref)


def unpack_small_kernel(
    own_ref,
    other_ref,
    qkv_ref,
    qv_bias_ref,
    norm_gain_ref,
    norm_shift_ref,
    whole_ref,
):
    _, core = own_place()
    cut, width = own_ref.shape
    size = width // HEADS
    di = 2 * size
    whole_ref[core] = own_ref[...]
    whole_ref[1 - core] = other_ref[...]

    def rows(start, count):
        pieces = []
        while count:
            side, row = divmod(start, cut)
            take = min(count, cut - row)
            pieces.append(whole_ref[side, row : row + take, :])
            start, count = start + take, count - take
        return (pieces[0] if len(pieces) == 1 else jnp.concatenate(pieces, axis=0)).astype(F32)

    start = 0
    queries, keys, values, q_bias, v_bias = [], [], [], [], []
    for h in range(HEADS):
        pack = rows(start + 208 * h, 208)
        queries.append(pack[:di, 256 : 256 + size])
        turned = pack[:di, :256].T
        keys.append(turned[:di, :size])
        values.append(turned[:di, size:])
        q_bias.append(pack[di : di + 1, 256 : 256 + size])
        v_bias.append(turned[di : di + 1, size:])
    qkv_ref[...] = jnp.concatenate(queries + keys + values, axis=1)
    qv_bias_ref[0:1, :] = jnp.concatenate(q_bias, axis=1)
    qv_bias_ref[1:2, :] = jnp.concatenate(v_bias, axis=1)
    norm_gain_ref[...] = turned[di + 1]
    norm_shift_ref[...] = turned[di + 2]


def sizes():
    return [lax.axis_size(name) for name in BOTH]


def exchange(value, mask):
    count = int(np.prod(sizes()))
    return lax.ppermute(value, BOTH, [(i, i ^ mask) for i in range(count)])


def stages():
    count = int(np.prod(sizes()))
    out = [(1, [1]), (2, [2, 4, 6])]
    bit = 8
    while bit < count:
        if bit * 2 < count:
            out.append((bit, [bit, 2 * bit, 3 * bit]))
            bit *= 4
        else:
            out.append((bit, [bit]))
            bit *= 2
    return out


def place(stage):
    return (lax.axis_index(BOTH) // stage[0]) % (len(stage[1]) + 1)


def sum_pieces(pieces):
    pieces = [p.astype(F32) for p in pieces]
    while len(pieces) > 1:
        pieces = [a + b for a, b in zip(pieces[::2], pieces[1::2])]
    return pieces[0]


class Sum:
    def __init__(self, keep, give, depth):
        self.plan = stages()
        self.depth = min(depth, len(self.plan) - 1)
        self.places = [place(stage) for stage in self.plan]
        self.held, self.pieces = keep, [give]
        self.at, self.back, self.done, self.summed = 0, False, False, False
        self.more = None

    def cut(self):
        masks = self.plan[self.at][1]
        if self.back or self.at > self.depth:
            self.pieces = [self.held] * len(masks)
            return
        size, where = len(masks) + 1, self.places[self.at]
        later = int(np.prod([len(self.plan[i][1]) + 1 for i in range(self.at + 1, self.depth + 1)]))
        rows, columns = self.held.shape
        whole = self.held.reshape(later, size, rows // (later * size), columns)

        def take(index):
            piece = lax.dynamic_index_in_dim(whole, index, 1, keepdims=False)
            return piece.reshape(rows // size, columns)

        self.held = take(where)
        self.pieces = [take(where ^ (k + 1)) for k in range(size - 1)]

    def send(self, other):
        (self.held, self.pieces), other = lax.optimization_barrier(((self.held, self.pieces), other))
        self.got = [exchange(p, mask) for p, mask in zip(self.pieces, self.plan[self.at][1])]
        self.done = self.back and self.at == 0
        return other

    def merge(self, other):
        (self.held, self.got), other = lax.optimization_barrier(((self.held, self.got), other))
        if not self.back:
            self.held = sum_pieces([self.held] + self.got).astype(BF16)
            if self.at == 0 and self.more is not None:
                self.held = jnp.concatenate([self.held, self.more])
            if self.at + 1 < len(self.plan):
                self.at += 1
            else:
                self.back, self.summed, self.at = True, True, self.depth
        else:
            size, where = len(self.got) + 1, self.places[self.at]
            stacked = jnp.stack([self.held] + self.got)
            self.held = jnp.concatenate(
                [
                    lax.dynamic_index_in_dim(stacked, where ^ k, 0, keepdims=False)
                    for k in range(size)
                ]
            )
            self.at -= 1
        self.cut()
        return other

    def advance(self, other):
        return other if self.done else self.send(self.merge(other))


def call(kernel, out_shape, args, flops=0, vmem=60, **kwargs):
    moved = sum(np.prod(a.shape) * a.dtype.itemsize for a in args) if flops else 1
    return pl.pallas_call(
        kernel,
        out_shape=out_shape,
        compiler_params=pltpu.CompilerParams(vmem_limit_bytes=vmem * MIB),
        cost_estimate=pl.CostEstimate(
            flops=int(max(flops, 1)), bytes_accessed=int(moved), transcendentals=0
        ),
        **kwargs,
    )(*args)


def body(
    tokens,
    cotangent,
    frames,
    norm_gain,
    norm_shift,
    w_qkv,
    qv_bias,
    w_proj,
    proj_bias,
    w_res,
    res_bias,
    mlp_gain,
    mlp_shift,
    w_fc1,
    fc1_bias,
    w_fc2,
    fc2_bias,
):
    clip_count, frame_local, grid_rows, grid_cols, di = tokens.shape
    width = w_proj.shape[0]
    head_dim = width // HEADS
    hidden = w_fc1.shape[1]
    frame = grid_rows * grid_cols
    rows = frame_local * frame
    half = rows // 4
    room = 1600
    chunk = 1280
    chunks = 4 * room // chunk
    wide = HEADS * LANES
    factor = 1.0 / head_dim**0.5
    vmem = pl.BlockSpec(memory_space=pltpu.VMEM)
    smem = pl.BlockSpec(memory_space=pltpu.SMEM)
    hbm = pl.BlockSpec(memory_space=pl.ANY)
    sds = jax.ShapeDtypeStruct

    raw = tokens.transpose(0, 2, 3, 1, 4).reshape(clip_count, frame, frame_local, di)
    cot_raw = cotangent.transpose(0, 2, 3, 1, 4).reshape(
        clip_count, frame // 4, frame_local, width
    )

    def pick(other):
        return call(
            functools.partial(pick_kernel, other),
            [sds((3 * rows // 2, LANES), BF16)],
            (raw,),
            vmem=16,
            in_specs=[hbm],
            out_specs=[vmem],
            scratch_shapes=[pltpu.VMEM(raw.shape[1:], BF16), pltpu.SemaphoreType.DMA],
        )[0]

    got = exchange(pick(True), 2)
    near = exchange(pick(False), 1)
    clip_at = lax.axis_index("next_y")
    cot_far = lax.dynamic_index_in_dim(cot_raw, 1 - clip_at, 0, keepdims=False)
    near, cot_far = lax.optimization_barrier((near, cot_far))
    cot_got = exchange(cot_far, 2)

    pool_np = np.zeros((half, rows), np.float32)
    token = np.arange(rows)
    position, f = token // frame_local, token % frame_local
    r, c = position // grid_cols, position % grid_cols
    pool_np[((r // 2) * (grid_cols // 2) + c // 2) * frame_local + f, token] = 0.25
    pool = jnp.asarray(pool_np, BF16)
    spread = jnp.asarray(pool_np.T, BF16)

    wq, wkv, w_kv_heads, w_proj_pad, bias = call(
        weights_kernel,
        [
            sds((di, wide), BF16),
            sds((di, 2 * wide), BF16),
            sds((HEADS, di, 2 * head_dim), BF16),
            sds((wide, width), BF16),
            sds((24, wide), F32),
        ],
        (w_qkv, qv_bias, w_proj),
        in_specs=[vmem] * 3,
        out_specs=[vmem] * 5,
    )
    whole = [
        sds((HEADS, 4 * room, LANES), BF16),
        sds((HEADS, 4 * room, LANES), BF16),
        sds((4 * room, 256), BF16),
        sds((4 * room, 256), BF16),
    ]
    key, value, low, hat, pooled_mine, pooled_hat_mine, peak = call(
        near_kernel,
        whole
        + [sds((half, di), F32), sds((half, di), F32), sds((8, LANES), F32)],
        (frames, raw, near, norm_gain, norm_shift, wkv, bias, pool),
        flops=3e9,
        in_specs=[smem, hbm] + [vmem] * 6,
        out_specs=[hbm] * 4 + [vmem] * 3,
        scratch_shapes=[
            pltpu.VMEM((HEADS, 2 * room, LANES), BF16),
            pltpu.VMEM((HEADS, 2 * room, LANES), BF16),
            pltpu.VMEM((2 * room, 256), BF16),
            pltpu.VMEM((2 * room, 256), BF16),
            pltpu.VMEM(raw.shape[1:], BF16),
            pltpu.SemaphoreType.DMA((9,)),
        ],
    )
    got, peak = lax.optimization_barrier((got, peak))
    near_got = exchange(got, 1)
    dims = (di, rows, room, half, chunk, chunks, head_dim)
    probs, att, residual, pooled, pooled_hat, key, value, query, low, hat = call(
        functools.partial(forward_kernel, dims),
        [
            sds((HEADS, 2 * half, 4 * room), BF16),
            sds((HEADS, 2 * half, LANES), F32),
            sds((2 * half, width), F32),
            sds((2 * half, 256), BF16),
            sds((2 * half, 256), BF16),
        ]
        + whole[:2]
        + [sds((HEADS, 2 * half, LANES), BF16)]
        + whole[2:],
        (
            frames,
            got,
            near_got,
            norm_gain,
            norm_shift,
            wkv,
            bias,
            wq,
            w_res,
            res_bias,
            pool,
            pooled_mine,
            pooled_hat_mine,
            peak,
            key,
            value,
            low,
            hat,
        ),
        flops=25e9,
        grid=(HEADS, chunks),
        in_specs=[smem] + [vmem] * 13 + [hbm] * 4,
        out_specs=[
            pl.BlockSpec((1, 2 * half, chunk), lambda h, j: (h, 0, j)),
            pl.BlockSpec((1, 2 * half, LANES), lambda h, j: (h, 0, 0)),
            vmem,
            vmem,
            vmem,
        ]
        + [hbm] * 5,
        input_output_aliases={14: 5, 15: 6, 16: 8, 17: 9},
        scratch_shapes=[
            pltpu.VMEM((HEADS, 4 * room, LANES), BF16),
            pltpu.VMEM((HEADS, 4 * room, LANES), BF16),
            pltpu.VMEM((HEADS, 2 * half, LANES), BF16),
            pltpu.VMEM((2 * room, 256), BF16),
            pltpu.VMEM((2 * room, 256), BF16),
            pltpu.VMEM((2 * half, LANES), F32),
            pltpu.VMEM((8, LANES), F32),
            pltpu.VMEM((2 * half, LANES), F32),
            pltpu.SemaphoreType.DMA((13,)),
        ],
    )

    out_raw = sds(cot_raw.shape, BF16)
    out_far = sds(cot_raw.shape[1:], BF16)
    out, out_far, fc_keep, fc_give, vectors, d_in, mid, cot = call(
        middle_kernel,
        [
            out_raw,
            out_far,
            sds((hidden, width), BF16),
            sds((hidden, width), BF16),
            sds((8, width), F32),
            sds((2 * half, width), F32),
            sds((2 * half, width), F32),
            sds((2 * half, width), BF16),
        ],
        (
            att,
            residual,
            cot_raw,
            cot_got,
            w_proj_pad,
            proj_bias,
            mlp_gain,
            mlp_shift,
            w_fc1,
            fc1_bias,
            w_fc2,
            fc2_bias,
        ),
        flops=8e9,
        in_specs=[vmem] * 12,
        out_specs=[vmem, vmem, hbm, hbm] + [vmem] * 4,
        scratch_shapes=[pltpu.VMEM((2, hidden, width), BF16), pltpu.SemaphoreType.DMA((2,))],
    )
    big = Sum(fc_keep, fc_give, 1)
    d_in = big.send(d_in)
    mlp_keep, mlp_give, d_mid, d_att = call(
        turn_kernel,
        [
            sds((width, width), BF16),
            sds((width, width), BF16),
            sds((2 * half, width), BF16),
            sds((HEADS, 2 * half, LANES), BF16),
        ],
        (att, mid, d_in, cot, pooled, w_proj_pad, mlp_gain, vectors),
        flops=2e9,
        in_specs=[vmem] * 8,
        out_specs=[hbm, hbm, vmem, vmem],
        scratch_shapes=[pltpu.VMEM((2, width, width), BF16), pltpu.SemaphoreType.DMA((2,))],
    )
    mlp_got = exchange(mlp_give, 1)
    big.more = sum_pieces([mlp_keep, mlp_got]).astype(BF16)
    d_att = big.merge(d_att)
    d_att = big.send(d_att)

    packs, dqs = [], []
    dn = None
    groups = ((0,), (1, 2, 3))
    for group in groups:
        first, last = group[0] == 0, group[-1] == HEADS - 1
        n, h = len(group), group[0]
        args = [probs, key, value, query, d_att, low, w_kv_heads, pooled]
        specs = [
            pl.BlockSpec((1, 2 * half, chunk), lambda i, j, h=h: (h + i, 0, j)),
            pl.BlockSpec((1, chunk, LANES), lambda i, j, h=h: (h + i, j, 0)),
            pl.BlockSpec((1, chunk, LANES), lambda i, j, h=h: (h + i, j, 0)),
            pl.BlockSpec((1, 2 * half, LANES), lambda i, j, h=h: (h + i, 0, 0)),
            pl.BlockSpec((1, 2 * half, LANES), lambda i, j, h=h: (h + i, 0, 0)),
            pl.BlockSpec((chunk, 256), lambda i, j: (j, 0)),
            pl.BlockSpec((1, di, 2 * head_dim), lambda i, j, h=h: (h + i, 0, 0)),
            vmem,
        ]
        if not first:
            args.append(dn)
            specs.append(pl.BlockSpec((di, chunk), lambda i, j: (0, jnp.where(i == 0, j, chunks - 1))))
        if last:
            args.append(hat)
            specs.append(
                pl.BlockSpec((chunk, 256), lambda i, j, n=n: (jnp.where(i == n - 1, j, 0), 0))
            )
        results = call(
            functools.partial(backward_kernel, first, last, n, chunks, factor),
            [
                sds((di, 4 * room), BF16 if last else F32),
                sds((n, 208, 384), F32),
                sds((n, 2 * half, LANES), BF16),
            ]
            + [sds((di, 256), F32)] * last,
            args,
            flops=9e9 * n,
            grid=(n, chunks),
            in_specs=specs,
            out_specs=[
                pl.BlockSpec((di, chunk), lambda i, j, n=n: (0, jnp.where(i == n - 1, j, 0))),
                pl.BlockSpec((1, 208, 384), lambda i, j: (i, 0, 0)),
                pl.BlockSpec((1, 2 * half, LANES), lambda i, j: (i, 0, 0)),
            ]
            + [vmem] * last,
            scratch_shapes=[
                pltpu.VMEM((di, 4 * room), F32),
                pltpu.VMEM((2 * head_dim, 256), F32),
                pltpu.VMEM((2 * half, LANES), F32),
            ],
        )
        dn, pack, dq = results[:3]
        packs.append(pack)
        dqs.append(dq)
        if first:
            dn = big.merge(dn)
            big.held, dn, out_far = lax.optimization_barrier((big.held, dn, out_far))
            dn = big.send(dn)
            out_got = exchange(out_far, 2)
        if last:
            dn, out_got = lax.optimization_barrier((dn, out_got))
            dn = big.merge(dn)
            while not big.summed:
                dn = big.merge(big.send(dn))
    norm_sums = results[3]

    cut = 448
    sib = dn[:, 2 * room :]
    sib, norm_sums = lax.optimization_barrier((sib, norm_sums))
    sib_got = exchange(sib, 1)
    norm_sums = big.send(norm_sums)
    d_pool, keep, give = call(
        gather_kernel,
        [sds((2 * half, di), BF16), sds((cut, width), BF16), sds((cut, width), BF16)],
        (norm_sums, *dqs, *packs, d_mid, wq, w_res, pooled_hat),
        in_specs=[vmem] * 9,
        out_specs=[vmem, hbm, hbm],
        scratch_shapes=[pltpu.VMEM((2, cut, width), BF16), pltpu.SemaphoreType.DMA((2,))],
    )
    small = Sum(keep, give, 1)
    sib_got = small.send(sib_got)
    sib_got = small.advance(sib_got)
    grad_tokens, grad_far = call(
        end_kernel,
        [sds(raw.shape, BF16), sds(got.shape, BF16)],
        (dn, sib_got, d_pool, spread, raw, got, norm_gain),
        grid=(1,),
        in_specs=[pl.BlockSpec((di, 2 * room), lambda i: (0, 0)), vmem, vmem, vmem, hbm, vmem, vmem],
        out_specs=[vmem, vmem],
        scratch_shapes=[pltpu.VMEM(raw.shape[1:], BF16), pltpu.SemaphoreType.DMA],
    )
    grad_far = small.advance(grad_far)
    grad_got = exchange(grad_far, 2)
    grad_tokens = big.advance(grad_tokens)
    big_own, big_other = big.held, big.got[0]
    vector = sds((width,), F32)
    (
        s_fc2,
        s_fc1,
        s_proj,
        s_res,
        s_fc1_bias,
        s_fc2_bias,
        s_mlp_gain,
        s_mlp_shift,
        s_proj_bias,
        s_res_bias,
    ) = call(
        unpack_big_kernel,
        [
            sds((hidden, width), F32),
            sds((width, hidden), F32),
            sds((width, width), F32),
            sds((di, width), F32),
            sds((hidden,), F32),
        ]
        + [vector] * 5,
        (big_own, big_other),
        vmem=24,
        in_specs=[vmem] * 2,
        out_specs=[vmem] * 10,
    )
    unpacked = (
        s_fc2,
        s_fc1,
        s_proj,
        s_res,
        s_fc1_bias,
        s_fc2_bias,
        s_mlp_gain,
        s_mlp_shift,
        s_proj_bias,
        s_res_bias,
    )
    while not small.summed:
        grad_got = small.advance(grad_got)
    unpacked = small.advance(unpacked)
    (
        s_fc2,
        s_fc1,
        s_proj,
        s_res,
        s_fc1_bias,
        s_fc2_bias,
        s_mlp_gain,
        s_mlp_shift,
        s_proj_bias,
        s_res_bias,
    ) = unpacked
    grad_tokens, block_out = call(
        finish_kernel,
        [sds(raw.shape, BF16), sds(cot_raw.shape, BF16)],
        (grad_tokens, out, grad_got, out_got),
        vmem=16,
        in_specs=[hbm, hbm, vmem, hbm],
        out_specs=[hbm, hbm],
        input_output_aliases={0: 0, 1: 1},
        scratch_shapes=[pltpu.VMEM(raw.shape[1:], BF16), pltpu.SemaphoreType.DMA((2,))],
    )

    def outward(value, like):
        shape = (clip_count, like.shape[2], like.shape[3], frame_local, like.shape[4])
        return value.reshape(shape).transpose(0, 3, 1, 2, 4)

    s_qkv, s_qv_bias, s_norm_gain, s_norm_shift = call(
        unpack_small_kernel,
        [sds((di, 3 * width), F32), sds((2, width), F32)] + [sds((di,), F32)] * 2,
        (small.held, small.got[0]),
        vmem=24,
        in_specs=[vmem] * 2,
        out_specs=[vmem] * 4,
        scratch_shapes=[pltpu.VMEM((2, cut, width), BF16)],
    )
    return (
        outward(block_out, cotangent),
        outward(grad_tokens, tokens),
        s_norm_gain,
        s_norm_shift,
        s_qkv,
        s_qv_bias,
        s_proj,
        s_proj_bias,
        s_res,
        s_res_bias,
        s_mlp_gain,
        s_mlp_shift,
        s_fc1,
        s_fc1_bias,
        s_fc2,
        s_fc2_bias,
    )


def solution(mesh):
    clips, units = mesh.shape["clips"], mesh.shape["units"]
    fine = jax.sharding.Mesh(mesh.devices.reshape(clips // 2, 2, units // 2, 2), BOTH)
    split = P(BOTH[:2], BOTH[2:], None, None, None)
    return jax.shard_map(
        body,
        mesh=fine,
        in_specs=(split, split, P(BOTH[:2])) + (P(),) * 14,
        out_specs=(split, split) + (P(),) * 14,
        check_vma=False,
    )
```

```python
import functools

import jax
import jax.numpy as jnp
import numpy as np
from jax import lax
from jax.experimental import pallas as pl
from jax.experimental.pallas import tpu as pltpu
from jax.sharding import PartitionSpec as P

HEADS = 4
LANES = 128
EPS = 1e-06
LOG2E = 1.4426950408889634
ABSENT = -1e30
BOTH = ("clips_far", "next_x", "next_y", "core")
F32 = jnp.float32
BF16 = jnp.bfloat16
MIB = 2**20


def dot(left, right, dim_left=1, dim_right=0):
    return lax.dot_general(
        left, right, (((dim_left,), (dim_right,)), ((), ())), preferred_element_type=F32
    )


def norm_stats(value):
    centre = value - jnp.mean(value, axis=-1, keepdims=True)
    scale_inv = lax.rsqrt(jnp.mean(centre * centre, axis=-1, keepdims=True) + EPS)
    return centre * scale_inv, scale_inv


def norm_back(d_hat, hat, scale_inv):
    first = jnp.mean(d_hat, axis=-1, keepdims=True)
    second = jnp.mean(d_hat * hat, axis=-1, keepdims=True)
    return scale_inv * (d_hat - first - hat * second)


def three_parts(value):
    high = value.astype(BF16).astype(F32)
    rest = value - high
    middle = rest.astype(BF16).astype(F32)
    return high, middle, rest - middle


def with_columns(base, lane, column):
    high, middle, small = three_parts(-column)
    out = jnp.where(lane == 96, high, base)
    out = jnp.where(lane == 98, middle, out)
    return jnp.where(lane == 99, small, out)


def own_place():
    return lax.axis_index("next_y"), lax.axis_index("core")


def pack_rows(value):
    rows = value.shape[0]
    rest = jnp.concatenate([value[: rows // 2, LANES:], value[rows // 2 :, LANES:]], axis=1)
    return value[:, :LANES], rest


def unpack_half(ref, half):
    rows = ref.shape[0] * 2 // 3
    size = rows // 2
    side = (ref.shape[1] // 2) * half
    first = ref[half * size : (half + 1) * size, :].astype(F32)
    rest = ref[rows:, :].astype(F32)[:, side : side + ref.shape[1] // 2]
    return jnp.concatenate([first, rest], axis=1)


def pick_kernel(other, raw_ref, out_ref, tokens_ref, sem):
    clip, _ = own_place()
    copy = pltpu.make_async_copy(raw_ref.at[1 - clip if other else clip], tokens_ref, sem)
    copy.start()
    copy.wait()
    positions, _, di = tokens_ref.shape
    rows = 2 * positions
    first, rest = pack_rows(tokens_ref[...].reshape(rows, di).astype(F32))
    out_ref[:rows, :] = first.astype(BF16)
    out_ref[rows:, :] = rest.astype(BF16)


def weights_kernel(w_qkv_ref, qv_bias_ref, w_proj_ref, wq_ref, wkv_ref, heads_ref, proj_ref, bias_ref):
    di = w_qkv_ref.shape[0]
    width = w_proj_ref.shape[0]
    size = width // HEADS

    def by_head(value):
        pad = jnp.zeros((value.shape[0], LANES - size), value.dtype)
        pieces = []
        for h in range(HEADS):
            pieces += [value[:, h * size : (h + 1) * size], pad]
        return jnp.concatenate(pieces, axis=1)

    w = w_qkv_ref[...].astype(F32)
    query, key, value = (w[:, i * width : (i + 1) * width] for i in range(3))
    wq_ref[...] = by_head(query).astype(BF16)
    wkv_ref[:, : HEADS * LANES] = by_head(key).astype(BF16)
    wkv_ref[:, HEADS * LANES :] = by_head(value).astype(BF16)
    for h in range(HEADS):
        at = slice(h * size, (h + 1) * size)
        heads_ref[h] = jnp.concatenate([key[:, at], value[:, at]], axis=1).astype(BF16)
        proj_ref[h * LANES : h * LANES + size, :] = w_proj_ref[at, :]
        proj_ref[h * LANES + size : (h + 1) * LANES, :] = jnp.zeros((LANES - size, width), BF16)
    lane = lax.broadcasted_iota(jnp.int32, (8, HEADS * LANES), 1) % LANES
    ones = jnp.where((lane == 96) | (lane >= 98) & (lane < 100), 1.0, 0.0)
    biases = by_head(jnp.broadcast_to(qv_bias_ref[0:1, :], (8, width)))
    bias_ref[0:8, :] = biases
    bias_ref[8:16, :] = by_head(jnp.broadcast_to(qv_bias_ref[1:2, :], (8, width))) + ones
    bias_ref[16:24, :] = ones


def row_of(ref):
    return ref[...].reshape(1, ref.shape[-1])


def keys_of(tokens, base, first_mask, second_mask, refs, targets):
    gain_ref, shift_ref, wkv_ref, bias_ref = refs
    key_ref, value_ref, low_ref, hat_ref, peak_ref = targets
    rows, di = tokens.shape
    wide = HEADS * LANES
    hat, _ = norm_stats(tokens)
    low = (hat * row_of(gain_ref) + row_of(shift_ref)).astype(BF16)
    at = pl.ds(base, rows)
    low_ref[at, :di] = low
    hat_ref[at, :di] = hat.astype(BF16)
    key = dot(low, wkv_ref[:, :wide])
    squares = key[:, :LANES] * key[:, :LANES]
    for h in range(1, HEADS):
        squares = squares + key[:, h * LANES : (h + 1) * LANES] * key[:, h * LANES : (h + 1) * LANES]
    top = jnp.max(jnp.sum(squares, axis=-1, keepdims=True))
    peak_ref[...] = jnp.maximum(peak_ref[...], top)
    row = lax.broadcasted_iota(jnp.int32, (8, wide), 0) % 2
    lane = lax.broadcasted_iota(jnp.int32, (8, wide), 1) % LANES
    mask = jnp.where(row == 0, first_mask, second_mask)
    pattern = bias_ref[16:24, :] + jnp.where(lane == 97, mask, 0.0)
    key = (key.reshape(rows // 8, 8, wide) + pattern[None]).reshape(rows, wide).astype(BF16)
    for h in range(HEADS):
        key_ref[h, at, :] = key[:, h * LANES : (h + 1) * LANES]
    value = dot(low, wkv_ref[:, wide:])
    value = (value.reshape(rows // 8, 8, wide) + bias_ref[8:16, :][None]).reshape(rows, wide)
    value = value.astype(BF16)
    for h in range(HEADS):
        value_ref[h, at, :] = value[:, h * LANES : (h + 1) * LANES]


def fill_pads(base, rows, room, di, targets):
    key_ref, value_ref, low_ref, hat_ref, _ = targets
    empty = room - rows
    lane = lax.broadcasted_iota(jnp.int32, (empty, LANES), 1)
    at = slice(base + rows, base + room)
    for h in range(HEADS):
        key_ref[h, at, :] = jnp.where(lane == 97, ABSENT, 0.0).astype(BF16)
        value_ref[h, at, :] = jnp.zeros((empty, LANES), BF16)
    tail = lax.broadcasted_iota(jnp.int32, (room, LANES), 1)
    ones_tail = jnp.where(tail == di - LANES, 1.0, 0.0).astype(BF16)
    for ref in (low_ref, hat_ref):
        ref[base : base + room, LANES:] = ones_tail
        ref[at, :di] = jnp.zeros((empty, di), BF16)


def absent(frames_ref, holder, frame):
    clip, core = own_place()
    index = 2 * ((2 * clip + core) ^ holder) + frame
    return jnp.where(index < frames_ref[clip], 0.0, ABSENT).astype(F32)


def near_kernel(
    frames_ref,
    raw_ref,
    near_ref,
    gain_ref,
    shift_ref,
    wkv_ref,
    bias_ref,
    pool_ref,
    key_out,
    value_out,
    low_out,
    hat_out,
    pooled_ref,
    pooled_hat_ref,
    peak_ref,
    key_ref,
    value_ref,
    low_ref,
    hat_ref,
    mine_ref,
    sems,
):
    positions, _, di = mine_ref.shape
    rows = 2 * positions
    clip, _ = own_place()
    load = pltpu.make_async_copy(raw_ref.at[clip], mine_ref, sems.at[8])
    load.start()
    load.wait()
    room = key_ref.shape[1] // 2
    refs = (gain_ref, shift_ref, wkv_ref, bias_ref)
    targets = (key_ref, value_ref, low_ref, hat_ref, peak_ref)
    peak_ref[...] = jnp.zeros(peak_ref.shape, F32)
    pieces = 2
    step = positions // pieces
    copies = []
    for i in range(2):
        base = i * room
        fill_pads(base, rows, room, di, targets)

        for j in range(pieces):
            if i == 0:
                tokens = mine_ref[j * step : (j + 1) * step].reshape(2 * step, di).astype(F32)
            else:
                tokens = unpack_half(near_ref, j)
            keys_of(
                tokens,
                base + 2 * j * step,
                absent(frames_ref, i, 0),
                absent(frames_ref, i, 1),
                refs,
                targets,
            )

        at, to = pl.ds(base, room), pl.ds(2 * base, room)
        for k, (src, dst) in enumerate(((key_ref, key_out), (value_ref, value_out))):
            copies.append(
                pltpu.make_async_copy(src.at[:, at, :], dst.at[:, to, :], sems.at[4 * i + k])
            )
        for k, (src, dst) in enumerate(((low_ref, low_out), (hat_ref, hat_out))):
            copies.append(
                pltpu.make_async_copy(src.at[at, :], dst.at[to, :], sems.at[4 * i + k + 2])
            )
        for copy in copies[-4:]:
            copy.start()
    pooled_ref[...] = dot(pool_ref[...], low_ref[:rows, :di])
    pooled_hat_ref[...] = dot(pool_ref[...], hat_ref[:rows, :di])
    for copy in copies:
        copy.wait()


def forward_kernel(
    dims,
    frames_ref,
    got_ref,
    near_got_ref,
    gain_ref,
    shift_ref,
    wkv_ref,
    bias_ref,
    wq_ref,
    wres_ref,
    res_bias_ref,
    pool_ref,
    pooled_in,
    pooled_hat_in,
    peak_in,
    key_in,
    value_in,
    low_in,
    hat_in,
    probs_ref,
    att_ref,
    residual_ref,
    pooled_ref,
    pooled_hat_ref,
    key_out,
    value_out,
    query_out,
    low_out,
    hat_out,
    key_ref,
    value_ref,
    query_ref,
    low_ref,
    hat_ref,
    acc_ref,
    norm_ref,
    peak_ref,
    sems,
):
    di, rows, room, half, chunk, chunks, head_dim = dims
    positions = rows // 2
    head = pl.program_id(0)
    step = pl.program_id(1)
    factor = 1.0 / head_dim**0.5
    loads, stores = [], []
    for i in range(2):
        at, to = pl.ds(2 * i * room, room), pl.ds((2 * i + 1) * room, room)
        for k, (src, dst) in enumerate(((key_in, key_ref), (value_in, value_ref))):
            loads.append(
                pltpu.make_async_copy(src.at[:, at, :], dst.at[:, at, :], sems.at[2 * i + k])
            )
        for k, (src, dst) in enumerate(((key_ref, key_out), (value_ref, value_out))):
            stores.append(
                pltpu.make_async_copy(src.at[:, to, :], dst.at[:, to, :], sems.at[4 + 2 * i + k])
            )
        for k, (src, dst) in enumerate(((low_ref, low_out), (hat_ref, hat_out))):
            stores.append(
                pltpu.make_async_copy(
                    src.at[pl.ds(i * room, room), :], dst.at[to, :], sems.at[8 + 2 * i + k]
                )
            )
    stores.append(pltpu.make_async_copy(query_ref, query_out, sems.at[12]))

    @pl.when((head == 0) & (step == 0))
    def _():
        for copy in loads:
            copy.start()
        refs = (gain_ref, shift_ref, wkv_ref, bias_ref)
        norm_ref[...] = peak_in[...]
        pieces = 2
        size = positions // pieces
        for i, ref in enumerate((got_ref, near_got_ref)):
            keys = (
                key_ref.at[:, pl.ds((2 * i + 1) * room, room), :],
                value_ref.at[:, pl.ds((2 * i + 1) * room, room), :],
                low_ref.at[pl.ds(i * room, room), :],
                hat_ref.at[pl.ds(i * room, room), :],
                norm_ref,
            )
            fill_pads(0, rows, room, di, keys)

            for j in range(pieces):
                keys_of(
                    unpack_half(ref, j),
                    2 * j * size,
                    absent(frames_ref, 2 + i, 0),
                    absent(frames_ref, 2 + i, 1),
                    refs,
                    keys,
                )

        for copy in stores[:-1]:
            copy.start()
        tail = lax.broadcasted_iota(jnp.int32, (2 * half, LANES), 1)
        ones_tail = jnp.where(tail == di - LANES, 1.0, 0.0).astype(BF16)
        pooled_ref[:, LANES:] = ones_tail
        pooled_hat_ref[:, LANES:] = ones_tail
        pooled = jnp.concatenate([pooled_in[...], dot(pool_ref[...], low_ref[:rows, :di])], axis=0)
        high = pooled.astype(BF16)
        rest = (pooled - high.astype(F32)).astype(BF16)
        pooled_ref[:, :di] = high
        pooled_hat_ref[:, :di] = jnp.concatenate(
            [pooled_hat_in[...], dot(pool_ref[...], hat_ref[:rows, :di])], axis=0
        ).astype(BF16)
        residual_ref[...] = (
            dot(high, wres_ref[...]) + dot(rest, wres_ref[...]) + row_of(res_bias_ref)
        )
        query = dot(high, wq_ref[...]) + dot(rest, wq_ref[...]) + bias_ref[0:1, :]
        query = query.astype(BF16).astype(F32)
        lane = lax.broadcasted_iota(jnp.int32, (2 * half, LANES), 1)
        top = jnp.float32(0.0)
        for h in range(HEADS):
            part_h = query[:, h * LANES : (h + 1) * LANES]
            top = jnp.maximum(top, jnp.max(jnp.sum(part_h * part_h, axis=-1, keepdims=True)))
            query_ref[h] = jnp.where(lane == 97, 1.0, part_h).astype(BF16)
        for copy in loads:
            copy.wait()
        reach = jnp.sqrt(jnp.max(norm_ref[...]) * top) * (1.02 * factor)

        @pl.when(jnp.logical_not(reach < 60.0))
        def _():
            peak_ref[...] = jnp.full((2 * half, LANES), -3e38, F32)

            @pl.loop(0, HEADS)
            def _(h):
                @pl.loop(0, chunks)
                def _(j):
                    at = pl.ds(pl.multiple_of(j * chunk, LANES), chunk)
                    scores = dot(query_ref[h], key_ref[h, at, :], 1, 1)
                    highest = jnp.max(scores, axis=-1, keepdims=True)
                    peak_ref[...] = jnp.where(
                        lane == h, jnp.maximum(peak_ref[...], highest), peak_ref[...]
                    )

            for h in range(HEADS):
                query_ref[h] = with_columns(
                    query_ref[h].astype(F32), lane, peak_ref[:, h : h + 1]
                ).astype(BF16)

        stores[-1].start()

    at = pl.ds(pl.multiple_of(step * chunk, LANES), chunk)
    scores = dot(query_ref[head], key_ref[head, at, :], 1, 1)
    probs = jnp.exp2(scores * (factor * LOG2E)).astype(BF16)
    probs_ref[0] = probs
    gathered = dot(probs, value_ref[head, at, :])

    @pl.when(step == 0)
    def _():
        acc_ref[...] = gathered

    @pl.when(step > 0)
    def _():
        acc_ref[...] += gathered

    @pl.when(step == chunks - 1)
    def _():
        lane = lax.broadcasted_iota(jnp.int32, (2 * half, LANES), 1)
        acc = acc_ref[...]
        total_inv = 1.0 / acc[:, 96:97]
        att_ref[0] = jnp.where(
            lane < 96, acc * total_inv, jnp.where(lane == 96, total_inv, 0.0)
        )

    @pl.when((head == HEADS - 1) & (step == chunks - 1))
    def _():
        for copy in stores:
            copy.wait()


def halves_out(halves_ref, keep_ref, give_ref, sems):
    core = lax.axis_index("core")
    copies = [
        pltpu.make_async_copy(halves_ref.at[core], keep_ref, sems.at[0]),
        pltpu.make_async_copy(halves_ref.at[1 - core], give_ref, sems.at[1]),
    ]
    for copy in copies:
        copy.start()
    return copies


def middle_kernel(
    att_ref,
    residual_ref,
    cot_ref,
    cot_got_ref,
    wproj_ref,
    proj_bias_ref,
    gain_ref,
    shift_ref,
    wfc1_ref,
    fc1_bias_ref,
    wfc2_ref,
    fc2_bias_ref,
    out_ref,
    out_far_ref,
    keep_ref,
    give_ref,
    vec_ref,
    d_in_ref,
    mid_ref,
    cot_out_ref,
    halves_ref,
    sems,
):
    clip, _ = own_place()
    count = att_ref.shape[1]
    half = count // 2
    width = residual_ref.shape[1]
    hidden = wfc1_ref.shape[1]
    lane = lax.broadcasted_iota(jnp.int32, (count, LANES), 1)
    attended = jnp.concatenate(
        [jnp.where(lane < 96, att_ref[h], 0.0).astype(BF16) for h in range(HEADS)], axis=1
    )
    mid = dot(attended, wproj_ref[...]) + row_of(proj_bias_ref) + residual_ref[...]
    mid_ref[...] = mid
    hat, scale_inv = norm_stats(mid)
    mlp_in = (hat * row_of(gain_ref) + row_of(shift_ref)).astype(BF16)
    cot32 = jnp.concatenate(
        [
            cot_ref[clip].reshape(half, width).astype(F32),
            cot_got_ref[...].reshape(half, width).astype(F32),
        ],
        axis=0,
    )
    cot = cot32.astype(BF16)
    cot_out_ref[...] = cot
    d_in = jnp.zeros((count, width), F32)
    out = mid + row_of(fc2_bias_ref)
    piece = 512
    fc1_bias = row_of(fc1_bias_ref)
    copies, sums = [], []
    for i in range(hidden // piece):
        at = slice(i * piece, (i + 1) * piece)
        x = dot(mlp_in, wfc1_ref[:, at]) + fc1_bias[:, at]
        c0 = 0.7978845608028654
        square = x * x
        th = jnp.tanh(c0 * x * (1.0 + 0.044715 * square))
        half_up = 0.5 * (1.0 + th)
        act = (x * half_up).astype(BF16)
        slope = half_up + (0.5 * c0) * x * (1.0 - th * th) * (1.0 + (3 * 0.044715) * square)
        out = out + dot(act, wfc2_ref[at, :])
        halves_ref[0, at, :] = dot(act, cot, 0, 0).astype(BF16)
        d_pre = (dot(cot, wfc2_ref[at, :], 1, 1) * slope).astype(BF16)
        g_fc1 = dot(mlp_in, d_pre, 0, 0).astype(BF16)
        for col in range(0, piece, LANES):
            block, lane_at = divmod(i * piece + col, width)
            halves_ref[1, block * width : (block + 1) * width, lane_at : lane_at + LANES] = g_fc1[
                :, col : col + LANES
            ]
        sums.append(jnp.sum(d_pre.astype(F32), axis=0, keepdims=True))
        d_in = d_in + dot(d_pre, wfc1_ref[:, at], 1, 1)
    copies = halves_out(halves_ref, keep_ref, give_ref, sems)
    sums = jnp.concatenate(sums, axis=1)
    blocks = hidden // width
    vec_row = lax.broadcasted_iota(jnp.int32, (8, width), 0)
    vectors = jnp.where(vec_row == blocks, jnp.sum(cot32, axis=0, keepdims=True), 0.0)
    for i in range(blocks):
        vectors = jnp.where(vec_row == i, sums[:, i * width : (i + 1) * width], vectors)
    vec_ref[...] = vectors
    d_in_ref[...] = d_in
    out_ref[clip] = out[:half].astype(BF16).reshape(out_far_ref.shape)
    out_far_ref[...] = out[half:].astype(BF16).reshape(out_far_ref.shape)
    for copy in copies:
        copy.wait()


def turn_kernel(
    att_ref,
    mid_ref,
    d_in_ref,
    cot_ref,
    pooled_ref,
    wproj_ref,
    gain_ref,
    vec_ref,
    keep_ref,
    give_ref,
    d_mid_ref,
    d_att_ref,
    halves_ref,
    sems,
):
    count, width = mid_ref.shape
    size = width // HEADS
    lane = lax.broadcasted_iota(jnp.int32, (count, LANES), 1)
    hat, scale_inv = norm_stats(mid_ref[...])
    d_in = d_in_ref[...]
    d_mid = cot_ref[...].astype(F32) + norm_back(d_in * row_of(gain_ref), hat, scale_inv)
    d_mid = d_mid.astype(BF16)
    d_mid_ref[...] = d_mid
    d_att = dot(d_mid, wproj_ref[...], 1, 1).astype(BF16).astype(F32)
    for h in range(HEADS):
        att = att_ref[h]
        scaled = (d_att[:, h * LANES : (h + 1) * LANES] * att[:, 96:97]).astype(BF16).astype(F32)
        delta = jnp.sum(jnp.where(lane < 96, scaled * att, 0.0), axis=-1, keepdims=True)
        d_att_ref[h] = with_columns(scaled, lane, delta).astype(BF16)
        halves_ref[0, size * h : size * (h + 1), :] = dot(
            jnp.where(lane < 96, att, 0.0).astype(BF16), d_mid, 0, 0
        )[:size].astype(BF16)
    di = 2 * size
    halves_ref[1, :di, :] = dot(pooled_ref[...], d_mid, 0, 0)[:di].astype(BF16)
    row = lax.broadcasted_iota(jnp.int32, (8, width), 0)
    extra = jnp.where(row == 0, jnp.sum(d_in * hat, axis=0, keepdims=True), 0.0)
    extra = jnp.where(row == 1, jnp.sum(d_in, axis=0, keepdims=True), extra)
    extra = jnp.where(row == 2, jnp.sum(d_mid.astype(F32), axis=0, keepdims=True), extra)
    halves_ref[1, di : di + 16, :] = jnp.concatenate([vec_ref[...], extra], axis=0).astype(BF16)
    halves_ref[1, di + 16 :, :] = jnp.zeros((width - di - 16, width), BF16)
    for copy in halves_out(halves_ref, keep_ref, give_ref, sems):
        copy.wait()


def backward_kernel(
    first,
    last,
    heads,
    chunks,
    factor,
    probs_ref,
    key_ref,
    value_ref,
    query_ref,
    d_att_ref,
    low_ref,
    wkv_ref,
    pooled_ref,
    *rest,
):
    rest = list(rest)
    prev_ref = None if first else rest.pop(0)
    hat_ref = rest.pop(0) if last else None
    out_ref, pack_ref, dq_ref = rest[:3]
    norm_ref = rest[3] if last else None
    dn_ref, gw_ref, acc_ref = rest[-3:]
    head, step = pl.program_id(0), pl.program_id(1)
    chunk = probs_ref.shape[2]
    at = pl.ds(pl.multiple_of(step * chunk, LANES), chunk)
    probs = probs_ref[0]
    d_prob = dot(d_att_ref[0], value_ref[0], 1, 1)
    d_value = dot(d_att_ref[0], probs, 0, 0)[:96]
    d_scores = (probs.astype(F32) * d_prob).astype(BF16)
    d_key = dot(query_ref[0], d_scores, 0, 0)[:96] * factor
    d_query = dot(d_scores, key_ref[0])
    both = jnp.concatenate([d_key, d_value], axis=0).astype(BF16)
    back = dot(wkv_ref[0], both)
    g_w = dot(both, low_ref[...])

    @pl.when(head == 0)
    def _():
        dn_ref[:, at] = back if first else prev_ref[...] + back

    if heads > 1:

        @pl.when(head > 0)
        def _():
            dn_ref[:, at] += back

    @pl.when(head == heads - 1)
    def _():
        dn = dn_ref[:, at].astype(out_ref.dtype)
        out_ref[...] = dn
        if last:
            sums = dot(dn, hat_ref[...])
            norm_ref[...] = jnp.where(step == 0, sums, norm_ref[...] + sums)

    @pl.when(step == 0)
    def _():
        gw_ref[...] = g_w
        acc_ref[...] = d_query

    @pl.when(step > 0)
    def _():
        gw_ref[...] += g_w
        acc_ref[...] += d_query

    @pl.when(step == chunks - 1)
    def _():
        lane = lax.broadcasted_iota(jnp.int32, acc_ref.shape, 1)
        dq = jnp.where(lane < 96, acc_ref[...] * factor, 0.0).astype(BF16)
        dq_ref[0] = dq
        g_q = dot(pooled_ref[...], dq, 0, 0)
        size = gw_ref.shape[0]
        rows = pack_ref.shape[1]
        pack_ref[0, :size, :256] = gw_ref[...]
        pack_ref[0, :, 256:] = g_q[:rows]
        pack_ref[0, size:, :256] = jnp.zeros((rows - size, 256), F32)


def gather_kernel(
    norm_ref,
    dq0_ref,
    dq1_ref,
    dq2_ref,
    pack0_ref,
    pack1_ref,
    pack2_ref,
    d_mid_ref,
    wq_ref,
    wres_ref,
    pooled_hat_ref,
    d_pool_ref,
    keep_ref,
    give_ref,
    halves_ref,
    sems,
):
    di = wq_ref.shape[0]
    d_pool = dot(d_mid_ref[...], wres_ref[...], 1, 1)
    for h, dq in enumerate((dq0_ref[0], dq1_ref[0], dq1_ref[1], dq2_ref[0])):
        d_pool = d_pool + dot(dq, wq_ref[:, h * LANES : (h + 1) * LANES], 1, 1)
    low = d_pool.astype(BF16)
    d_pool_ref[...] = low
    both = norm_ref[...] + dot(low, pooled_hat_ref[...], 0, 0)
    row = lax.broadcasted_iota(jnp.int32, both.shape, 0)
    col = lax.broadcasted_iota(jnp.int32, both.shape, 1)
    gain = jnp.sum(jnp.where(row == col, both, 0.0), axis=1, keepdims=True)
    lane = lax.broadcasted_iota(jnp.int32, (di, LANES), 1)
    norms = jnp.where(lane == 65, gain, jnp.where(lane == 66, both[:, di : di + 1], 0.0))
    pieces = []
    for pack in (pack0_ref[0], pack1_ref[0], pack1_ref[1]):
        pieces.append(pack.astype(BF16))
    last = pack2_ref[0]
    middle = last[:, LANES : 2 * LANES] + jnp.concatenate(
        [norms, jnp.zeros((last.shape[0] - di, LANES), F32)], axis=0
    )
    pieces.append(
        jnp.concatenate([last[:, :LANES], middle, last[:, 2 * LANES :]], axis=1).astype(BF16)
    )
    cut, width = keep_ref.shape
    pieces.append(jnp.zeros((2 * cut - sum(p.shape[0] for p in pieces), width), BF16))
    at = 0
    for piece in pieces:
        size = piece.shape[0]
        done = 0
        while done < size:
            side, row = divmod(at + done, cut)
            take = min(size - done, cut - row)
            halves_ref[side, row : row + take, :] = piece[done : done + take]
            done += take
        at += size
    for copy in halves_out(halves_ref, keep_ref, give_ref, sems):
        copy.wait()


def end_kernel(
    dn_ref,
    got_ref,
    d_pool_ref,
    spread_ref,
    raw_ref,
    far_ref,
    gain_ref,
    out_ref,
    out_far_ref,
    held_ref,
    sem,
):
    clip, _ = own_place()
    load = pltpu.make_async_copy(raw_ref.at[clip], held_ref, sem)
    load.start()
    positions, _, di = held_ref.shape
    rows = 2 * positions
    half = spread_ref.shape[1]
    room = dn_ref.shape[1] // 2
    for own in (1, 0):
        start = own * room
        lead = start % LANES
        at = slice(start - lead, start - lead + -(-(lead + rows) // LANES) * LANES)
        turned = (dn_ref[:, at].astype(F32) + got_ref[:, at].astype(F32)).T[lead : lead + rows]
        spread = dot(spread_ref[...], d_pool_ref[own * half : (own + 1) * half, :])
        if own == 0:
            load.wait()
            tokens = held_ref[...].reshape(rows, di).astype(F32)
        else:
            tokens = jnp.concatenate([unpack_half(far_ref, 0), unpack_half(far_ref, 1)], axis=0)
        hat, scale_inv = norm_stats(tokens)
        grad = norm_back((turned + spread) * row_of(gain_ref), hat, scale_inv)
        if own == 0:
            out_ref[clip] = grad.astype(BF16).reshape(positions, 2, di)
        else:
            first, rest = pack_rows(grad)
            out_far_ref[:rows, :] = first.astype(BF16)
            out_far_ref[rows:, :] = rest.astype(BF16)


def finish_kernel(tokens_in, out_in, got_ref, out_got_ref, tokens_ref, out_ref, held_ref, sems):
    clip, _ = own_place()
    positions, _, di = held_ref.shape
    copies = [
        pltpu.make_async_copy(out_got_ref, out_ref.at[1 - clip], sems.at[0]),
        pltpu.make_async_copy(held_ref, tokens_ref.at[1 - clip], sems.at[1]),
    ]
    copies[0].start()
    for j in range(2):
        at = slice(j * positions // 2, (j + 1) * positions // 2)
        held_ref[at] = unpack_half(got_ref, j).astype(BF16).reshape(positions // 2, 2, di)
    copies[1].start()
    for copy in copies:
        copy.wait()


def unpack_big_kernel(
    own_ref,
    other_ref,
    fc2_ref,
    fc1_ref,
    proj_ref,
    res_ref,
    fc1_bias_ref,
    fc2_bias_ref,
    mlp_gain_ref,
    mlp_shift_ref,
    proj_bias_ref,
    res_bias_ref,
):
    _, core = own_place()
    width = own_ref.shape[1]
    hidden = fc2_ref.shape[0]
    di = res_ref.shape[0]

    def write(first, second):
        fc2_ref[...] = first[:hidden, :].astype(F32)
        for i in range(hidden // width):
            at = slice(i * width, (i + 1) * width)
            fc1_ref[:, at] = second[at, :].astype(F32)
        proj_ref[...] = first[hidden : hidden + width, :].astype(F32)
        res_ref[...] = second[hidden : hidden + di, :].astype(F32)
        vectors = second[hidden + di : hidden + di + 16, :].astype(F32)
        blocks = hidden // width
        fc1_bias_ref[...] = jnp.concatenate([vectors[i : i + 1] for i in range(blocks)], axis=1)[0]
        fc2_bias_ref[...] = vectors[blocks]
        mlp_gain_ref[...] = vectors[8]
        mlp_shift_ref[...] = vectors[9]
        proj_bias_ref[...] = vectors[10]
        res_bias_ref[...] = vectors[10]

    @pl.when(core == 0)
    def _():
        write(own_ref, other_ref)

    @pl.when(core == 1)
    def _():
        write(other_ref, own_ref)


def unpack_small_kernel(
    own_ref,
    other_ref,
    qkv_ref,
    qv_bias_ref,
    norm_gain_ref,
    norm_shift_ref,
    whole_ref,
):
    _, core = own_place()
    cut, width = own_ref.shape
    size = width // HEADS
    di = 2 * size
    whole_ref[core] = own_ref[...]
    whole_ref[1 - core] = other_ref[...]

    def rows(start, count):
        pieces = []
        while count:
            side, row = divmod(start, cut)
            take = min(count, cut - row)
            pieces.append(whole_ref[side, row : row + take, :])
            start, count = start + take, count - take
        return (pieces[0] if len(pieces) == 1 else jnp.concatenate(pieces, axis=0)).astype(F32)

    start = 0
    queries, keys, values, q_bias, v_bias = [], [], [], [], []
    for h in range(HEADS):
        pack = rows(start + 208 * h, 208)
        queries.append(pack[:di, 256 : 256 + size])
        turned = pack[:di, :256].T
        keys.append(turned[:di, :size])
        values.append(turned[:di, size:])
        q_bias.append(pack[di : di + 1, 256 : 256 + size])
        v_bias.append(turned[di : di + 1, size:])
    qkv_ref[...] = jnp.concatenate(queries + keys + values, axis=1)
    qv_bias_ref[0:1, :] = jnp.concatenate(q_bias, axis=1)
    qv_bias_ref[1:2, :] = jnp.concatenate(v_bias, axis=1)
    norm_gain_ref[...] = turned[di + 1]
    norm_shift_ref[...] = turned[di + 2]


def sizes():
    return [lax.axis_size(name) for name in BOTH]


def exchange(value, mask):
    count = int(np.prod(sizes()))
    return lax.ppermute(value, BOTH, [(i, i ^ mask) for i in range(count)])


def stages():
    count = int(np.prod(sizes()))
    out = [(1, [1]), (2, [2, 4, 6])]
    bit = 8
    while bit < count:
        if bit * 2 < count:
            out.append((bit, [bit, 2 * bit, 3 * bit]))
            bit *= 4
        else:
            out.append((bit, [bit]))
            bit *= 2
    return out


def place(stage):
    return (lax.axis_index(BOTH) // stage[0]) % (len(stage[1]) + 1)


def sum_pieces(pieces):
    pieces = [p.astype(F32) for p in pieces]
    while len(pieces) > 1:
        pieces = [a + b for a, b in zip(pieces[::2], pieces[1::2])]
    return pieces[0]


class Sum:
    def __init__(self, keep, give, depth):
        self.plan = stages()
        self.depth = min(depth, len(self.plan) - 1)
        self.places = [place(stage) for stage in self.plan]
        self.held, self.pieces = keep, [give]
        self.at, self.back, self.done, self.summed = 0, False, False, False
        self.more = None

    def cut(self):
        masks = self.plan[self.at][1]
        if self.back or self.at > self.depth:
            self.pieces = [self.held] * len(masks)
            return
        size, where = len(masks) + 1, self.places[self.at]
        later = int(np.prod([len(self.plan[i][1]) + 1 for i in range(self.at + 1, self.depth + 1)]))
        rows, columns = self.held.shape
        whole = self.held.reshape(later, size, rows // (later * size), columns)

        def take(index):
            piece = lax.dynamic_index_in_dim(whole, index, 1, keepdims=False)
            return piece.reshape(rows // size, columns)

        self.held = take(where)
        self.pieces = [take(where ^ (k + 1)) for k in range(size - 1)]

    def send(self, other):
        (self.held, self.pieces), other = lax.optimization_barrier(((self.held, self.pieces), other))
        self.got = [exchange(p, mask) for p, mask in zip(self.pieces, self.plan[self.at][1])]
        self.done = self.back and self.at == 0
        return other

    def merge(self, other):
        (self.held, self.got), other = lax.optimization_barrier(((self.held, self.got), other))
        if not self.back:
            self.held = sum_pieces([self.held] + self.got).astype(BF16)
            if self.at == 0 and self.more is not None:
                self.held = jnp.concatenate([self.held, self.more])
            if self.at + 1 < len(self.plan):
                self.at += 1
            else:
                self.back, self.summed, self.at = True, True, self.depth
        else:
            size, where = len(self.got) + 1, self.places[self.at]
            stacked = jnp.stack([self.held] + self.got)
            self.held = jnp.concatenate(
                [
                    lax.dynamic_index_in_dim(stacked, where ^ k, 0, keepdims=False)
                    for k in range(size)
                ]
            )
            self.at -= 1
        self.cut()
        return other

    def advance(self, other):
        return other if self.done else self.send(self.merge(other))


def call(kernel, out_shape, args, flops=0, vmem=60, **kwargs):
    moved = sum(np.prod(a.shape) * a.dtype.itemsize for a in args) if flops else 1
    return pl.pallas_call(
        kernel,
        out_shape=out_shape,
        compiler_params=pltpu.CompilerParams(vmem_limit_bytes=vmem * MIB),
        cost_estimate=pl.CostEstimate(
            flops=int(max(flops, 1)), bytes_accessed=int(moved), transcendentals=0
        ),
        **kwargs,
    )(*args)


def body(
    tokens,
    cotangent,
    frames,
    norm_gain,
    norm_shift,
    w_qkv,
    qv_bias,
    w_proj,
    proj_bias,
    w_res,
    res_bias,
    mlp_gain,
    mlp_shift,
    w_fc1,
    fc1_bias,
    w_fc2,
    fc2_bias,
):
    clip_count, frame_local, grid_rows, grid_cols, di = tokens.shape
    width = w_proj.shape[0]
    head_dim = width // HEADS
    hidden = w_fc1.shape[1]
    frame = grid_rows * grid_cols
    rows = frame_local * frame
    half = rows // 4
    room = 1600
    chunk = 1280
    chunks = 4 * room // chunk
    wide = HEADS * LANES
    factor = 1.0 / head_dim**0.5
    vmem = pl.BlockSpec(memory_space=pltpu.VMEM)
    smem = pl.BlockSpec(memory_space=pltpu.SMEM)
    hbm = pl.BlockSpec(memory_space=pl.ANY)
    sds = jax.ShapeDtypeStruct

    raw = tokens.transpose(0, 2, 3, 1, 4).reshape(clip_count, frame, frame_local, di)
    cot_raw = cotangent.transpose(0, 2, 3, 1, 4).reshape(
        clip_count, frame // 4, frame_local, width
    )

    def pick(other):
        return call(
            functools.partial(pick_kernel, other),
            [sds((3 * rows // 2, LANES), BF16)],
            (raw,),
            vmem=16,
            in_specs=[hbm],
            out_specs=[vmem],
            scratch_shapes=[pltpu.VMEM(raw.shape[1:], BF16), pltpu.SemaphoreType.DMA],
        )[0]

    got = exchange(pick(True), 2)
    near = exchange(pick(False), 1)
    clip_at = lax.axis_index("next_y")
    cot_far = lax.dynamic_index_in_dim(cot_raw, 1 - clip_at, 0, keepdims=False)
    near, cot_far = lax.optimization_barrier((near, cot_far))
    cot_got = exchange(cot_far, 2)

    pool_np = np.zeros((half, rows), np.float32)
    token = np.arange(rows)
    position, f = token // frame_local, token % frame_local
    r, c = position // grid_cols, position % grid_cols
    pool_np[((r // 2) * (grid_cols // 2) + c // 2) * frame_local + f, token] = 0.25
    pool = jnp.asarray(pool_np, BF16)
    spread = jnp.asarray(pool_np.T, BF16)

    wq, wkv, w_kv_heads, w_proj_pad, bias = call(
        weights_kernel,
        [
            sds((di, wide), BF16),
            sds((di, 2 * wide), BF16),
            sds((HEADS, di, 2 * head_dim), BF16),
            sds((wide, width), BF16),
            sds((24, wide), F32),
        ],
        (w_qkv, qv_bias, w_proj),
        in_specs=[vmem] * 3,
        out_specs=[vmem] * 5,
    )
    whole = [
        sds((HEADS, 4 * room, LANES), BF16),
        sds((HEADS, 4 * room, LANES), BF16),
        sds((4 * room, 256), BF16),
        sds((4 * room, 256), BF16),
    ]
    key, value, low, hat, pooled_mine, pooled_hat_mine, peak = call(
        near_kernel,
        whole
        + [sds((half, di), F32), sds((half, di), F32), sds((8, LANES), F32)],
        (frames, raw, near, norm_gain, norm_shift, wkv, bias, pool),
        flops=3e9,
        in_specs=[smem, hbm] + [vmem] * 6,
        out_specs=[hbm] * 4 + [vmem] * 3,
        scratch_shapes=[
            pltpu.VMEM((HEADS, 2 * room, LANES), BF16),
            pltpu.VMEM((HEADS, 2 * room, LANES), BF16),
            pltpu.VMEM((2 * room, 256), BF16),
            pltpu.VMEM((2 * room, 256), BF16),
            pltpu.VMEM(raw.shape[1:], BF16),
            pltpu.SemaphoreType.DMA((9,)),
        ],
    )
    got, peak = lax.optimization_barrier((got, peak))
    near_got = exchange(got, 1)
    dims = (di, rows, room, half, chunk, chunks, head_dim)
    probs, att, residual, pooled, pooled_hat, key, value, query, low, hat = call(
        functools.partial(forward_kernel, dims),
        [
            sds((HEADS, 2 * half, 4 * room), BF16),
            sds((HEADS, 2 * half, LANES), F32),
            sds((2 * half, width), F32),
            sds((2 * half, 256), BF16),
            sds((2 * half, 256), BF16),
        ]
        + whole[:2]
        + [sds((HEADS, 2 * half, LANES), BF16)]
        + whole[2:],
        (
            frames,
            got,
            near_got,
            norm_gain,
            norm_shift,
            wkv,
            bias,
            wq,
            w_res,
            res_bias,
            pool,
            pooled_mine,
            pooled_hat_mine,
            peak,
            key,
            value,
            low,
            hat,
        ),
        flops=25e9,
        grid=(HEADS, chunks),
        in_specs=[smem] + [vmem] * 13 + [hbm] * 4,
        out_specs=[
            pl.BlockSpec((1, 2 * half, chunk), lambda h, j: (h, 0, j)),
            pl.BlockSpec((1, 2 * half, LANES), lambda h, j: (h, 0, 0)),
            vmem,
            vmem,
            vmem,
        ]
        + [hbm] * 5,
        input_output_aliases={14: 5, 15: 6, 16: 8, 17: 9},
        scratch_shapes=[
            pltpu.VMEM((HEADS, 4 * room, LANES), BF16),
            pltpu.VMEM((HEADS, 4 * room, LANES), BF16),
            pltpu.VMEM((HEADS, 2 * half, LANES), BF16),
            pltpu.VMEM((2 * room, 256), BF16),
            pltpu.VMEM((2 * room, 256), BF16),
            pltpu.VMEM((2 * half, LANES), F32),
            pltpu.VMEM((8, LANES), F32),
            pltpu.VMEM((2 * half, LANES), F32),
            pltpu.SemaphoreType.DMA((13,)),
        ],
    )

    out_raw = sds(cot_raw.shape, BF16)
    out_far = sds(cot_raw.shape[1:], BF16)
    out, out_far, fc_keep, fc_give, vectors, d_in, mid, cot = call(
        middle_kernel,
        [
            out_raw,
            out_far,
            sds((hidden, width), BF16),
            sds((hidden, width), BF16),
            sds((8, width), F32),
            sds((2 * half, width), F32),
            sds((2 * half, width), F32),
            sds((2 * half, width), BF16),
        ],
        (
            att,
            residual,
            cot_raw,
            cot_got,
            w_proj_pad,
            proj_bias,
            mlp_gain,
            mlp_shift,
            w_fc1,
            fc1_bias,
            w_fc2,
            fc2_bias,
        ),
        flops=8e9,
        in_specs=[vmem] * 12,
        out_specs=[vmem, vmem, hbm, hbm] + [vmem] * 4,
        scratch_shapes=[pltpu.VMEM((2, hidden, width), BF16), pltpu.SemaphoreType.DMA((2,))],
    )
    big = Sum(fc_keep, fc_give, 1)
    d_in = big.send(d_in)
    mlp_keep, mlp_give, d_mid, d_att = call(
        turn_kernel,
        [
            sds((width, width), BF16),
            sds((width, width), BF16),
            sds((2 * half, width), BF16),
            sds((HEADS, 2 * half, LANES), BF16),
        ],
        (att, mid, d_in, cot, pooled, w_proj_pad, mlp_gain, vectors),
        flops=2e9,
        in_specs=[vmem] * 8,
        out_specs=[hbm, hbm, vmem, vmem],
        scratch_shapes=[pltpu.VMEM((2, width, width), BF16), pltpu.SemaphoreType.DMA((2,))],
    )
    mlp_got = exchange(mlp_give, 1)
    big.more = sum_pieces([mlp_keep, mlp_got]).astype(BF16)
    d_att = big.merge(d_att)
    d_att = big.send(d_att)

    packs, dqs = [], []
    dn = None
    groups = ((0,), (1, 2), (3,))
    for group in groups:
        first, last = group[0] == 0, group[-1] == HEADS - 1
        n, h = len(group), group[0]
        args = [probs, key, value, query, d_att, low, w_kv_heads, pooled]
        specs = [
            pl.BlockSpec((1, 2 * half, chunk), lambda i, j, h=h: (h + i, 0, j)),
            pl.BlockSpec((1, chunk, LANES), lambda i, j, h=h: (h + i, j, 0)),
            pl.BlockSpec((1, chunk, LANES), lambda i, j, h=h: (h + i, j, 0)),
            pl.BlockSpec((1, 2 * half, LANES), lambda i, j, h=h: (h + i, 0, 0)),
            pl.BlockSpec((1, 2 * half, LANES), lambda i, j, h=h: (h + i, 0, 0)),
            pl.BlockSpec((chunk, 256), lambda i, j: (j, 0)),
            pl.BlockSpec((1, di, 2 * head_dim), lambda i, j, h=h: (h + i, 0, 0)),
            vmem,
        ]
        if not first:
            args.append(dn)
            specs.append(pl.BlockSpec((di, chunk), lambda i, j: (0, jnp.where(i == 0, j, chunks - 1))))
        if last:
            args.append(hat)
            specs.append(
                pl.BlockSpec((chunk, 256), lambda i, j, n=n: (jnp.where(i == n - 1, j, 0), 0))
            )
        results = call(
            functools.partial(backward_kernel, first, last, n, chunks, factor),
            [
                sds((di, 4 * room), BF16 if last else F32),
                sds((n, 208, 384), F32),
                sds((n, 2 * half, LANES), BF16),
            ]
            + [sds((di, 256), F32)] * last,
            args,
            flops=9e9 * n,
            grid=(n, chunks),
            in_specs=specs,
            out_specs=[
                pl.BlockSpec((di, chunk), lambda i, j, n=n: (0, jnp.where(i == n - 1, j, 0))),
                pl.BlockSpec((1, 208, 384), lambda i, j: (i, 0, 0)),
                pl.BlockSpec((1, 2 * half, LANES), lambda i, j: (i, 0, 0)),
            ]
            + [vmem] * last,
            scratch_shapes=[
                pltpu.VMEM((di, 4 * room), F32),
                pltpu.VMEM((2 * head_dim, 256), F32),
                pltpu.VMEM((2 * half, LANES), F32),
            ],
        )
        dn, pack, dq = results[:3]
        packs.append(pack)
        dqs.append(dq)
        dn = big.merge(dn)
        if first:
            big.held, dn, out_far = lax.optimization_barrier((big.held, dn, out_far))
            out_got = exchange(out_far, 2)
        elif not last:
            dn, out_got = lax.optimization_barrier((dn, out_got))
        if not last:
            dn = big.send(dn)
    while not big.summed:
        dn = big.merge(big.send(dn))
    norm_sums = results[3]

    cut = 448
    sib_got = exchange(dn, 1)
    d_pool, keep, give = call(
        gather_kernel,
        [sds((2 * half, di), BF16), sds((cut, width), BF16), sds((cut, width), BF16)],
        (norm_sums, *dqs, *packs, d_mid, wq, w_res, pooled_hat),
        flops=4e9,
        in_specs=[vmem] * 11,
        out_specs=[vmem, hbm, hbm],
        scratch_shapes=[pltpu.VMEM((2, cut, width), BF16), pltpu.SemaphoreType.DMA((2,))],
    )
    small = Sum(keep, give, 1)
    sib_got = small.send(sib_got)
    sib_got = small.advance(sib_got)
    (big.held, big.pieces), small.pieces = lax.optimization_barrier(
        ((big.held, big.pieces), small.pieces)
    )
    sib_got = big.send(sib_got)
    grad_tokens, grad_far = call(
        end_kernel,
        [sds(raw.shape, BF16), sds(got.shape, BF16)],
        (dn, sib_got, d_pool, spread, raw, got, norm_gain),
        flops=9e9,
        grid=(1,),
        in_specs=[
            pl.BlockSpec((di, 2 * room), lambda i: (0, 0)),
            pl.BlockSpec((di, 2 * room), lambda i: (0, 1)),
            vmem,
            vmem,
            hbm,
            vmem,
            vmem,
        ],
        out_specs=[vmem, vmem],
        scratch_shapes=[pltpu.VMEM(raw.shape[1:], BF16), pltpu.SemaphoreType.DMA],
    )
    grad_far = small.advance(grad_far)
    grad_got = exchange(grad_far, 2)
    while not big.done:
        grad_tokens = big.advance(grad_tokens)
    big_own, big_other = big.held, big.got[0]
    vector = sds((width,), F32)
    (
        s_fc2,
        s_fc1,
        s_proj,
        s_res,
        s_fc1_bias,
        s_fc2_bias,
        s_mlp_gain,
        s_mlp_shift,
        s_proj_bias,
        s_res_bias,
    ) = call(
        unpack_big_kernel,
        [
            sds((hidden, width), F32),
            sds((width, hidden), F32),
            sds((width, width), F32),
            sds((di, width), F32),
            sds((hidden,), F32),
        ]
        + [vector] * 5,
        (big_own, big_other),
        vmem=24,
        in_specs=[vmem] * 2,
        out_specs=[vmem] * 10,
    )
    unpacked = (
        s_fc2,
        s_fc1,
        s_proj,
        s_res,
        s_fc1_bias,
        s_fc2_bias,
        s_mlp_gain,
        s_mlp_shift,
        s_proj_bias,
        s_res_bias,
    )
    while not small.summed:
        unpacked = small.advance(unpacked)
    grad_got, small.got = lax.optimization_barrier((grad_got, small.got))
    unpacked = small.advance(unpacked)
    (
        s_fc2,
        s_fc1,
        s_proj,
        s_res,
        s_fc1_bias,
        s_fc2_bias,
        s_mlp_gain,
        s_mlp_shift,
        s_proj_bias,
        s_res_bias,
    ) = unpacked
    grad_tokens, block_out = call(
        finish_kernel,
        [sds(raw.shape, BF16), sds(cot_raw.shape, BF16)],
        (grad_tokens, out, grad_got, out_got),
        vmem=16,
        in_specs=[hbm, hbm, vmem, hbm],
        out_specs=[hbm, hbm],
        input_output_aliases={0: 0, 1: 1},
        scratch_shapes=[pltpu.VMEM(raw.shape[1:], BF16), pltpu.SemaphoreType.DMA((2,))],
    )

    def outward(value, like):
        shape = (clip_count, like.shape[2], like.shape[3], frame_local, like.shape[4])
        return value.reshape(shape).transpose(0, 3, 1, 2, 4)

    s_qkv, s_qv_bias, s_norm_gain, s_norm_shift = call(
        unpack_small_kernel,
        [sds((di, 3 * width), F32), sds((2, width), F32)] + [sds((di,), F32)] * 2,
        (small.held, small.got[0]),
        vmem=24,
        in_specs=[vmem] * 2,
        out_specs=[vmem] * 4,
        scratch_shapes=[pltpu.VMEM((2, cut, width), BF16)],
    )
    return (
        outward(block_out, cotangent),
        outward(grad_tokens, tokens),
        s_norm_gain,
        s_norm_shift,
        s_qkv,
        s_qv_bias,
        s_proj,
        s_proj_bias,
        s_res,
        s_res_bias,
        s_mlp_gain,
        s_mlp_shift,
        s_fc1,
        s_fc1_bias,
        s_fc2,
        s_fc2_bias,
    )


def solution(mesh):
    clips, units = mesh.shape["clips"], mesh.shape["units"]
    fine = jax.sharding.Mesh(mesh.devices.reshape(clips // 2, 2, units // 2, 2), BOTH)
    split = P(BOTH[:2], BOTH[2:], None, None, None)
    return jax.shard_map(
        body,
        mesh=fine,
        in_specs=(split, split, P(BOTH[:2])) + (P(),) * 14,
        out_specs=(split, split) + (P(),) * 14,
        check_vma=False,
    )
```

```python
import functools

import jax
import jax.numpy as jnp
import numpy as np
from jax import lax
from jax.experimental import pallas as pl
from jax.experimental.pallas import tpu as pltpu
from jax.sharding import PartitionSpec as P

HEADS = 4
LANES = 128
EPS = 1e-06
LOG2E = 1.4426950408889634
ABSENT = -1e30
BOTH = ("clips_far", "next_x", "next_y", "core")
F32 = jnp.float32
BF16 = jnp.bfloat16
MIB = 2**20


def dot(left, right, dim_left=1, dim_right=0):
    return lax.dot_general(
        left, right, (((dim_left,), (dim_right,)), ((), ())), preferred_element_type=F32
    )


def norm_stats(value):
    centre = value - jnp.mean(value, axis=-1, keepdims=True)
    scale_inv = lax.rsqrt(jnp.mean(centre * centre, axis=-1, keepdims=True) + EPS)
    return centre * scale_inv, scale_inv


def norm_back(d_hat, hat, scale_inv):
    first = jnp.mean(d_hat, axis=-1, keepdims=True)
    second = jnp.mean(d_hat * hat, axis=-1, keepdims=True)
    return scale_inv * (d_hat - first - hat * second)


def three_parts(value):
    high = value.astype(BF16).astype(F32)
    rest = value - high
    middle = rest.astype(BF16).astype(F32)
    return high, middle, rest - middle


def with_columns(base, lane, column):
    high, middle, small = three_parts(-column)
    out = jnp.where(lane == 96, high, base)
    out = jnp.where(lane == 98, middle, out)
    return jnp.where(lane == 99, small, out)


def own_place():
    return lax.axis_index("next_y"), lax.axis_index("core")


def pack_rows(value):
    rows = value.shape[0]
    rest = jnp.concatenate([value[: rows // 2, LANES:], value[rows // 2 :, LANES:]], axis=1)
    return value[:, :LANES], rest


def unpack_half(ref, half):
    rows = ref.shape[0] * 2 // 3
    size = rows // 2
    side = (ref.shape[1] // 2) * half
    first = ref[half * size : (half + 1) * size, :].astype(F32)
    rest = ref[rows:, :].astype(F32)[:, side : side + ref.shape[1] // 2]
    return jnp.concatenate([first, rest], axis=1)


def pick_kernel(other, raw_ref, out_ref, tokens_ref, sem):
    clip, _ = own_place()
    copy = pltpu.make_async_copy(raw_ref.at[1 - clip if other else clip], tokens_ref, sem)
    copy.start()
    copy.wait()
    positions, _, di = tokens_ref.shape
    rows = 2 * positions
    first, rest = pack_rows(tokens_ref[...].reshape(rows, di).astype(F32))
    out_ref[:rows, :] = first.astype(BF16)
    out_ref[rows:, :] = rest.astype(BF16)


def weights_kernel(w_qkv_ref, qv_bias_ref, w_proj_ref, wq_ref, wkv_ref, heads_ref, proj_ref, bias_ref):
    di = w_qkv_ref.shape[0]
    width = w_proj_ref.shape[0]
    size = width // HEADS

    def by_head(value):
        pad = jnp.zeros((value.shape[0], LANES - size), value.dtype)
        pieces = []
        for h in range(HEADS):
            pieces += [value[:, h * size : (h + 1) * size], pad]
        return jnp.concatenate(pieces, axis=1)

    w = w_qkv_ref[...].astype(F32)
    query, key, value = (w[:, i * width : (i + 1) * width] for i in range(3))
    wq_ref[...] = by_head(query).astype(BF16)
    wkv_ref[:, : HEADS * LANES] = by_head(key).astype(BF16)
    wkv_ref[:, HEADS * LANES :] = by_head(value).astype(BF16)
    for h in range(HEADS):
        at = slice(h * size, (h + 1) * size)
        heads_ref[h] = jnp.concatenate([key[:, at], value[:, at]], axis=1).astype(BF16)
        proj_ref[h * LANES : h * LANES + size, :] = w_proj_ref[at, :]
        proj_ref[h * LANES + size : (h + 1) * LANES, :] = jnp.zeros((LANES - size, width), BF16)
    lane = lax.broadcasted_iota(jnp.int32, (8, HEADS * LANES), 1) % LANES
    ones = jnp.where((lane == 96) | (lane >= 98) & (lane < 100), 1.0, 0.0)
    biases = by_head(jnp.broadcast_to(qv_bias_ref[0:1, :], (8, width)))
    bias_ref[0:8, :] = biases
    bias_ref[8:16, :] = by_head(jnp.broadcast_to(qv_bias_ref[1:2, :], (8, width))) + ones
    bias_ref[16:24, :] = ones


def row_of(ref):
    return ref[...].reshape(1, ref.shape[-1])


def keys_of(tokens, base, first_mask, second_mask, refs, targets):
    gain_ref, shift_ref, wkv_ref, bias_ref = refs
    key_ref, value_ref, low_ref, hat_ref, peak_ref = targets
    rows, di = tokens.shape
    wide = HEADS * LANES
    hat, _ = norm_stats(tokens)
    low = (hat * row_of(gain_ref) + row_of(shift_ref)).astype(BF16)
    at = pl.ds(base, rows)
    low_ref[at, :di] = low
    hat_ref[at, :di] = hat.astype(BF16)
    key = dot(low, wkv_ref[:, :wide])
    squares = key[:, :LANES] * key[:, :LANES]
    for h in range(1, HEADS):
        squares = squares + key[:, h * LANES : (h + 1) * LANES] * key[:, h * LANES : (h + 1) * LANES]
    top = jnp.max(jnp.sum(squares, axis=-1, keepdims=True))
    peak_ref[...] = jnp.maximum(peak_ref[...], top)
    row = lax.broadcasted_iota(jnp.int32, (8, wide), 0) % 2
    lane = lax.broadcasted_iota(jnp.int32, (8, wide), 1) % LANES
    mask = jnp.where(row == 0, first_mask, second_mask)
    pattern = bias_ref[16:24, :] + jnp.where(lane == 97, mask, 0.0)
    key = (key.reshape(rows // 8, 8, wide) + pattern[None]).reshape(rows, wide).astype(BF16)
    for h in range(HEADS):
        key_ref[h, at, :] = key[:, h * LANES : (h + 1) * LANES]
    value = dot(low, wkv_ref[:, wide:])
    value = (value.reshape(rows // 8, 8, wide) + bias_ref[8:16, :][None]).reshape(rows, wide)
    value = value.astype(BF16)
    for h in range(HEADS):
        value_ref[h, at, :] = value[:, h * LANES : (h + 1) * LANES]


def fill_pads(base, rows, room, di, targets):
    key_ref, value_ref, low_ref, hat_ref, _ = targets
    empty = room - rows
    lane = lax.broadcasted_iota(jnp.int32, (empty, LANES), 1)
    at = slice(base + rows, base + room)
    for h in range(HEADS):
        key_ref[h, at, :] = jnp.where(lane == 97, ABSENT, 0.0).astype(BF16)
        value_ref[h, at, :] = jnp.zeros((empty, LANES), BF16)
    tail = lax.broadcasted_iota(jnp.int32, (room, LANES), 1)
    ones_tail = jnp.where(tail == di - LANES, 1.0, 0.0).astype(BF16)
    for ref in (low_ref, hat_ref):
        ref[base : base + room, LANES:] = ones_tail
        ref[at, :di] = jnp.zeros((empty, di), BF16)


def absent(frames_ref, holder, frame):
    clip, core = own_place()
    index = 2 * ((2 * clip + core) ^ holder) + frame
    return jnp.where(index < frames_ref[clip], 0.0, ABSENT).astype(F32)


def near_kernel(
    frames_ref,
    raw_ref,
    near_ref,
    gain_ref,
    shift_ref,
    wkv_ref,
    bias_ref,
    pool_ref,
    key_out,
    value_out,
    low_out,
    hat_out,
    pooled_ref,
    pooled_hat_ref,
    peak_ref,
    key_ref,
    value_ref,
    low_ref,
    hat_ref,
    mine_ref,
    sems,
):
    positions, _, di = mine_ref.shape
    rows = 2 * positions
    clip, _ = own_place()
    load = pltpu.make_async_copy(raw_ref.at[clip], mine_ref, sems.at[8])
    load.start()
    load.wait()
    room = key_ref.shape[1] // 2
    refs = (gain_ref, shift_ref, wkv_ref, bias_ref)
    targets = (key_ref, value_ref, low_ref, hat_ref, peak_ref)
    peak_ref[...] = jnp.zeros(peak_ref.shape, F32)
    pieces = 2
    step = positions // pieces
    copies = []
    for i in range(2):
        base = i * room
        fill_pads(base, rows, room, di, targets)

        for j in range(pieces):
            if i == 0:
                tokens = mine_ref[j * step : (j + 1) * step].reshape(2 * step, di).astype(F32)
            else:
                tokens = unpack_half(near_ref, j)
            keys_of(
                tokens,
                base + 2 * j * step,
                absent(frames_ref, i, 0),
                absent(frames_ref, i, 1),
                refs,
                targets,
            )

        at, to = pl.ds(base, room), pl.ds(2 * base, room)
        for k, (src, dst) in enumerate(((key_ref, key_out), (value_ref, value_out))):
            copies.append(
                pltpu.make_async_copy(src.at[:, at, :], dst.at[:, to, :], sems.at[4 * i + k])
            )
        for k, (src, dst) in enumerate(((low_ref, low_out), (hat_ref, hat_out))):
            copies.append(
                pltpu.make_async_copy(src.at[at, :], dst.at[to, :], sems.at[4 * i + k + 2])
            )
        for copy in copies[-4:]:
            copy.start()
    pooled_ref[...] = dot(pool_ref[...], low_ref[:rows, :di])
    pooled_hat_ref[...] = dot(pool_ref[...], hat_ref[:rows, :di])
    for copy in copies:
        copy.wait()


def forward_kernel(
    dims,
    frames_ref,
    got_ref,
    near_got_ref,
    gain_ref,
    shift_ref,
    wkv_ref,
    bias_ref,
    wq_ref,
    wres_ref,
    res_bias_ref,
    pool_ref,
    pooled_in,
    pooled_hat_in,
    peak_in,
    key_in,
    value_in,
    low_in,
    hat_in,
    probs_ref,
    att_ref,
    residual_ref,
    pooled_ref,
    pooled_hat_ref,
    key_out,
    value_out,
    query_out,
    low_out,
    hat_out,
    key_ref,
    value_ref,
    query_ref,
    low_ref,
    hat_ref,
    acc_ref,
    norm_ref,
    peak_ref,
    sems,
):
    di, rows, room, half, chunk, chunks, head_dim = dims
    positions = rows // 2
    head = pl.program_id(0)
    step = pl.program_id(1)
    factor = 1.0 / head_dim**0.5
    loads, stores = [], []
    for i in range(2):
        at, to = pl.ds(2 * i * room, room), pl.ds((2 * i + 1) * room, room)
        for k, (src, dst) in enumerate(((key_in, key_ref), (value_in, value_ref))):
            loads.append(
                pltpu.make_async_copy(src.at[:, at, :], dst.at[:, at, :], sems.at[2 * i + k])
            )
        for k, (src, dst) in enumerate(((key_ref, key_out), (value_ref, value_out))):
            stores.append(
                pltpu.make_async_copy(src.at[:, to, :], dst.at[:, to, :], sems.at[4 + 2 * i + k])
            )
        for k, (src, dst) in enumerate(((low_ref, low_out), (hat_ref, hat_out))):
            stores.append(
                pltpu.make_async_copy(
                    src.at[pl.ds(i * room, room), :], dst.at[to, :], sems.at[8 + 2 * i + k]
                )
            )
    stores.append(pltpu.make_async_copy(query_ref, query_out, sems.at[12]))

    @pl.when((head == 0) & (step == 0))
    def _():
        for copy in loads:
            copy.start()
        refs = (gain_ref, shift_ref, wkv_ref, bias_ref)
        norm_ref[...] = peak_in[...]
        pieces = 2
        size = positions // pieces
        for i, ref in enumerate((got_ref, near_got_ref)):
            keys = (
                key_ref.at[:, pl.ds((2 * i + 1) * room, room), :],
                value_ref.at[:, pl.ds((2 * i + 1) * room, room), :],
                low_ref.at[pl.ds(i * room, room), :],
                hat_ref.at[pl.ds(i * room, room), :],
                norm_ref,
            )
            fill_pads(0, rows, room, di, keys)

            for j in range(pieces):
                keys_of(
                    unpack_half(ref, j),
                    2 * j * size,
                    absent(frames_ref, 2 + i, 0),
                    absent(frames_ref, 2 + i, 1),
                    refs,
                    keys,
                )

        for copy in stores[:-1]:
            copy.start()
        tail = lax.broadcasted_iota(jnp.int32, (2 * half, LANES), 1)
        ones_tail = jnp.where(tail == di - LANES, 1.0, 0.0).astype(BF16)
        pooled_ref[:, LANES:] = ones_tail
        pooled_hat_ref[:, LANES:] = ones_tail
        pooled = jnp.concatenate([pooled_in[...], dot(pool_ref[...], low_ref[:rows, :di])], axis=0)
        high = pooled.astype(BF16)
        rest = (pooled - high.astype(F32)).astype(BF16)
        pooled_ref[:, :di] = high
        pooled_hat_ref[:, :di] = jnp.concatenate(
            [pooled_hat_in[...], dot(pool_ref[...], hat_ref[:rows, :di])], axis=0
        ).astype(BF16)
        residual_ref[...] = (
            dot(high, wres_ref[...]) + dot(rest, wres_ref[...]) + row_of(res_bias_ref)
        )
        query = dot(high, wq_ref[...]) + dot(rest, wq_ref[...]) + bias_ref[0:1, :]
        query = query.astype(BF16).astype(F32)
        lane = lax.broadcasted_iota(jnp.int32, (2 * half, LANES), 1)
        top = jnp.float32(0.0)
        for h in range(HEADS):
            part_h = query[:, h * LANES : (h + 1) * LANES]
            top = jnp.maximum(top, jnp.max(jnp.sum(part_h * part_h, axis=-1, keepdims=True)))
            query_ref[h] = jnp.where(lane == 97, 1.0, part_h).astype(BF16)
        for copy in loads:
            copy.wait()
        reach = jnp.sqrt(jnp.max(norm_ref[...]) * top) * (1.02 * factor)

        @pl.when(jnp.logical_not(reach < 60.0))
        def _():
            peak_ref[...] = jnp.full((2 * half, LANES), -3e38, F32)

            @pl.loop(0, HEADS)
            def _(h):
                @pl.loop(0, chunks)
                def _(j):
                    at = pl.ds(pl.multiple_of(j * chunk, LANES), chunk)
                    scores = dot(query_ref[h], key_ref[h, at, :], 1, 1)
                    highest = jnp.max(scores, axis=-1, keepdims=True)
                    peak_ref[...] = jnp.where(
                        lane == h, jnp.maximum(peak_ref[...], highest), peak_ref[...]
                    )

            for h in range(HEADS):
                query_ref[h] = with_columns(
                    query_ref[h].astype(F32), lane, peak_ref[:, h : h + 1]
                ).astype(BF16)

        stores[-1].start()

    at = pl.ds(pl.multiple_of(step * chunk, LANES), chunk)
    scores = dot(query_ref[head], key_ref[head, at, :], 1, 1)
    probs = jnp.exp2(scores * (factor * LOG2E)).astype(BF16)
    probs_ref[0] = probs
    gathered = dot(probs, value_ref[head, at, :])

    @pl.when(step == 0)
    def _():
        acc_ref[...] = gathered

    @pl.when(step > 0)
    def _():
        acc_ref[...] += gathered

    @pl.when(step == chunks - 1)
    def _():
        lane = lax.broadcasted_iota(jnp.int32, (2 * half, LANES), 1)
        acc = acc_ref[...]
        total_inv = 1.0 / acc[:, 96:97]
        att_ref[0] = jnp.where(
            lane < 96, acc * total_inv, jnp.where(lane == 96, total_inv, 0.0)
        )

    @pl.when((head == HEADS - 1) & (step == chunks - 1))
    def _():
        for copy in stores:
            copy.wait()


def halves_out(halves_ref, keep_ref, give_ref, sems):
    core = lax.axis_index("core")
    copies = [
        pltpu.make_async_copy(halves_ref.at[core], keep_ref, sems.at[0]),
        pltpu.make_async_copy(halves_ref.at[1 - core], give_ref, sems.at[1]),
    ]
    for copy in copies:
        copy.start()
    return copies


def middle_kernel(
    att_ref,
    residual_ref,
    cot_ref,
    cot_got_ref,
    wproj_ref,
    proj_bias_ref,
    gain_ref,
    shift_ref,
    wfc1_ref,
    fc1_bias_ref,
    wfc2_ref,
    fc2_bias_ref,
    pooled_ref,
    out_ref,
    out_far_ref,
    keep_ref,
    give_ref,
    d_mid_ref,
    d_att_ref,
    halves_ref,
    sems,
):
    clip, _ = own_place()
    count = att_ref.shape[1]
    half = count // 2
    width = residual_ref.shape[1]
    hidden = wfc1_ref.shape[1]
    lane = lax.broadcasted_iota(jnp.int32, (count, LANES), 1)
    attended = jnp.concatenate(
        [jnp.where(lane < 96, att_ref[h], 0.0).astype(BF16) for h in range(HEADS)], axis=1
    )
    mid = dot(attended, wproj_ref[...]) + row_of(proj_bias_ref) + residual_ref[...]
    hat, scale_inv = norm_stats(mid)
    mlp_in = (hat * row_of(gain_ref) + row_of(shift_ref)).astype(BF16)
    cot32 = jnp.concatenate(
        [
            cot_ref[clip].reshape(half, width).astype(F32),
            cot_got_ref[...].reshape(half, width).astype(F32),
        ],
        axis=0,
    )
    cot = cot32.astype(BF16)
    d_in = jnp.zeros((count, width), F32)
    out = mid + row_of(fc2_bias_ref)
    piece = 512
    fc1_bias = row_of(fc1_bias_ref)
    copies, sums = [], []
    for i in range(hidden // piece):
        at = slice(i * piece, (i + 1) * piece)
        x = dot(mlp_in, wfc1_ref[:, at]) + fc1_bias[:, at]
        c0 = 0.7978845608028654
        square = x * x
        th = jnp.tanh(c0 * x * (1.0 + 0.044715 * square))
        half_up = 0.5 * (1.0 + th)
        act = (x * half_up).astype(BF16)
        slope = half_up + (0.5 * c0) * x * (1.0 - th * th) * (1.0 + (3 * 0.044715) * square)
        out = out + dot(act, wfc2_ref[at, :])
        halves_ref[0, at, :] = dot(act, cot, 0, 0).astype(BF16)
        d_pre = (dot(cot, wfc2_ref[at, :], 1, 1) * slope).astype(BF16)
        g_fc1 = dot(mlp_in, d_pre, 0, 0).astype(BF16)
        for col in range(0, piece, LANES):
            block, lane_at = divmod(i * piece + col, width)
            halves_ref[1, block * width : (block + 1) * width, lane_at : lane_at + LANES] = g_fc1[
                :, col : col + LANES
            ]
        sums.append(jnp.sum(d_pre.astype(F32), axis=0, keepdims=True))
        d_in = d_in + dot(d_pre, wfc1_ref[:, at], 1, 1)
    sums = jnp.concatenate(sums, axis=1)
    blocks = hidden // width
    size = width // HEADS
    di = 2 * size
    d_mid = (cot32 + norm_back(d_in * row_of(gain_ref), hat, scale_inv)).astype(BF16)
    d_mid_ref[...] = d_mid
    for h in range(HEADS):
        at = slice(hidden + size * h, hidden + size * (h + 1))
        halves_ref[0, at, :] = dot(
            attended[:, h * LANES : (h + 1) * LANES], d_mid, 0, 0
        )[:size].astype(BF16)
    halves_ref[1, hidden : hidden + di, :] = dot(pooled_ref[...], d_mid, 0, 0)[:di].astype(BF16)
    vec_row = lax.broadcasted_iota(jnp.int32, (16, width), 0)
    vectors = jnp.where(vec_row == blocks, jnp.sum(cot32, axis=0, keepdims=True), 0.0)
    for i in range(blocks):
        vectors = jnp.where(vec_row == i, sums[:, i * width : (i + 1) * width], vectors)
    for i, vector in enumerate((d_in * hat, d_in, d_mid.astype(F32))):
        vectors = jnp.where(vec_row == 8 + i, jnp.sum(vector, axis=0, keepdims=True), vectors)
    halves_ref[1, hidden + di : hidden + di + 16, :] = vectors.astype(BF16)
    halves_ref[1, hidden + di + 16 :, :] = jnp.zeros((width - di - 16, width), BF16)
    copies = halves_out(halves_ref, keep_ref, give_ref, sems)
    d_att = dot(d_mid, wproj_ref[...], 1, 1).astype(BF16).astype(F32)
    for h in range(HEADS):
        att = att_ref[h]
        scaled = (d_att[:, h * LANES : (h + 1) * LANES] * att[:, 96:97]).astype(BF16).astype(F32)
        delta = jnp.sum(jnp.where(lane < 96, scaled * att, 0.0), axis=-1, keepdims=True)
        d_att_ref[h] = with_columns(scaled, lane, delta).astype(BF16)
    out_ref[clip] = out[:half].astype(BF16).reshape(out_far_ref.shape)
    out_far_ref[...] = out[half:].astype(BF16).reshape(out_far_ref.shape)
    for copy in copies:
        copy.wait()


def backward_kernel(
    first,
    last,
    heads,
    chunks,
    factor,
    probs_ref,
    key_ref,
    value_ref,
    query_ref,
    d_att_ref,
    low_ref,
    wkv_ref,
    pooled_ref,
    *rest,
):
    rest = list(rest)
    prev_ref = None if first else rest.pop(0)
    hat_ref = rest.pop(0) if last else None
    out_ref, pack_ref, dq_ref = rest[:3]
    norm_ref = rest[3] if last else None
    dn_ref, gw_ref, acc_ref = rest[-3:]
    head, step = pl.program_id(0), pl.program_id(1)
    chunk = probs_ref.shape[2]
    at = pl.ds(pl.multiple_of(step * chunk, LANES), chunk)
    probs = probs_ref[0]
    d_prob = dot(d_att_ref[0], value_ref[0], 1, 1)
    d_value = dot(d_att_ref[0], probs, 0, 0)[:96]
    d_scores = (probs.astype(F32) * d_prob).astype(BF16)
    d_key = dot(query_ref[0], d_scores, 0, 0)[:96] * factor
    d_query = dot(d_scores, key_ref[0])
    both = jnp.concatenate([d_key, d_value], axis=0).astype(BF16)
    back = dot(wkv_ref[0], both)
    g_w = dot(both, low_ref[...])

    @pl.when(head == 0)
    def _():
        dn_ref[:, at] = back if first else prev_ref[...] + back

    if heads > 1:

        @pl.when(head > 0)
        def _():
            dn_ref[:, at] += back

    @pl.when(head == heads - 1)
    def _():
        dn = dn_ref[:, at].astype(out_ref.dtype)
        out_ref[...] = dn
        if last:
            sums = dot(dn, hat_ref[...])
            norm_ref[...] = jnp.where(step == 0, sums, norm_ref[...] + sums)

    @pl.when(step == 0)
    def _():
        gw_ref[...] = g_w
        acc_ref[...] = d_query

    @pl.when(step > 0)
    def _():
        gw_ref[...] += g_w
        acc_ref[...] += d_query

    @pl.when(step == chunks - 1)
    def _():
        lane = lax.broadcasted_iota(jnp.int32, acc_ref.shape, 1)
        dq = jnp.where(lane < 96, acc_ref[...] * factor, 0.0).astype(BF16)
        dq_ref[0] = dq
        g_q = dot(pooled_ref[...], dq, 0, 0)
        size = gw_ref.shape[0]
        rows = pack_ref.shape[1]
        pack_ref[0, :size, :256] = gw_ref[...]
        pack_ref[0, :, 256:] = g_q[:rows]
        pack_ref[0, size:, :256] = jnp.zeros((rows - size, 256), F32)


def gather_kernel(
    norm_ref,
    dq0_ref,
    dq1_ref,
    dq2_ref,
    pack0_ref,
    pack1_ref,
    pack2_ref,
    d_mid_ref,
    wq_ref,
    wres_ref,
    pooled_hat_ref,
    d_pool_ref,
    keep_ref,
    give_ref,
    halves_ref,
    sems,
):
    di = wq_ref.shape[0]
    d_pool = dot(d_mid_ref[...], wres_ref[...], 1, 1)
    for h, dq in enumerate((dq0_ref[0], dq1_ref[0], dq1_ref[1], dq2_ref[0])):
        d_pool = d_pool + dot(dq, wq_ref[:, h * LANES : (h + 1) * LANES], 1, 1)
    low = d_pool.astype(BF16)
    d_pool_ref[...] = low
    both = norm_ref[...] + dot(low, pooled_hat_ref[...], 0, 0)
    row = lax.broadcasted_iota(jnp.int32, both.shape, 0)
    col = lax.broadcasted_iota(jnp.int32, both.shape, 1)
    gain = jnp.sum(jnp.where(row == col, both, 0.0), axis=1, keepdims=True)
    lane = lax.broadcasted_iota(jnp.int32, (di, LANES), 1)
    norms = jnp.where(lane == 65, gain, jnp.where(lane == 66, both[:, di : di + 1], 0.0))
    pieces = []
    for pack in (pack0_ref[0], pack1_ref[0], pack1_ref[1]):
        pieces.append(pack.astype(BF16))
    last = pack2_ref[0]
    middle = last[:, LANES : 2 * LANES] + jnp.concatenate(
        [norms, jnp.zeros((last.shape[0] - di, LANES), F32)], axis=0
    )
    pieces.append(
        jnp.concatenate([last[:, :LANES], middle, last[:, 2 * LANES :]], axis=1).astype(BF16)
    )
    cut, width = keep_ref.shape
    pieces.append(jnp.zeros((2 * cut - sum(p.shape[0] for p in pieces), width), BF16))
    at = 0
    for piece in pieces:
        size = piece.shape[0]
        done = 0
        while done < size:
            side, row = divmod(at + done, cut)
            take = min(size - done, cut - row)
            halves_ref[side, row : row + take, :] = piece[done : done + take]
            done += take
        at += size
    for copy in halves_out(halves_ref, keep_ref, give_ref, sems):
        copy.wait()


def end_kernel(
    dn_ref,
    got_ref,
    d_pool_ref,
    spread_ref,
    raw_ref,
    far_ref,
    gain_ref,
    out_ref,
    out_far_ref,
    held_ref,
    sem,
):
    clip, _ = own_place()
    load = pltpu.make_async_copy(raw_ref.at[clip], held_ref, sem)
    load.start()
    positions, _, di = held_ref.shape
    rows = 2 * positions
    half = spread_ref.shape[1]
    room = dn_ref.shape[1] // 2
    for own in (1, 0):
        start = own * room
        lead = start % LANES
        at = slice(start - lead, start - lead + -(-(lead + rows) // LANES) * LANES)
        turned = (dn_ref[:, at].astype(F32) + got_ref[:, at].astype(F32)).T[lead : lead + rows]
        spread = dot(spread_ref[...], d_pool_ref[own * half : (own + 1) * half, :])
        if own == 0:
            load.wait()
            tokens = held_ref[...].reshape(rows, di).astype(F32)
        else:
            tokens = jnp.concatenate([unpack_half(far_ref, 0), unpack_half(far_ref, 1)], axis=0)
        hat, scale_inv = norm_stats(tokens)
        grad = norm_back((turned + spread) * row_of(gain_ref), hat, scale_inv)
        if own == 0:
            out_ref[clip] = grad.astype(BF16).reshape(positions, 2, di)
        else:
            first, rest = pack_rows(grad)
            out_far_ref[:rows, :] = first.astype(BF16)
            out_far_ref[rows:, :] = rest.astype(BF16)


def finish_kernel(tokens_in, out_in, got_ref, out_got_ref, tokens_ref, out_ref, held_ref, sems):
    clip, _ = own_place()
    positions, _, di = held_ref.shape
    copies = [
        pltpu.make_async_copy(out_got_ref, out_ref.at[1 - clip], sems.at[0]),
        pltpu.make_async_copy(held_ref, tokens_ref.at[1 - clip], sems.at[1]),
    ]
    copies[0].start()
    for j in range(2):
        at = slice(j * positions // 2, (j + 1) * positions // 2)
        held_ref[at] = unpack_half(got_ref, j).astype(BF16).reshape(positions // 2, 2, di)
    copies[1].start()
    for copy in copies:
        copy.wait()


def unpack_big_kernel(
    own_ref,
    other_ref,
    fc2_ref,
    fc1_ref,
    proj_ref,
    res_ref,
    fc1_bias_ref,
    fc2_bias_ref,
    mlp_gain_ref,
    mlp_shift_ref,
    proj_bias_ref,
    res_bias_ref,
):
    _, core = own_place()
    width = own_ref.shape[1]
    hidden = fc2_ref.shape[0]
    di = res_ref.shape[0]

    def write(first, second):
        fc2_ref[...] = first[:hidden, :].astype(F32)
        for i in range(hidden // width):
            at = slice(i * width, (i + 1) * width)
            fc1_ref[:, at] = second[at, :].astype(F32)
        proj_ref[...] = first[hidden : hidden + width, :].astype(F32)
        res_ref[...] = second[hidden : hidden + di, :].astype(F32)
        vectors = second[hidden + di : hidden + di + 16, :].astype(F32)
        blocks = hidden // width
        fc1_bias_ref[...] = jnp.concatenate([vectors[i : i + 1] for i in range(blocks)], axis=1)[0]
        fc2_bias_ref[...] = vectors[blocks]
        mlp_gain_ref[...] = vectors[8]
        mlp_shift_ref[...] = vectors[9]
        proj_bias_ref[...] = vectors[10]
        res_bias_ref[...] = vectors[10]

    @pl.when(core == 0)
    def _():
        write(own_ref, other_ref)

    @pl.when(core == 1)
    def _():
        write(other_ref, own_ref)


def unpack_small_kernel(
    own_ref,
    other_ref,
    qkv_ref,
    qv_bias_ref,
    norm_gain_ref,
    norm_shift_ref,
    whole_ref,
):
    _, core = own_place()
    cut, width = own_ref.shape
    size = width // HEADS
    di = 2 * size
    whole_ref[core] = own_ref[...]
    whole_ref[1 - core] = other_ref[...]

    def rows(start, count):
        pieces = []
        while count:
            side, row = divmod(start, cut)
            take = min(count, cut - row)
            pieces.append(whole_ref[side, row : row + take, :])
            start, count = start + take, count - take
        return (pieces[0] if len(pieces) == 1 else jnp.concatenate(pieces, axis=0)).astype(F32)

    start = 0
    queries, keys, values, q_bias, v_bias = [], [], [], [], []
    for h in range(HEADS):
        pack = rows(start + 208 * h, 208)
        queries.append(pack[:di, 256 : 256 + size])
        turned = pack[:di, :256].T
        keys.append(turned[:di, :size])
        values.append(turned[:di, size:])
        q_bias.append(pack[di : di + 1, 256 : 256 + size])
        v_bias.append(turned[di : di + 1, size:])
    qkv_ref[...] = jnp.concatenate(queries + keys + values, axis=1)
    qv_bias_ref[0:1, :] = jnp.concatenate(q_bias, axis=1)
    qv_bias_ref[1:2, :] = jnp.concatenate(v_bias, axis=1)
    norm_gain_ref[...] = turned[di + 1]
    norm_shift_ref[...] = turned[di + 2]


def sizes():
    return [lax.axis_size(name) for name in BOTH]


def exchange(value, mask):
    count = int(np.prod(sizes()))
    return lax.ppermute(value, BOTH, [(i, i ^ mask) for i in range(count)])


def stages():
    count = int(np.prod(sizes()))
    out = [(1, [1]), (2, [2, 4, 6])]
    bit = 8
    while bit < count:
        if bit * 2 < count:
            out.append((bit, [bit, 2 * bit, 3 * bit]))
            bit *= 4
        else:
            out.append((bit, [bit]))
            bit *= 2
    return out


def place(stage):
    return (lax.axis_index(BOTH) // stage[0]) % (len(stage[1]) + 1)


def sum_pieces(pieces):
    pieces = [p.astype(F32) for p in pieces]
    while len(pieces) > 1:
        pieces = [a + b for a, b in zip(pieces[::2], pieces[1::2])]
    return pieces[0]


class Sum:
    def __init__(self, keep, give, depth):
        self.plan = stages()
        self.depth = min(depth, len(self.plan) - 1)
        self.places = [place(stage) for stage in self.plan]
        self.held, self.pieces = keep, [give]
        self.at, self.back, self.done, self.summed = 0, False, False, False

    def cut(self):
        masks = self.plan[self.at][1]
        if self.back or self.at > self.depth:
            self.pieces = [self.held] * len(masks)
            return
        size, where = len(masks) + 1, self.places[self.at]
        later = int(np.prod([len(self.plan[i][1]) + 1 for i in range(self.at + 1, self.depth + 1)]))
        rows, columns = self.held.shape
        whole = self.held.reshape(later, size, rows // (later * size), columns)

        def take(index):
            piece = lax.dynamic_index_in_dim(whole, index, 1, keepdims=False)
            return piece.reshape(rows // size, columns)

        self.held = take(where)
        self.pieces = [take(where ^ (k + 1)) for k in range(size - 1)]

    def send(self, other):
        (self.held, self.pieces), other = lax.optimization_barrier(((self.held, self.pieces), other))
        self.got = [exchange(p, mask) for p, mask in zip(self.pieces, self.plan[self.at][1])]
        self.done = self.back and self.at == 0
        return other

    def merge(self, other):
        (self.held, self.got), other = lax.optimization_barrier(((self.held, self.got), other))
        if not self.back:
            self.held = sum_pieces([self.held] + self.got).astype(BF16)
            if self.at + 1 < len(self.plan):
                self.at += 1
            else:
                self.back, self.summed, self.at = True, True, self.depth
        else:
            size, where = len(self.got) + 1, self.places[self.at]
            stacked = jnp.stack([self.held] + self.got)
            self.held = jnp.concatenate(
                [
                    lax.dynamic_index_in_dim(stacked, where ^ k, 0, keepdims=False)
                    for k in range(size)
                ]
            )
            self.at -= 1
        self.cut()
        return other

    def advance(self, other):
        return other if self.done else self.send(self.merge(other))


def call(kernel, out_shape, args, flops=0, vmem=60, **kwargs):
    moved = sum(np.prod(a.shape) * a.dtype.itemsize for a in args) if flops else 1
    return pl.pallas_call(
        kernel,
        out_shape=out_shape,
        compiler_params=pltpu.CompilerParams(vmem_limit_bytes=vmem * MIB),
        cost_estimate=pl.CostEstimate(
            flops=int(max(flops, 1)), bytes_accessed=int(moved), transcendentals=0
        ),
        **kwargs,
    )(*args)


def body(
    tokens,
    cotangent,
    frames,
    norm_gain,
    norm_shift,
    w_qkv,
    qv_bias,
    w_proj,
    proj_bias,
    w_res,
    res_bias,
    mlp_gain,
    mlp_shift,
    w_fc1,
    fc1_bias,
    w_fc2,
    fc2_bias,
):
    clip_count, frame_local, grid_rows, grid_cols, di = tokens.shape
    width = w_proj.shape[0]
    head_dim = width // HEADS
    hidden = w_fc1.shape[1]
    frame = grid_rows * grid_cols
    rows = frame_local * frame
    half = rows // 4
    room = 1600
    chunk = 1280
    chunks = 4 * room // chunk
    wide = HEADS * LANES
    factor = 1.0 / head_dim**0.5
    vmem = pl.BlockSpec(memory_space=pltpu.VMEM)
    smem = pl.BlockSpec(memory_space=pltpu.SMEM)
    hbm = pl.BlockSpec(memory_space=pl.ANY)
    sds = jax.ShapeDtypeStruct

    raw = tokens.transpose(0, 2, 3, 1, 4).reshape(clip_count, frame, frame_local, di)
    cot_raw = cotangent.transpose(0, 2, 3, 1, 4).reshape(
        clip_count, frame // 4, frame_local, width
    )

    def pick(other):
        return call(
            functools.partial(pick_kernel, other),
            [sds((3 * rows // 2, LANES), BF16)],
            (raw,),
            vmem=16,
            in_specs=[hbm],
            out_specs=[vmem],
            scratch_shapes=[pltpu.VMEM(raw.shape[1:], BF16), pltpu.SemaphoreType.DMA],
        )[0]

    got = exchange(pick(True), 2)
    near = exchange(pick(False), 1)
    clip_at = lax.axis_index("next_y")
    cot_far = lax.dynamic_index_in_dim(cot_raw, 1 - clip_at, 0, keepdims=False)
    near, cot_far = lax.optimization_barrier((near, cot_far))
    cot_got = exchange(cot_far, 2)

    pool_np = np.zeros((half, rows), np.float32)
    token = np.arange(rows)
    position, f = token // frame_local, token % frame_local
    r, c = position // grid_cols, position % grid_cols
    pool_np[((r // 2) * (grid_cols // 2) + c // 2) * frame_local + f, token] = 0.25
    pool = jnp.asarray(pool_np, BF16)
    spread = jnp.asarray(pool_np.T, BF16)

    wq, wkv, w_kv_heads, w_proj_pad, bias = call(
        weights_kernel,
        [
            sds((di, wide), BF16),
            sds((di, 2 * wide), BF16),
            sds((HEADS, di, 2 * head_dim), BF16),
            sds((wide, width), BF16),
            sds((24, wide), F32),
        ],
        (w_qkv, qv_bias, w_proj),
        in_specs=[vmem] * 3,
        out_specs=[vmem] * 5,
    )
    whole = [
        sds((HEADS, 4 * room, LANES), BF16),
        sds((HEADS, 4 * room, LANES), BF16),
        sds((4 * room, 256), BF16),
        sds((4 * room, 256), BF16),
    ]
    key, value, low, hat, pooled_mine, pooled_hat_mine, peak = call(
        near_kernel,
        whole
        + [sds((half, di), F32), sds((half, di), F32), sds((8, LANES), F32)],
        (frames, raw, near, norm_gain, norm_shift, wkv, bias, pool),
        flops=3e9,
        in_specs=[smem, hbm] + [vmem] * 6,
        out_specs=[hbm] * 4 + [vmem] * 3,
        scratch_shapes=[
            pltpu.VMEM((HEADS, 2 * room, LANES), BF16),
            pltpu.VMEM((HEADS, 2 * room, LANES), BF16),
            pltpu.VMEM((2 * room, 256), BF16),
            pltpu.VMEM((2 * room, 256), BF16),
            pltpu.VMEM(raw.shape[1:], BF16),
            pltpu.SemaphoreType.DMA((9,)),
        ],
    )
    got, peak = lax.optimization_barrier((got, peak))
    near_got = exchange(got, 1)
    dims = (di, rows, room, half, chunk, chunks, head_dim)
    probs, att, residual, pooled, pooled_hat, key, value, query, low, hat = call(
        functools.partial(forward_kernel, dims),
        [
            sds((HEADS, 2 * half, 4 * room), BF16),
            sds((HEADS, 2 * half, LANES), F32),
            sds((2 * half, width), F32),
            sds((2 * half, 256), BF16),
            sds((2 * half, 256), BF16),
        ]
        + whole[:2]
        + [sds((HEADS, 2 * half, LANES), BF16)]
        + whole[2:],
        (
            frames,
            got,
            near_got,
            norm_gain,
            norm_shift,
            wkv,
            bias,
            wq,
            w_res,
            res_bias,
            pool,
            pooled_mine,
            pooled_hat_mine,
            peak,
            key,
            value,
            low,
            hat,
        ),
        flops=25e9,
        grid=(HEADS, chunks),
        in_specs=[smem] + [vmem] * 13 + [hbm] * 4,
        out_specs=[
            pl.BlockSpec((1, 2 * half, chunk), lambda h, j: (h, 0, j)),
            pl.BlockSpec((1, 2 * half, LANES), lambda h, j: (h, 0, 0)),
            vmem,
            vmem,
            vmem,
        ]
        + [hbm] * 5,
        input_output_aliases={14: 5, 15: 6, 16: 8, 17: 9},
        scratch_shapes=[
            pltpu.VMEM((HEADS, 4 * room, LANES), BF16),
            pltpu.VMEM((HEADS, 4 * room, LANES), BF16),
            pltpu.VMEM((HEADS, 2 * half, LANES), BF16),
            pltpu.VMEM((2 * room, 256), BF16),
            pltpu.VMEM((2 * room, 256), BF16),
            pltpu.VMEM((2 * half, LANES), F32),
            pltpu.VMEM((8, LANES), F32),
            pltpu.VMEM((2 * half, LANES), F32),
            pltpu.SemaphoreType.DMA((13,)),
        ],
    )

    out_raw = sds(cot_raw.shape, BF16)
    out_far = sds(cot_raw.shape[1:], BF16)
    both = hidden + width
    out, out_far, fc_keep, fc_give, d_mid, d_att = call(
        middle_kernel,
        [
            out_raw,
            out_far,
            sds((both, width), BF16),
            sds((both, width), BF16),
            sds((2 * half, width), BF16),
            sds((HEADS, 2 * half, LANES), BF16),
        ],
        (
            att,
            residual,
            cot_raw,
            cot_got,
            w_proj_pad,
            proj_bias,
            mlp_gain,
            mlp_shift,
            w_fc1,
            fc1_bias,
            w_fc2,
            fc2_bias,
            pooled,
        ),
        flops=8e9,
        in_specs=[vmem] * 13,
        out_specs=[vmem, vmem, hbm, hbm, vmem, vmem],
        scratch_shapes=[pltpu.VMEM((2, both, width), BF16), pltpu.SemaphoreType.DMA((2,))],
    )
    big = Sum(fc_keep, fc_give, 1)
    d_att = big.send(d_att)
    d_att = big.merge(d_att)
    d_att = big.send(d_att)

    packs, dqs = [], []
    dn = None
    groups = ((0,), (1, 2), (3,))
    for group in groups:
        first, last = group[0] == 0, group[-1] == HEADS - 1
        n, h = len(group), group[0]
        args = [probs, key, value, query, d_att, low, w_kv_heads, pooled]
        specs = [
            pl.BlockSpec((1, 2 * half, chunk), lambda i, j, h=h: (h + i, 0, j)),
            pl.BlockSpec((1, chunk, LANES), lambda i, j, h=h: (h + i, j, 0)),
            pl.BlockSpec((1, chunk, LANES), lambda i, j, h=h: (h + i, j, 0)),
            pl.BlockSpec((1, 2 * half, LANES), lambda i, j, h=h: (h + i, 0, 0)),
            pl.BlockSpec((1, 2 * half, LANES), lambda i, j, h=h: (h + i, 0, 0)),
            pl.BlockSpec((chunk, 256), lambda i, j: (j, 0)),
            pl.BlockSpec((1, di, 2 * head_dim), lambda i, j, h=h: (h + i, 0, 0)),
            vmem,
        ]
        if not first:
            args.append(dn)
            specs.append(pl.BlockSpec((di, chunk), lambda i, j: (0, jnp.where(i == 0, j, chunks - 1))))
        if last:
            args.append(hat)
            specs.append(
                pl.BlockSpec((chunk, 256), lambda i, j, n=n: (jnp.where(i == n - 1, j, 0), 0))
            )
        results = call(
            functools.partial(backward_kernel, first, last, n, chunks, factor),
            [
                sds((di, 4 * room), BF16 if last else F32),
                sds((n, 208, 384), F32),
                sds((n, 2 * half, LANES), BF16),
            ]
            + [sds((di, 256), F32)] * last,
            args,
            flops=9e9 * n,
            grid=(n, chunks),
            in_specs=specs,
            out_specs=[
                pl.BlockSpec((di, chunk), lambda i, j, n=n: (0, jnp.where(i == n - 1, j, 0))),
                pl.BlockSpec((1, 208, 384), lambda i, j: (i, 0, 0)),
                pl.BlockSpec((1, 2 * half, LANES), lambda i, j: (i, 0, 0)),
            ]
            + [vmem] * last,
            scratch_shapes=[
                pltpu.VMEM((di, 4 * room), F32),
                pltpu.VMEM((2 * head_dim, 256), F32),
                pltpu.VMEM((2 * half, LANES), F32),
            ],
        )
        dn, pack, dq = results[:3]
        packs.append(pack)
        dqs.append(dq)
        dn = big.merge(dn)
        if first:
            big.held, dn, out_far = lax.optimization_barrier((big.held, dn, out_far))
            out_got = exchange(out_far, 2)
        elif not last:
            dn, out_got = lax.optimization_barrier((dn, out_got))
        if not last:
            dn = big.send(dn)
    while not big.summed:
        dn = big.merge(big.send(dn))
    norm_sums = results[3]

    cut = 448
    sib_got = exchange(dn, 1)
    d_pool, keep, give = call(
        gather_kernel,
        [sds((2 * half, di), BF16), sds((cut, width), BF16), sds((cut, width), BF16)],
        (norm_sums, *dqs, *packs, d_mid, wq, w_res, pooled_hat),
        flops=4e9,
        in_specs=[vmem] * 11,
        out_specs=[vmem, hbm, hbm],
        scratch_shapes=[pltpu.VMEM((2, cut, width), BF16), pltpu.SemaphoreType.DMA((2,))],
    )
    small = Sum(keep, give, 1)
    sib_got = small.send(sib_got)
    sib_got = small.advance(sib_got)
    (big.held, big.pieces), small.pieces = lax.optimization_barrier(
        ((big.held, big.pieces), small.pieces)
    )
    sib_got = big.send(sib_got)
    grad_tokens, grad_far = call(
        end_kernel,
        [sds(raw.shape, BF16), sds(got.shape, BF16)],
        (dn, sib_got, d_pool, spread, raw, got, norm_gain),
        flops=9e9,
        grid=(1,),
        in_specs=[
            pl.BlockSpec((di, 2 * room), lambda i: (0, 0)),
            pl.BlockSpec((di, 2 * room), lambda i: (0, 1)),
            vmem,
            vmem,
            hbm,
            vmem,
            vmem,
        ],
        out_specs=[vmem, vmem],
        scratch_shapes=[pltpu.VMEM(raw.shape[1:], BF16), pltpu.SemaphoreType.DMA],
    )
    grad_far = small.advance(grad_far)
    grad_got = exchange(grad_far, 2)
    while not big.done:
        grad_tokens = big.advance(grad_tokens)
    big_own, big_other = big.held, big.got[0]
    vector = sds((width,), F32)
    (
        s_fc2,
        s_fc1,
        s_proj,
        s_res,
        s_fc1_bias,
        s_fc2_bias,
        s_mlp_gain,
        s_mlp_shift,
        s_proj_bias,
        s_res_bias,
    ) = call(
        unpack_big_kernel,
        [
            sds((hidden, width), F32),
            sds((width, hidden), F32),
            sds((width, width), F32),
            sds((di, width), F32),
            sds((hidden,), F32),
        ]
        + [vector] * 5,
        (big_own, big_other),
        vmem=24,
        in_specs=[vmem] * 2,
        out_specs=[vmem] * 10,
    )
    unpacked = (
        s_fc2,
        s_fc1,
        s_proj,
        s_res,
        s_fc1_bias,
        s_fc2_bias,
        s_mlp_gain,
        s_mlp_shift,
        s_proj_bias,
        s_res_bias,
    )
    while not small.summed:
        unpacked = small.advance(unpacked)
    grad_got, small.got = lax.optimization_barrier((grad_got, small.got))
    unpacked = small.advance(unpacked)
    (
        s_fc2,
        s_fc1,
        s_proj,
        s_res,
        s_fc1_bias,
        s_fc2_bias,
        s_mlp_gain,
        s_mlp_shift,
        s_proj_bias,
        s_res_bias,
    ) = unpacked
    grad_tokens, block_out = call(
        finish_kernel,
        [sds(raw.shape, BF16), sds(cot_raw.shape, BF16)],
        (grad_tokens, out, grad_got, out_got),
        vmem=16,
        in_specs=[hbm, hbm, vmem, hbm],
        out_specs=[hbm, hbm],
        input_output_aliases={0: 0, 1: 1},
        scratch_shapes=[pltpu.VMEM(raw.shape[1:], BF16), pltpu.SemaphoreType.DMA((2,))],
    )

    def outward(value, like):
        shape = (clip_count, like.shape[2], like.shape[3], frame_local, like.shape[4])
        return value.reshape(shape).transpose(0, 3, 1, 2, 4)

    s_qkv, s_qv_bias, s_norm_gain, s_norm_shift = call(
        unpack_small_kernel,
        [sds((di, 3 * width), F32), sds((2, width), F32)] + [sds((di,), F32)] * 2,
        (small.held, small.got[0]),
        vmem=24,
        in_specs=[vmem] * 2,
        out_specs=[vmem] * 4,
        scratch_shapes=[pltpu.VMEM((2, cut, width), BF16)],
    )
    return (
        outward(block_out, cotangent),
        outward(grad_tokens, tokens),
        s_norm_gain,
        s_norm_shift,
        s_qkv,
        s_qv_bias,
        s_proj,
        s_proj_bias,
        s_res,
        s_res_bias,
        s_mlp_gain,
        s_mlp_shift,
        s_fc1,
        s_fc1_bias,
        s_fc2,
        s_fc2_bias,
    )


def solution(mesh):
    clips, units = mesh.shape["clips"], mesh.shape["units"]
    fine = jax.sharding.Mesh(mesh.devices.reshape(clips // 2, 2, units // 2, 2), BOTH)
    split = P(BOTH[:2], BOTH[2:], None, None, None)
    return jax.shard_map(
        body,
        mesh=fine,
        in_specs=(split, split, P(BOTH[:2])) + (P(),) * 14,
        out_specs=(split, split) + (P(),) * 14,
        check_vma=False,
    )
```
